32 devices in a mesh: wide: 16 (over z, x, core), narrow: 2 (over y).
Axes of the slice: x: 2, y: 2, z: 4, core: 2. Of those that a mesh axis runs over, the one named last changes fastest.
Arguments:
- inputs: bfloat16 [64, 256, 768], P(('wide', 'narrow')), may hold values from -6 to 6
- encoded: bfloat16 [64, 1024, 768], P(('wide', 'narrow')), may hold values from -6 to 6
- target_lengths: int32 [64], P(('wide', 'narrow')), may hold values from 32 to 256, as said below
- memory_lengths: int32 [64], P(('wide', 'narrow')), may hold values from 40 to 1024, as said below
- buckets: int32 [256, 256], replicated, may hold values from 0 to 31
- cotangent: bfloat16 [64, 256, 768], P(('wide', 'narrow')), may hold values from -6 to 6
- self_inward: bfloat16 [768, 2304], P('wide', 'narrow'), may hold values from -0.21875 to 0.21875
- self_outward: bfloat16 [768, 768], P('wide', 'narrow'), may hold values from -1.75 to 1.75
- cross_query: bfloat16 [768, 768], P('wide', 'narrow'), may hold values from -0.21875 to 0.21875
- cross_reader: bfloat16 [768, 1536], P('wide', 'narrow'), may hold values from -0.21875 to 0.21875
- cross_writer: bfloat16 [768, 768], P('wide', 'narrow'), may hold values from -3.5 to 3.5
- expand_weight: bfloat16 [768, 3072], P('wide', 'narrow'), may hold values from -0.21875 to 0.21875
- shrink_weight: bfloat16 [3072, 768], P('wide', 'narrow'), may hold values from -0.3125 to 0.3125
- norm_gains: float32 [3, 768], replicated, may hold values from 0.5 to 1.5
- bias_table: float32 [32, 12], replicated, may hold values from -5 to 5
Outputs:
- layer_out: bfloat16 [64, 256, 768], P(('wide', 'narrow'))
- inputs_grad: float32 [64, 256, 768], P(('wide', 'narrow'))
- encoded_grad: float32 [64, 1024, 768], P(('wide', 'narrow'))
- inward_grad: float32 [768, 2304], P('wide', 'narrow')
- inward_step: float32 [768, 2304], P('wide', 'narrow')
- inward_rows: float32 [768], P('wide')
- inward_cols: float32 [2304], P('narrow')
- outward_grad: float32 [768, 768], P('wide', 'narrow')
- outward_step: float32 [768, 768], P('wide', 'narrow')
- outward_rows: float32 [768], P('wide')
- outward_cols: float32 [768], P('narrow')
- query_grad: float32 [768, 768], P('wide', 'narrow')
- query_step: float32 [768, 768], P('wide', 'narrow')
- query_rows: float32 [768], P('wide')
- query_cols: float32 [768], P('narrow')
- reader_grad: float32 [768, 1536], P('wide', 'narrow')
- reader_step: float32 [768, 1536], P('wide', 'narrow')
- reader_rows: float32 [768], P('wide')
- reader_cols: float32 [1536], P('narrow')
- writer_grad: float32 [768, 768], P('wide', 'narrow')
- writer_step: float32 [768, 768], P('wide', 'narrow')
- writer_rows: float32 [768], P('wide')
- writer_cols: float32 [768], P('narrow')
- expand_grad: float32 [768, 3072], P('wide', 'narrow')
- expand_step: float32 [768, 3072], P('wide', 'narrow')
- expand_rows: float32 [768], P('wide')
- expand_cols: float32 [3072], P('narrow')
- shrink_grad: float32 [3072, 768], P('wide', 'narrow')
- shrink_step: float32 [3072, 768], P('wide', 'narrow')
- shrink_rows: float32 [3072], P('wide')
- shrink_cols: float32 [768], P('narrow')
- gains_grad: float32 [3, 768], replicated
- table_grad: float32 [32, 12], replicated
The draws below stay inside these ranges and needn't reach their ends.
Inputs may be any that keep to these rules, and one draw needn't show every extreme that they name: `target_lengths`: some sequence has exactly 256 valid target positions and some exactly 32. `memory_lengths`: most sequences are short; some sequence has exactly 1024 valid memory positions and some exactly 40.
All inputs are finite; a program needn't handle non-finite values.
Results may differ from the reference program's by a relative error of at most 0.02.
Values may be sent and summed in bfloat16 or wider, within the bound.
No kernel may reach another device: no remote copies, remote signals or barrier semaphores. Data moves between devices by JAX's collectives and lax.ppermute only.
A program may use at most 192 MiB of HBM per device.

```python
import jax
import jax.numpy as jnp
from jax import lax

D = 768
HEADS = 12
DH = 64
FF = 3072
NB = 32
TGT = 256
TGT_MIN = 32
MEM = 1024
MEM_MIN = 40
SEQS = 64


def ends_fixed(key, base, least, most):
    top_key, bottom_key = jax.random.split(key)
    places = jnp.arange(SEQS)
    top = jax.random.randint(top_key, (), 0, SEQS)
    bottom = (top + 1 + jax.random.randint(bottom_key, (), 0, SEQS - 1)) % SEQS
    base = jnp.where(places == top, most, base)
    return jnp.where(places == bottom, least, base).astype(jnp.int32)


def draw_target_lengths(key, part):
    key = jax.random.fold_in(key, 11)
    first, second = jax.random.split(key)
    base = jax.random.randint(first, (SEQS,), TGT_MIN, TGT + 1)
    return ends_fixed(second, base, TGT_MIN, TGT)


def draw_memory_lengths(key, part):
    key = jax.random.fold_in(key, 23)
    first, second = jax.random.split(key)
    raw = jax.random.randint(first, (SEQS,), 0, 1024)
    tail = raw * raw // 1024
    base = MEM_MIN + (MEM - MEM_MIN) * tail // 1024
    return ends_fixed(second, base, MEM_MIN, MEM)


def with_ends(result, stream_key, low, high):
    spot = [jax.random.randint(jax.random.fold_in(stream_key, axis), (), 0, length) for axis, length in enumerate(result.shape)]
    longest = result.shape.index(max(result.shape))
    next_to = spot[:longest] + [(spot[longest] + 1) % result.shape[longest]] + spot[longest + 1:]
    return result.at[tuple(spot)].set(low).at[tuple(next_to)].set(high)


def level_of(key, shape, pieces, low, largest):
    factor_of, own = 1.0, jax.random.fold_in(key, 6)
    for position, blocks in pieces:
        heights = jnp.exp(jax.random.uniform(jax.random.fold_in(own, position), (blocks,), jnp.float32, low / len(pieces), largest / len(pieces)))
        factor_of = factor_of * jnp.repeat(heights, shape[position] // blocks).reshape([-1 if axis == position else 1 for axis in range(len(shape))])
    return factor_of


def noise(own_key, dims, deviation, bound, pieces=(), held_as=jnp.bfloat16):
    result = deviation * jax.random.normal(own_key, dims, jnp.float32)
    if pieces:
        result = result * level_of(own_key, dims, pieces, -0.22, 0.18)
    return jnp.clip(result, -bound, bound).astype(held_as)


def setup_inputs(seed: int = 0) -> dict:
    streams_of = jax.random.split(jax.random.key(seed), 16)
    inputs = noise(streams_of[0], (SEQS, TGT, D), 1.0, 6.0, ((0, 32),))
    encoded = noise(streams_of[1], (SEQS, MEM, D), 1.0, 6.0, ((0, 32),))
    target_lengths = draw_target_lengths(jax.random.fold_in(streams_of[15], 71), 0)
    memory_lengths = draw_memory_lengths(jax.random.fold_in(streams_of[15], 71), 0)
    buckets = with_ends(jax.random.randint(streams_of[4], (TGT, TGT), 0, NB), jax.random.fold_in(streams_of[4], 1), 0, NB - 1).astype(jnp.int32)
    cotangent = noise(streams_of[5], (SEQS, TGT, D), 1.0, 6.0, ((0, 32),))
    self_inward = noise(streams_of[6], (D, 3 * D), D ** -0.5, 0.21875, ((0, 16), (1, 2)))
    self_outward = noise(streams_of[7], (D, D), (max(D // 64, 1)) ** -0.5, 1.75, ((0, 16), (1, 2)))
    cross_query = noise(streams_of[8], (D, D), D ** -0.5, 0.21875, ((0, 16), (1, 2)))
    cross_reader = noise(streams_of[9], (D, 2 * D), D ** -0.5, 0.21875, ((0, 16), (1, 2)))
    cross_writer = noise(streams_of[10], (D, D), (max(D // 256, 1)) ** -0.5, 3.5, ((0, 16), (1, 2)))
    expand_weight = noise(streams_of[11], (D, FF), D ** -0.5, 0.21875, ((0, 16), (1, 2)))
    shrink_weight = noise(streams_of[12], (FF, D), (max(FF // 8, 1)) ** -0.5, 0.3125, ((0, 16), (1, 2)))
    norm_gains = jnp.clip(1.0 + 0.1 * jax.random.normal(streams_of[13], (3, D), jnp.float32), 0.5, 1.5)
    bias_table = noise(streams_of[14], (NB, HEADS), 1.0, 5.0, (), jnp.float32)
    return {"inputs": inputs, "encoded": encoded, "target_lengths": target_lengths, "memory_lengths": memory_lengths, "buckets": buckets, "cotangent": cotangent, "self_inward": self_inward, "self_outward": self_outward, "cross_query": cross_query, "cross_reader": cross_reader, "cross_writer": cross_writer, "expand_weight": expand_weight, "shrink_weight": shrink_weight, "norm_gains": norm_gains, "bias_table": bias_table}


EPS = 1e-06
TINY = 1e-30
NEGATIVE = -1e+30
HIGHEST = lax.Precision.HIGHEST

@jax.custom_vjp
def low(v):
    return lax.optimization_barrier(v.astype(jnp.bfloat16)).astype(jnp.float32)

@jax.custom_vjp
def low_back(v):
    return v

def low_keep(v):
    return (low(v), None)

def low_pass(kept, grad):
    return (grad,)

def back_keep(v):
    return (v, None)

def back_low(kept, grad):
    return (low(grad),)
low.defvjp(low_keep, low_pass)
low_back.defvjp(back_keep, back_low)

def both(values):
    return low_back(low(values))

def norm_row(values, gain):
    return values * lax.rsqrt(lax.optimization_barrier(jnp.mean(values * values, axis=-1, keepdims=True)) + EPS) * gain

def matmul(left, right):
    return jnp.dot(left, right, precision=HIGHEST)

def attend(query, keys, values, extra, allowed):
    scores = jnp.einsum('qhd,khd->hqk', query, keys, precision=HIGHEST) * DH ** (-0.5) + extra
    scores = jnp.where(allowed, low_back(scores), NEGATIVE)
    probs = jax.nn.softmax(scores, axis=-1)
    mixed = jnp.einsum('hqk,khd->qhd', low(probs), values, precision=HIGHEST)
    return both(mixed.reshape(query.shape[0], HEADS * DH))

def factored(grad):
    square = grad * grad + TINY
    rows = lax.optimization_barrier(jnp.mean(square, axis=1))
    cols = lax.optimization_barrier(jnp.mean(square, axis=0))
    step = grad * lax.rsqrt(rows[:, None] * cols[None, :] / jnp.mean(rows))
    return (step, rows, cols)

def reference(inputs, encoded, target_lengths, memory_lengths, buckets, cotangent, self_inward, self_outward, cross_query, cross_reader, cross_writer, expand_weight, shrink_weight, norm_gains, bias_table):
    places = jnp.arange(TGT)
    causal = (places[None, :] <= places[:, None])[None]
    memory_places = jnp.arange(MEM)

    def forward(state, memory, inward, outward, asking, reader, writer, expand, shrink, gains, table):
        extra = jnp.transpose(table[buckets], (2, 0, 1))

        def single(item):
            values, memory_rows, target_length, memory_length = item
            first = low(norm_row(values, gains[0]))
            packed = both(matmul(first, inward)).reshape(TGT, 3, HEADS, DH)
            mixed = attend(packed[:, 0], packed[:, 1], packed[:, 2], extra, causal)
            after_self = values + low_back(matmul(mixed, outward))
            second = low(norm_row(after_self, gains[1]))
            asks = both(matmul(second, asking)).reshape(TGT, HEADS, DH)
            pairs = both(matmul(memory_rows, reader)).reshape(MEM, 2, HEADS, DH)
            allowed = (memory_places < memory_length)[None, None, :]
            crossed = attend(asks, pairs[:, 0], pairs[:, 1], 0.0, allowed)
            after_cross = after_self + low_back(matmul(crossed, writer))
            third = low(norm_row(after_cross, gains[2]))
            before = low_back(matmul(third, expand))
            hidden = low(jax.nn.gelu(before, approximate=False))
            output = after_cross + low_back(matmul(hidden, shrink))
            return output * (places < target_length)[:, None].astype(jnp.float32)
        return lax.map(jax.checkpoint(single), (state, memory, target_lengths, memory_lengths))
    output, pull = jax.vjp(forward, inputs.astype(jnp.float32), encoded.astype(jnp.float32), self_inward.astype(jnp.float32), self_outward.astype(jnp.float32), cross_query.astype(jnp.float32), cross_reader.astype(jnp.float32), cross_writer.astype(jnp.float32), expand_weight.astype(jnp.float32), shrink_weight.astype(jnp.float32), norm_gains, bias_table)
    grads = pull(cotangent.astype(jnp.float32))
    stats = [factored(grads[2 + index]) for index in range(7)]
    return (output.astype(jnp.bfloat16), grads[0], grads[1], grads[2], stats[0][0], stats[0][1], stats[0][2], grads[3], stats[1][0], stats[1][1], stats[1][2], grads[4], stats[2][0], stats[2][1], stats[2][2], grads[5], stats[3][0], stats[3][1], stats[3][2], grads[6], stats[4][0], stats[4][1], stats[4][2], grads[7], stats[5][0], stats[5][1], stats[5][2], grads[8], stats[6][0], stats[6][1], stats[6][2], grads[9], grads[10])
```

```python
import functools

import jax
import jax.numpy as jnp
from jax import lax
from jax.experimental import pallas as pl
from jax.experimental.pallas import tpu as pltpu
from jax.sharding import PartitionSpec as P

HEADS = 12
DH = 64
EPS = 1e-06
TINY = 1e-30
NEGATIVE = -1e30
SCALE = DH ** (-0.5)

BF = jnp.bfloat16
F32 = jnp.float32
BOTH = ("wide", "narrow")
VMEM_LIMIT = 56 * 1024 * 1024
KEY_TILE = 256

COUNTS = {
    "inward": 3,
    "outward": 1,
    "query": 1,
    "reader": 2,
    "writer": 1,
    "expand": 4,
    "shrink": 4,
}
NAMES = ("inward", "outward", "query", "reader", "writer", "expand", "shrink")
GATHERS = (
    ("x", ("inward", "outward", "query")),
    ("y", ("reader", "writer")),
    ("x", ("expand",)),
    ("y", ("shrink",)),
)


def nn(left, right):
    return lax.dot_general(left, right, (((1,), (0,)), ((), ())), preferred_element_type=F32)


def nt(left, right):
    return lax.dot_general(left, right, (((1,), (1,)), ((), ())), preferred_element_type=F32)


def tn(left, right):
    return lax.dot_general(left, right, (((0,), (0,)), ((), ())), preferred_element_type=F32)


VM = pl.BlockSpec(memory_space=pltpu.VMEM)
SM = pl.BlockSpec(memory_space=pltpu.SMEM)
HB = pl.BlockSpec(memory_space=pl.ANY)


def launch(body, ins, outs, scratch=(), grid=None, alias=None, gflop=1.0, name=None):
    arrays = [a for a, _ in ins]
    return pl.pallas_call(
        body,
        grid=grid if grid is not None else (),
        in_specs=[s for _, s in ins],
        out_specs=[s for _, s in outs],
        out_shape=[o for o, _ in outs],
        scratch_shapes=list(scratch),
        input_output_aliases=alias or {},
        compiler_params=pltpu.CompilerParams(vmem_limit_bytes=VMEM_LIMIT),
        cost_estimate=pl.CostEstimate(
            flops=int(gflop * 1e9), bytes_accessed=1 << 22, transcendentals=0
        ),
        name=name,
    )(*arrays)


def shape(dims, dtype):
    return jax.ShapeDtypeStruct(tuple(dims), dtype)


def weight_scratch(name, width):
    if name == "shrink":
        return pltpu.VMEM((4, 2, 2, 4, width // 16, width), BF)
    return pltpu.VMEM((4, 2, 2, width // 16, width * COUNTS[name]), BF)


class Held:
    def __init__(self, arrays, first, start):
        self.arrays, self.first, self.start = tuple(arrays), first, start

    def ins(self):
        return [(a, HB) for a in self.arrays]


def load(name, held, refs, scratch, me, sem):
    if len(refs) == 1:
        pltpu.make_async_copy(refs[0], scratch, sem).start()
        return
    count = COUNTS[name]
    piece = refs[0].shape[-1]
    for a in range(2):
        for b in range(2):
            for k in range(2):
                c = me[2] ^ b
                if held.first == "x":
                    x, y = me[1] ^ k, me[3] ^ a
                else:
                    x, y = me[1] ^ a, me[3] ^ k
                for p in range(count):
                    src = refs[a * 2 + b].at[k, :, held.start + p]
                    if name == "shrink":
                        cols = pl.ds(pl.multiple_of(y * piece, 128), piece)
                        dst = scratch.at[:, x, c, p, :, cols]
                    else:
                        cols = pl.ds(pl.multiple_of((y * count + p) * piece, 128), piece)
                        dst = scratch.at[:, x, c, :, cols]
                    pltpu.make_async_copy(src, dst, sem).start()


def arrived(scratch, sem):
    pltpu.make_async_copy(scratch, scratch, sem).wait()


def store(name, scratch, outs, start, me, sem):
    if len(outs) == 1:
        pltpu.make_async_copy(scratch, outs[0], sem).start()
        return
    count = COUNTS[name]
    piece = outs[0].shape[-1]
    for b in range(2):
        c = me[2] ^ b
        for y in range(2):
            for p in range(count):
                if name == "shrink":
                    src = scratch.at[:, :, c, p, :, pl.ds(y * piece, piece)]
                else:
                    src = scratch.at[:, :, c, :, pl.ds((y * count + p) * piece, piece)]
                pltpu.make_async_copy(src, outs[b].at[:, :, y, start + p], sem).start()


def flat(block):
    return block.reshape(-1, block.shape[-1])


def put_rows(scratch, value, cols):
    scratch[:, :, :, :, cols] = value.reshape(scratch.shape[:4] + (value.shape[-1],))


def normed(values, gain):
    r = lax.rsqrt(jnp.mean(values * values, axis=-1, keepdims=True) + EPS)
    return values * r * gain


def norm_back(values, gain, grad):
    r = lax.rsqrt(jnp.mean(values * values, axis=-1, keepdims=True) + EPS)
    inner = jnp.mean(values * gain * grad, axis=-1, keepdims=True)
    back = r * gain * grad - values * (r * r * r * inner)
    return back, jnp.sum(grad * values * r, axis=0, keepdims=True)


def prepare_kernel(lens, x, cot, gains, buckets, table, n1, kept, bias):
    rows = cot.shape[1]
    for s in range(x.shape[0]):
        values = x[s].astype(F32)
        n1[s * rows : (s + 1) * rows, :] = normed(values, gains[0:1, :]).astype(BF)
        keep = lax.broadcasted_iota(jnp.int32, (rows, 1), 0) < lens[s]
        kept[s * rows : (s + 1) * rows, :] = jnp.where(keep, cot[s].astype(F32), 0.0).astype(BF)
    half = 128
    heads = bias.shape[0]

    @pl.loop(0, rows // 8)
    def _(step):
        start = pl.multiple_of(step * 8, 8)
        for side in range(rows // half):
            which = buckets[pl.ds(start, 8), side * half : (side + 1) * half]
            key = start + lax.broadcasted_iota(jnp.int32, (8, half), 0)
            query = side * half + lax.broadcasted_iota(jnp.int32, (8, half), 1)
            for h in range(heads):
                row = jnp.broadcast_to(table[h : h + 1, :], (8, half))
                found = jnp.take_along_axis(row, which, axis=1)
                bias[h, pl.ds(start, 8), side * half : (side + 1) * half] = jnp.where(
                    key <= query, found, NEGATIVE
                )


def head_parts(block):
    lane = lax.broadcasted_iota(jnp.int32, block.shape, 1)
    zero = jnp.zeros_like(block)
    return jnp.where(lane < DH, block, zero), jnp.where(lane < DH, zero, block)


def forward_pair(query, keys, values, fix, mixed, logsum):
    parts = head_parts(query * jnp.asarray(SCALE, BF))
    tops = []
    for h in range(2):
        scores = fix(nt(keys, parts[h]), h)
        highest = jnp.max(scores, axis=0, keepdims=True)
        weights = jnp.exp(scores - highest)
        total = jnp.sum(weights, axis=0, keepdims=True)
        raw = tn(values, weights.astype(BF))
        tops.append(raw[h * DH : (h + 1) * DH, :] * (1.0 / total))
        logsum[0, h : h + 1, :] = highest + jnp.log(total)
    mixed[...] = jnp.concatenate(tops, axis=0).T.astype(BF)


def backward_pair(query, keys, values, grad, fix, logsum, each):
    scaled = head_parts(query * jnp.asarray(SCALE, BF))
    grads = head_parts(grad)
    grad_keys = grad_values = 0.0
    tops = []
    for h in range(2):
        scores = fix(nt(keys, scaled[h]), h)
        probs = jnp.exp(scores - logsum[0, h : h + 1, :])
        grad_probs = nt(values, grads[h])
        inner = jnp.sum(probs * grad_probs, axis=0, keepdims=True)
        grad_scores = (probs * (grad_probs - inner)).astype(BF)
        each(h, grad_scores)
        grad_values = grad_values + nn(probs.astype(BF), grads[h])
        grad_keys = grad_keys + nn(grad_scores, scaled[h])
        raw = tn(keys, grad_scores)
        tops.append(raw[h * DH : (h + 1) * DH, :] * SCALE)
    return jnp.concatenate(tops, axis=0).T, grad_keys, grad_values


def self_forward_kernel(query, keys, values, bias, mixed, logsum):
    def fix(scores, h):
        return scores + bias[h]

    forward_pair(query[...], keys[...], values[...], fix, mixed, logsum)


def self_backward_kernel(
    query, keys, values, grad, bias, logsum, grad_query, grad_keys, grad_values, grad_bias
):
    first = pl.program_id(1) == 0

    def fix(scores, h):
        return scores + bias[h]

    def each(h, grad_scores):
        grown = grad_scores.astype(F32)
        grad_bias[h] = jnp.where(first, grown, grad_bias[h] + grown)

    gq, gk, gv = backward_pair(query[...], keys[...], values[...], grad[...], fix, logsum, each)
    grad_query[...] = gq.astype(BF)
    grad_keys[...] = gk.astype(BF)
    grad_values[...] = gv.astype(BF)


def masked_last(valid, size):
    def fix(scores, h):
        head, tail = scores[: size - KEY_TILE], scores[size - KEY_TILE :]
        place = size - KEY_TILE + lax.broadcasted_iota(jnp.int32, tail.shape, 0)
        tail = jnp.where(place < valid, tail, NEGATIVE)
        return jnp.concatenate((head, tail), axis=0) if size > KEY_TILE else tail

    return fix


def cross_forward_kernel(lens, query, keys, values, mixed, logsum):
    valid = lens[pl.program_id(0)]
    for tiles in range(1, keys.shape[0] // KEY_TILE + 1):

        @pl.when((valid + KEY_TILE - 1) // KEY_TILE == tiles)
        def _():
            size = tiles * KEY_TILE
            forward_pair(
                query[...], keys[:size], values[:size], masked_last(valid, size), mixed, logsum
            )


def cross_backward_kernel(
    lens, query, keys, values, grad, logsum, grad_query, grad_keys, grad_values
):
    valid = lens[pl.program_id(0)]
    for tiles in range(1, keys.shape[0] // KEY_TILE + 1):

        @pl.when((valid + KEY_TILE - 1) // KEY_TILE == tiles)
        def _():
            size = tiles * KEY_TILE
            gq, gk, gv = backward_pair(
                query[...],
                keys[:size],
                values[:size],
                grad[...],
                masked_last(valid, size),
                logsum,
                lambda h, g: None,
            )
            grad_query[...] = gq.astype(BF)
            grad_keys[:size] = gk.astype(BF)
            grad_values[:size] = gv.astype(BF)


def pair_spec(rows, base=0, flip=False):
    if flip:
        return pl.BlockSpec((rows, 128), lambda p, s: (s, base + p))
    return pl.BlockSpec((rows, 128), lambda s, p: (s, base + p))


def inward_kernel(held, me, n1, *rest):
    refs, (packed, weight, sem) = rest[: len(held.arrays)], rest[len(held.arrays) :]
    load("inward", held, refs, weight, me, sem)
    arrived(weight, sem)
    size = n1.shape[1]
    left = n1[...]
    for block in range(3):
        cols = slice(block * size, (block + 1) * size)
        packed[:, cols] = nn(left, flat(weight[..., cols])).astype(BF)


def memory_kernel(held, me, lens, encoded, *rest):
    refs, (pairs, weight, sem) = rest[: len(held.arrays)], rest[len(held.arrays) :]
    step = pl.program_id(0)
    tiles = pl.num_programs(0) // lens.shape[0]

    @pl.when(step == 0)
    def _():
        load("reader", held, refs, weight, me, sem)
        arrived(weight, sem)

    @pl.when(lax.rem(step, tiles) * KEY_TILE < lens[step // tiles])
    def _():
        size = encoded.shape[1]
        left = encoded[...]
        for block in range(2):
            cols = slice(block * size, (block + 1) * size)
            pairs[:, cols] = nn(left, flat(weight[..., cols])).astype(BF)


def middle_kernel(held_out, held_query, me, x, mixed, gains, *rest):
    k = len(held_out.arrays)
    refs_out, refs_query = rest[:k], rest[k : 2 * k]
    after, n2, asks, weight_out, weight_query, sems = rest[2 * k :]
    load("outward", held_out, refs_out, weight_out, me, sems.at[0])
    load("query", held_query, refs_query, weight_query, me, sems.at[1])
    arrived(weight_out, sems.at[0])
    values = x[...].astype(F32) + nn(mixed[...], flat(weight_out[...]))
    after[...] = values
    second = normed(values, gains[1:2, :]).astype(BF)
    n2[...] = second
    arrived(weight_query, sems.at[1])
    asks[...] = nn(second, flat(weight_query[...])).astype(BF)


def gelu_parts(v):
    phi = 0.5 * (1.0 + lax.erf(v * (0.5**0.5)))
    density = jnp.exp(-0.5 * v * v) * 0.3989422804014327
    return v * phi, phi + v * density


def widen_kernel(held_writer, held_expand, me, after_self, mixed, gains, kept, *rest):
    k = len(held_writer.arrays)
    refs_writer, refs_expand = rest[:k], rest[k : 2 * k]
    outs = rest[2 * k :]
    after_cross, n3, hidden, slope = outs[:4]
    grads, (weight_writer, weight_expand, shrink_grad, sems) = outs[4:-4], outs[-4:]
    load("writer", held_writer, refs_writer, weight_writer, me, sems.at[0])
    load("expand", held_expand, refs_expand, weight_expand, me, sems.at[1])
    arrived(weight_writer, sems.at[0])
    values = after_self[...] + nn(mixed[...], flat(weight_writer[...]))
    after_cross[...] = values
    n3[...] = normed(values, gains[2:3, :]).astype(BF)
    arrived(weight_expand, sems.at[1])
    size = n3.shape[1]

    @pl.loop(0, 4)
    def _(z):
        cols = pl.ds(pl.multiple_of(z * size, 128), size)
        before = nn(n3[...], flat(weight_expand[:, :, :, :, cols]))
        active, gate = gelu_parts(before)
        active = active.astype(BF)
        hidden[:, cols] = active
        slope[:, cols] = gate.astype(BF)
        grad = tn(active, kept[...]).astype(BF)
        shrink_grad[z] = grad.reshape(shrink_grad.shape[1:])

    store("shrink", shrink_grad, grads, 0, me, sems.at[2])
    arrived(shrink_grad, sems.at[2])


def narrow_kernel(
    held_shrink, held_expand, me, lens, after_cross, n3, hidden, slope, kept, gains, *rest
):
    k = len(held_shrink.arrays)
    refs_shrink, refs_expand = rest[:k], rest[k : 2 * k]
    outs = rest[2 * k :]
    layer_out, grad_cross, gain_part = outs[:3]
    grads, (weight_shrink, weight_expand, expand_grad, grad_norm, total, sems) = (
        outs[3:-6],
        outs[-6:],
    )
    load("shrink", held_shrink, refs_shrink, weight_shrink, me, sems.at[0])
    load("expand", held_expand, refs_expand, weight_expand, me, sems.at[1])
    size = n3.shape[1]
    total[...] = after_cross[...]
    grad_norm[...] = jnp.zeros_like(grad_norm)
    arrived(weight_shrink, sems.at[0])
    arrived(weight_expand, sems.at[1])

    @pl.loop(0, 4)
    def _(z):
        cols = pl.ds(pl.multiple_of(z * size, 128), size)
        shrink_rows = flat(weight_shrink[z])
        grad = (slope[:, cols].astype(F32) * nt(kept[...], shrink_rows)).astype(BF)
        put_rows(expand_grad, tn(n3[...], grad).astype(BF), cols)
        grad_norm[...] += nt(grad, flat(weight_expand[:, :, :, :, cols]))
        total[...] += nn(hidden[:, cols], shrink_rows)

    store("expand", expand_grad, grads, 0, me, sems.at[2])
    rows = total.shape[0] // lens.shape[0]
    for s in range(lens.shape[0]):
        part = slice(s * rows, (s + 1) * rows)
        keep = lax.broadcasted_iota(jnp.int32, (rows, 1), 0) < lens[s]
        layer_out[s] = jnp.where(keep, total[part, :], 0.0).astype(BF)
    back, gain = norm_back(after_cross[...], gains[2:3, :], grad_norm[...])
    grad_cross[...] = kept[...].astype(F32) + back
    gain_part[...] = gain
    arrived(expand_grad, sems.at[2])


def writer_back_kernel(held, me, grad_cross, mixed, *rest):
    k = len(held.arrays)
    refs, outs = rest[:k], rest[k:]
    grad_mixed, grads, (weight, grad_scratch, sems) = outs[0], outs[1:-3], outs[-3:]
    load("writer", held, refs, weight, me, sems.at[0])
    branch = grad_cross[...].astype(BF)
    put_rows(grad_scratch, tn(mixed[...], branch).astype(BF), slice(None))
    store("writer", grad_scratch, grads, 0, me, sems.at[1])
    arrived(weight, sems.at[0])
    grad_mixed[...] = nt(branch, flat(weight[...])).astype(BF)
    arrived(grad_scratch, sems.at[1])


def query_back_kernel(
    packed_mode,
    held_query,
    held_out,
    me,
    grad_asks,
    n2,
    after_self,
    grad_cross,
    mixed,
    gains,
    *rest,
):
    k = len(held_query.arrays)
    refs_query, refs_out = rest[:k], rest[k : 2 * k]
    rest = rest[2 * k :]
    if packed_mode:
        rest = rest[2:]
    grad_self, grad_mixed, gain_part = rest[:3]
    weight_query, weight_out, query_grad, out_grad, sems = rest[-5:]
    grads = rest[3:-5]
    load("query", held_query, refs_query, weight_query, me, sems.at[0])
    load("outward", held_out, refs_out, weight_out, me, sems.at[1])
    put_rows(query_grad, tn(n2[...], grad_asks[...]).astype(BF), slice(None))
    store("query", query_grad, grads if packed_mode else grads[:1], 1, me, sems.at[2])
    arrived(weight_query, sems.at[0])
    back, gain = norm_back(
        after_self[...], gains[1:2, :], nt(grad_asks[...], flat(weight_query[...]))
    )
    total = grad_cross[...] + back
    grad_self[...] = total
    gain_part[...] = gain
    branch = total.astype(BF)
    arrived(weight_out, sems.at[1])
    grad_mixed[...] = nt(branch, flat(weight_out[...])).astype(BF)
    put_rows(out_grad, tn(mixed[...], branch).astype(BF), slice(None))
    store("outward", out_grad, grads if packed_mode else grads[1:], 2, me, sems.at[3])
    arrived(query_grad, sems.at[2])
    arrived(out_grad, sems.at[3])


def inward_grad_kernel(me, n1, gq, gk, gv, *rest):
    grads, (scratch, sem) = rest[:-2], rest[-2:]
    size = n1.shape[1]
    for block, grad in enumerate((gq, gk, gv)):
        cols = slice(block * size, (block + 1) * size)
        put_rows(scratch, tn(n1[...], grad[...]).astype(BF), cols)
    store("inward", scratch, grads, 0, me, sem)
    arrived(scratch, sem)


def inputs_grad_kernel(held, me, x, gq, gk, gv, grad_self, gains, *rest):
    k = len(held.arrays)
    refs, (out, gain_part, weight, sem) = rest[:k], rest[k:]
    load("inward", held, refs, weight, me, sem)
    arrived(weight, sem)
    size = x.shape[1]
    total = 0.0
    for block, grad in enumerate((gq, gk, gv)):
        cols = slice(block * size, (block + 1) * size)
        total = total + nt(grad[...], flat(weight[..., cols]))
    back, gain = norm_back(x[...].astype(F32), gains[0:1, :], total)
    out[...] = grad_self[...] + back
    gain_part[...] = gain


def reader_grad_kernel(packed_mode, me, lens, encoded, gk, gv, *rest):
    if packed_mode:
        rest = rest[2:]
    grads, (scratch, total, sem) = rest[:-3], rest[-3:]
    step = pl.program_id(0)
    steps = pl.num_programs(0)
    tiles = steps // lens.shape[0]
    size = encoded.shape[1]

    @pl.when(step == 0)
    def _():
        total[...] = jnp.zeros_like(total)

    @pl.when(lax.rem(step, tiles) * KEY_TILE < lens[step // tiles])
    def _():
        left = encoded[...]
        total[:, :size] += tn(left, gk[...])
        total[:, size:] += tn(left, gv[...])

    @pl.when(step == steps - 1)
    def _():
        put_rows(scratch, total[...].astype(BF), slice(None))
        store("reader", scratch, grads, 3, me, sem)
        arrived(scratch, sem)


def encoded_grad_kernel(held, me, lens, gk, gv, *rest):
    refs, (out, weight, sem) = rest[: len(held.arrays)], rest[len(held.arrays) :]
    step = pl.program_id(0)
    tiles = pl.num_programs(0) // lens.shape[0]
    valid = lax.rem(step, tiles) * KEY_TILE < lens[step // tiles]
    size = gk.shape[1]

    @pl.when(step == 0)
    def _():
        load("reader", held, refs, weight, me, sem)
        arrived(weight, sem)

    @pl.when(valid)
    def _():
        out[...] = nt(gk[...], flat(weight[..., :size])) + nt(gv[...], flat(weight[..., size:]))

    @pl.when(jnp.logical_not(valid))
    def _():
        out[...] = jnp.zeros_like(out)


def table_kernel(buckets, grad_bias, out):
    heads = grad_bias.shape[0]

    @pl.loop(0, out.shape[0])
    def _(b):
        hit = buckets[...] == b
        for h in range(heads):
            out[b, h : h + 1, :] = jnp.sum(
                jnp.where(hit, grad_bias[h], 0.0), axis=0, keepdims=True
            )


class Hyper:
    MASKS = {"y": 1, "c": 2, "x": 4, "z1": 8, "z2": 16}

    def __init__(self):
        wide = lax.axis_index("wide")
        self.z, self.x, self.c = wide // 4, (wide // 2) % 2, wide % 2
        self.y = lax.axis_index("narrow")
        self.me = jnp.stack((self.z, self.x, self.c, self.y)).astype(jnp.int32)

    def swap(self, value, bit):
        mask = self.MASKS[bit]
        return lax.ppermute(value, BOTH, [(i, i ^ mask) for i in range(32)])

    def gather(self, shard, first):
        second = "y" if first == "x" else "x"
        other = self.swap(shard, "z1")
        pair = jnp.where(
            self.z % 2 == 0, jnp.stack((shard, other)), jnp.stack((other, shard))
        )
        other = self.swap(pair, "z2")
        quad = jnp.where(
            self.z // 2 == 0, jnp.concatenate((pair, other)), jnp.concatenate((other, pair))
        )
        near = jnp.stack((quad, self.swap(quad, first)))
        far = self.swap(near, second)
        return near, self.swap(near, "c"), far, self.swap(far, "c")

    def scatter(self, keep, send, first):
        where = {"x": self.x, "y": self.y}
        axis = {"x": 1, "y": 2}
        second = "y" if first == "x" else "x"
        parts = [keep, self.swap(send, "c")]

        def add(pick):
            return sum(pick(p).astype(F32) for p in parts)

        pick = functools.partial(lax.dynamic_slice_in_dim, slice_size=1, axis=axis[first])
        sent = add(lambda p: pick(p, 1 - where[first])).astype(BF)
        other = self.swap(sent, first)
        parts = [pick(p, where[first]) for p in parts] + [other]
        pick2 = functools.partial(lax.dynamic_slice_in_dim, slice_size=1, axis=axis[second])
        sent = add(lambda p: pick2(p, 1 - where[second])).astype(BF)
        other = self.swap(sent, second)
        parts = [pick2(p, where[second]) for p in parts] + [other]
        half = self.z // 2
        pick3 = functools.partial(lax.dynamic_slice_in_dim, slice_size=2, axis=0)
        sent = add(lambda p: pick3(p, (1 - half) * 2)).astype(BF)
        other = self.swap(sent, "z2")
        parts = [pick3(p, half * 2) for p in parts] + [other]
        low = self.z % 2
        pick4 = functools.partial(lax.dynamic_slice_in_dim, slice_size=1, axis=0)
        sent = add(lambda p: pick4(p, 1 - low)).astype(BF)
        other = self.swap(sent, "z1")
        parts = [pick4(p, low) for p in parts] + [other]
        return add(lambda p: p)[0, 0, 0]

    def total(self, value, bits):
        for bit in bits:
            value = value + self.swap(value, bit)
        return value


def cut(name, shard, width):
    count = COUNTS[name]
    if name == "shrink":
        return shard.reshape(count, shard.shape[0] // count, shard.shape[1])
    rows, cols = shard.shape
    return jnp.transpose(shard.reshape(rows, count, cols // count), (1, 0, 2))


def uncut(name, pieces):
    count, rows, cols = pieces.shape
    if name == "shrink":
        return pieces.reshape(count * rows, cols)
    return jnp.transpose(pieces, (1, 0, 2)).reshape(rows, count * cols)


def whole_shape(name, width):
    if name == "shrink":
        return (4, 2, 2, 4, width // 16, width)
    return (4, 2, 2, width // 16, width * COUNTS[name])


def local(
    inputs,
    encoded,
    target_lengths,
    memory_lengths,
    buckets,
    cotangent,
    self_inward,
    self_outward,
    cross_query,
    cross_reader,
    cross_writer,
    expand_weight,
    shrink_weight,
    norm_gains,
    bias_table,
):
    wide_count = lax.axis_size("wide")
    narrow_count = lax.axis_size("narrow")
    fast = (wide_count, narrow_count) == (16, 2)
    seqs, length, width = inputs.shape
    memory_size = encoded.shape[1]
    rows, mem_rows = seqs * length, seqs * memory_size
    wide_hidden = expand_weight.shape[1] * narrow_count
    shards = dict(
        zip(
            NAMES,
            (
                self_inward,
                self_outward,
                cross_query,
                cross_reader,
                cross_writer,
                expand_weight,
                shrink_weight,
            ),
        )
    )
    hyper = Hyper() if fast else None
    me = hyper.me if fast else jnp.zeros((4,), jnp.int32)

    held = {}
    if fast:
        for first, names in GATHERS:
            packed = jnp.concatenate([cut(name, shards[name], width) for name in names])
            near, near_c, far, far_c = hyper.gather(packed, first)
            start = 0
            for name in names:
                held[name] = Held((near, near_c, far, far_c), first, start)
                start += COUNTS[name]
    else:
        for name in NAMES:
            full = lax.all_gather(shards[name], "narrow", axis=1, tiled=True)
            full = lax.all_gather(full, "wide", axis=0, tiled=True)
            held[name] = Held((full.reshape(whole_shape(name, width)),), "x", 0)

    def grad_outs(name, count):
        if fast:
            block = shape((4, 2, 2, count, width // 16, width // 2), BF)
            return [(block, HB), (block, HB)]
        return [(shape(whole_shape(name, width), BF), HB)]

    dma = pltpu.SemaphoreType.DMA
    x_rows = inputs.reshape(rows, width)
    mem_flat = encoded.reshape(mem_rows, width)
    heads = HEADS
    pairs_count = heads // 2
    turned = buckets.T
    table = jnp.pad(bias_table.T, ((0, 0), (0, 128 - bias_table.shape[0])))

    n1, kept, bias = launch(
        prepare_kernel,
        [(target_lengths, SM), (inputs, VM), (cotangent, VM), (norm_gains, VM), (turned, VM), (table, VM)],
        [
            (shape((rows, width), BF), VM),
            (shape((rows, width), BF), VM),
            (shape((heads, length, length), F32), VM),
        ],
        name="prepare",
    )

    (packed,) = launch(
        functools.partial(inward_kernel, held["inward"]),
        [(me, SM), (n1, VM)] + held["inward"].ins(),
        [(shape((rows, 3 * width), BF), VM)],
        [weight_scratch("inward", width), dma],
        gflop=2.0,
        name="inward",
    )

    bias_spec = pl.BlockSpec((2, length, length), lambda s, p: (p, 0, 0))
    log_spec = pl.BlockSpec((1, 2, length), lambda s, p: (s * pairs_count + p, 0, 0))
    self_mixed, self_log = launch(
        self_forward_kernel,
        [
            (packed, pair_spec(length)),
            (packed, pair_spec(length, pairs_count)),
            (packed, pair_spec(length, 2 * pairs_count)),
            (bias, bias_spec),
        ],
        [
            (shape((rows, width), BF), pair_spec(length)),
            (shape((seqs * pairs_count, 2, length), F32), log_spec),
        ],
        grid=(seqs, pairs_count),
        gflop=3.0,
        name="self_forward",
    )

    (pairs,) = launch(
        functools.partial(memory_kernel, held["reader"]),
        [(me, SM), (memory_lengths, SM), (mem_flat, pl.BlockSpec((KEY_TILE, width), lambda i: (i, 0)))]
        + held["reader"].ins(),
        [(shape((mem_rows, 2 * width), BF), pl.BlockSpec((KEY_TILE, 2 * width), lambda i: (i, 0)))],
        [weight_scratch("reader", width), dma],
        grid=(mem_rows // KEY_TILE,),
        gflop=5.0,
        name="memory",
    )

    after_self, n2, asks = launch(
        functools.partial(middle_kernel, held["outward"], held["query"]),
        [(me, SM), (x_rows, VM), (self_mixed, VM), (norm_gains, VM)]
        + held["outward"].ins()
        + held["query"].ins(),
        [
            (shape((rows, width), F32), VM),
            (shape((rows, width), BF), VM),
            (shape((rows, width), BF), VM),
        ],
        [weight_scratch("outward", width), weight_scratch("query", width), dma((2,))],
        gflop=2.0,
        name="middle",
    )

    cross_mixed, cross_log = launch(
        cross_forward_kernel,
        [
            (memory_lengths, SM),
            (asks, pair_spec(length)),
            (pairs, pair_spec(memory_size)),
            (pairs, pair_spec(memory_size, pairs_count)),
        ],
        [
            (shape((rows, width), BF), pair_spec(length)),
            (shape((seqs * pairs_count, 2, length), F32), log_spec),
        ],
        grid=(seqs, pairs_count),
        gflop=10.0,
        name="cross_forward",
    )

    after_cross, n3, hidden, slope, *shrink_parts = launch(
        functools.partial(widen_kernel, held["writer"], held["expand"]),
        [(me, SM), (after_self, VM), (cross_mixed, VM), (norm_gains, VM), (kept, VM)]
        + held["writer"].ins()
        + held["expand"].ins(),
        [
            (shape((rows, width), F32), VM),
            (shape((rows, width), BF), VM),
            (shape((rows, wide_hidden), BF), VM),
            (shape((rows, wide_hidden), BF), VM),
        ]
        + grad_outs("shrink", 4),
        [
            weight_scratch("writer", width),
            weight_scratch("expand", width),
            weight_scratch("shrink", width),
            dma((3,)),
        ],
        gflop=10.0,
        name="widen",
    )

    layer_out, grad_cross, gain_third, *expand_parts = launch(
        functools.partial(narrow_kernel, held["shrink"], held["expand"]),
        [
            (me, SM),
            (target_lengths, SM),
            (after_cross, VM),
            (n3, VM),
            (hidden, VM),
            (slope, VM),
            (kept, VM),
            (norm_gains, VM),
        ]
        + held["shrink"].ins()
        + held["expand"].ins(),
        [
            (shape((seqs, length, width), BF), VM),
            (shape((rows, width), F32), VM),
            (shape((1, width), F32), VM),
        ]
        + grad_outs("expand", 4),
        [
            weight_scratch("shrink", width),
            weight_scratch("expand", width),
            weight_scratch("expand", width),
            pltpu.VMEM((rows, width), F32),
            pltpu.VMEM((rows, width), F32),
            dma((3,)),
        ],
        gflop=14.0,
        name="narrow",
    )

    grad_mixed, *rest_parts = launch(
        functools.partial(writer_back_kernel, held["writer"]),
        [(me, SM), (grad_cross, VM), (cross_mixed, VM)] + held["writer"].ins(),
        [(shape((rows, width), BF), VM)] + grad_outs("writer", 5),
        [weight_scratch("writer", width), weight_scratch("writer", width), dma((2,))],
        gflop=2.0,
        name="writer_back",
    )
    writer_parts = rest_parts

    grad_asks, grad_mem_keys, grad_mem_values = launch(
        cross_backward_kernel,
        [
            (memory_lengths, SM),
            (asks, pair_spec(length)),
            (pairs, pair_spec(memory_size)),
            (pairs, pair_spec(memory_size, pairs_count)),
            (grad_mixed, pair_spec(length)),
            (cross_log, log_spec),
        ],
        [
            (shape((rows, width), BF), pair_spec(length)),
            (shape((mem_rows, width), BF), pair_spec(memory_size)),
            (shape((mem_rows, width), BF), pair_spec(memory_size)),
        ],
        grid=(seqs, pairs_count),
        gflop=20.0,
        name="cross_backward",
    )

    tile_spec = pl.BlockSpec((KEY_TILE, width), lambda i: (i, 0))
    into = [(a, HB) for a in rest_parts] if fast else []
    rest_parts = launch(
        functools.partial(reader_grad_kernel, fast),
        [
            (me, SM),
            (memory_lengths, SM),
            (mem_flat, tile_spec),
            (grad_mem_keys, tile_spec),
            (grad_mem_values, tile_spec),
        ]
        + into,
        grad_outs("reader", 5),
        [weight_scratch("reader", width), pltpu.VMEM((width, 2 * width), F32), dma],
        grid=(mem_rows // KEY_TILE,),
        alias={5: 0, 6: 1} if fast else None,
        gflop=5.0,
        name="reader_grad",
    )
    reader_parts = rest_parts

    into = [(a, HB) for a in rest_parts] if fast else []
    base = 7 + 2 * len(held["query"].arrays)
    grad_self, grad_mixed, gain_second, *rest_parts = launch(
        functools.partial(query_back_kernel, fast, held["query"], held["outward"]),
        [
            (me, SM),
            (grad_asks, VM),
            (n2, VM),
            (after_self, VM),
            (grad_cross, VM),
            (self_mixed, VM),
            (norm_gains, VM),
        ]
        + held["query"].ins()
        + held["outward"].ins()
        + into,
        [
            (shape((rows, width), F32), VM),
            (shape((rows, width), BF), VM),
            (shape((1, width), F32), VM),
        ]
        + (grad_outs("query", 5) if fast else grad_outs("query", 1) + grad_outs("outward", 1)),
        [
            weight_scratch("query", width),
            weight_scratch("outward", width),
            weight_scratch("query", width),
            weight_scratch("outward", width),
            dma((4,)),
        ],
        alias={base: 3, base + 1: 4} if fast else None,
        gflop=3.0,
        name="query_back",
    )

    bias_flip = pl.BlockSpec((2, length, length), lambda p, s: (p, 0, 0))
    log_flip = pl.BlockSpec((1, 2, length), lambda p, s: (s * pairs_count + p, 0, 0))
    grad_query, grad_keys, grad_values, grad_bias = launch(
        self_backward_kernel,
        [
            (packed, pair_spec(length, 0, True)),
            (packed, pair_spec(length, pairs_count, True)),
            (packed, pair_spec(length, 2 * pairs_count, True)),
            (grad_mixed, pair_spec(length, 0, True)),
            (bias, bias_flip),
            (self_log, log_flip),
        ],
        [(shape((rows, width), BF), pair_spec(length, 0, True))] * 3
        + [(shape((heads, length, length), F32), bias_flip)],
        grid=(pairs_count, seqs),
        gflop=6.0,
        name="self_backward",
    )

    inward_parts = launch(
        inward_grad_kernel,
        [(me, SM), (n1, VM), (grad_query, VM), (grad_keys, VM), (grad_values, VM)],
        grad_outs("inward", 3),
        [weight_scratch("inward", width), dma],
        gflop=2.0,
        name="inward_grad",
    )

    inputs_grad, gain_first = launch(
        functools.partial(inputs_grad_kernel, held["inward"]),
        [
            (me, SM),
            (x_rows, VM),
            (grad_query, VM),
            (grad_keys, VM),
            (grad_values, VM),
            (grad_self, VM),
            (norm_gains, VM),
        ]
        + held["inward"].ins(),
        [(shape((rows, width), F32), VM), (shape((1, width), F32), VM)],
        [weight_scratch("inward", width), dma],
        gflop=2.0,
        name="inputs_grad",
    )

    (encoded_grad,) = launch(
        functools.partial(encoded_grad_kernel, held["reader"]),
        [(me, SM), (memory_lengths, SM), (grad_mem_keys, tile_spec), (grad_mem_values, tile_spec)]
        + held["reader"].ins(),
        [(shape((mem_rows, width), F32), tile_spec)],
        [weight_scratch("reader", width), dma],
        grid=(mem_rows // KEY_TILE,),
        gflop=5.0,
        name="encoded_grad",
    )

    (table_part,) = launch(
        table_kernel,
        [(turned, VM), (grad_bias, VM)],
        [(shape((bias_table.shape[0], heads, length), F32), VM)],
        gflop=3.0,
        name="table",
    )
    table_part = jnp.sum(table_part, axis=-1)
    gains_part = jnp.concatenate((gain_first, gain_second, gain_third))

    sums = {}
    if fast:
        chunks = (
            (shrink_parts, "x", ("shrink",)),
            (expand_parts, "y", ("expand",)),
            (rest_parts, "x", ("writer", "query", "outward", "reader")),
            (inward_parts, "y", ("inward",)),
        )
        for (keep, send), first, names in chunks:
            pieces = hyper.scatter(keep, send, first)
            start = 0
            for name in names:
                sums[name] = uncut(name, pieces[start : start + COUNTS[name]])
                start += COUNTS[name]
    else:
        parts = {
            "shrink": shrink_parts[0],
            "expand": expand_parts[0],
            "writer": writer_parts[0],
            "reader": reader_parts[0],
            "query": rest_parts[0],
            "outward": rest_parts[1],
            "inward": inward_parts[0],
        }
        for name in NAMES:
            full = parts[name].reshape(-1, parts[name].shape[-1]).astype(F32)
            full = lax.psum_scatter(full, "wide", scatter_dimension=0, tiled=True)
            sums[name] = lax.psum_scatter(full, "narrow", scatter_dimension=1, tiled=True)

    row_parts = [jnp.sum(sums[name] * sums[name], axis=1) for name in NAMES]
    col_parts = [jnp.sum(sums[name] * sums[name], axis=0) for name in NAMES]
    totals = jnp.stack([jnp.sum(part) for part in row_parts])
    shared = jnp.concatenate((totals, gains_part.reshape(-1), table_part.reshape(-1)))
    row_sizes = [part.shape[0] for part in row_parts]
    col_sizes = [part.shape[0] for part in col_parts]
    first_sum = jnp.concatenate(row_parts + [shared])
    if fast:
        first_sum = hyper.total(first_sum, ("y",))
    else:
        first_sum = lax.psum(first_sum, "narrow")
    second_sum = jnp.concatenate(col_parts + [first_sum[sum(row_sizes) :]])
    if fast:
        second_sum = hyper.total(second_sum, ("c", "x", "z1", "z2"))
    else:
        second_sum = lax.psum(second_sum, "wide")

    results = []
    row_at = col_at = 0
    tail = sum(col_sizes)
    for index, name in enumerate(NAMES):
        grad = sums[name]
        full_rows = grad.shape[0] * wide_count
        full_cols = grad.shape[1] * narrow_count
        row_stat = first_sum[row_at : row_at + row_sizes[index]] / full_cols + TINY
        col_stat = second_sum[col_at : col_at + col_sizes[index]] / full_rows + TINY
        row_at += row_sizes[index]
        col_at += col_sizes[index]
        mean_rows = second_sum[tail + index] / (full_rows * full_cols) + TINY
        step = grad * lax.rsqrt(row_stat[:, None] * col_stat[None, :] / mean_rows)
        results.extend([grad, step, row_stat, col_stat])
    gains_grad = second_sum[tail + 7 : tail + 7 + gains_part.size].reshape(gains_part.shape)
    table_grad = second_sum[tail + 7 + gains_part.size :].reshape(table_part.shape)
    return (
        (
            layer_out,
            inputs_grad.reshape(inputs.shape),
            encoded_grad.reshape(encoded.shape),
        )
        + tuple(results)
        + (gains_grad, table_grad)
    )


def solution(mesh):
    tokens = P(BOTH, None, None)
    weight = P("wide", "narrow")
    per_weight = (weight, weight, P("wide"), P("narrow"))
    return jax.shard_map(
        local,
        mesh=mesh,
        in_specs=(tokens, tokens, P(BOTH), P(BOTH), P(), tokens) + (weight,) * 7 + (P(), P()),
        out_specs=(tokens, tokens, tokens) + per_weight * 7 + (P(), P()),
        check_vma=False,
    )
```

```python
import functools

import jax
import jax.numpy as jnp
from jax import lax
from jax.experimental import pallas as pl
from jax.experimental.pallas import tpu as pltpu
from jax.sharding import PartitionSpec as P

HEADS = 12
DH = 64
EPS = 1e-06
TINY = 1e-30
NEGATIVE = -1e30
SCALE = DH ** (-0.5)

BF = jnp.bfloat16
F32 = jnp.float32
BOTH = ("wide", "narrow")
VMEM_LIMIT = 63 * 1024 * 1024
KEY_TILE = 256

COUNTS = {
    "inward": 3,
    "outward": 1,
    "query": 1,
    "reader": 2,
    "writer": 1,
    "expand": 4,
    "shrink": 4,
}
NAMES = ("inward", "outward", "query", "reader", "writer", "expand", "shrink")
GATHERS = (
    ((("inward", 0), ("inward", 1)), (("inward", 2), ("outward", 0))),
    ((("query", 0), ("writer", 0)), (("reader", 0), ("reader", 1))),
    ((("expand", 0), ("expand", 1)), (("expand", 2), ("expand", 3))),
    ((("shrink", 0), ("shrink", 1)), (("shrink", 2), ("shrink", 3))),
)


def nn(left, right):
    return lax.dot_general(left, right, (((1,), (0,)), ((), ())), preferred_element_type=F32)


def nt(left, right):
    return lax.dot_general(left, right, (((1,), (1,)), ((), ())), preferred_element_type=F32)


def tn(left, right):
    return lax.dot_general(left, right, (((0,), (0,)), ((), ())), preferred_element_type=F32)


VM = pl.BlockSpec(memory_space=pltpu.VMEM)
SM = pl.BlockSpec(memory_space=pltpu.SMEM)
HB = pl.BlockSpec(memory_space=pl.ANY)


def launch(
    body, ins, outs, scratch=(), grid=None, alias=None, gflop=1.0, name=None, after=(), prefetch=()
):
    ahead, count, extra = len(prefetch), len(ins), len(after)

    def trimmed(*refs):
        body(*refs[: ahead + count], *refs[ahead + count + extra :])

    params = dict(
        out_shape=[o for o, _ in outs],
        input_output_aliases={ahead + k: v for k, v in (alias or {}).items()},
        compiler_params=pltpu.CompilerParams(vmem_limit_bytes=VMEM_LIMIT),
        cost_estimate=pl.CostEstimate(
            flops=int(gflop * 1e10), bytes_accessed=1 << 22, transcendentals=0
        ),
        name=name,
    )
    specs = dict(
        grid=grid if grid is not None else (),
        in_specs=[s for _, s in ins] + [HB] * extra,
        out_specs=[s for _, s in outs],
        scratch_shapes=list(scratch),
    )
    if ahead:
        specs = dict(grid_spec=pltpu.PrefetchScalarGridSpec(num_scalar_prefetch=ahead, **specs))
    return pl.pallas_call(trimmed, **params, **specs)(*prefetch, *[a for a, _ in ins], *after)


def shape(dims, dtype):
    return jax.ShapeDtypeStruct(tuple(dims), dtype)


def weight_scratch(name, width):
    if name == "shrink":
        return pltpu.VMEM((4, 2, 2, 4, width // 16, width), BF)
    return pltpu.VMEM((4, 2, 2, width // 16, width * COUNTS[name]), BF)


class Held:
    def __init__(self, groups, places):
        self.groups, self.places = groups, places
        self.arrays = [a for arrays, _ in groups for a in arrays]

    def ins(self):
        return [(a, HB) for a in self.arrays]


def load(name, held, refs, scratch, me, sem):
    if len(refs) == 1:
        pltpu.make_async_copy(refs[0], scratch, sem).start()
        return
    count = COUNTS[name]
    piece = refs[0].shape[-1]
    for p, (group, start) in enumerate(held.places):
        for a in range(2):
            for b in range(2):
                for k in range(2):
                    c = me[2] ^ b
                    if held.groups[group][1] == "x":
                        x, y = me[1] ^ k, me[3] ^ a
                    else:
                        x, y = me[1] ^ a, me[3] ^ k
                    src = refs[group * 4 + a * 2 + b].at[k, :, start]
                    if name == "shrink":
                        cols = pl.ds(pl.multiple_of(y * piece, 128), piece)
                        dst = scratch.at[:, x, c, p, :, cols]
                    else:
                        cols = pl.ds(pl.multiple_of((y * count + p) * piece, 128), piece)
                        dst = scratch.at[:, x, c, :, cols]
                    pltpu.make_async_copy(src, dst, sem).start()


def arrived(scratch, sem):
    pltpu.make_async_copy(scratch, scratch, sem).wait()


def store(name, scratch, outs, start, me, sem, split=None):
    if len(outs) == 1:
        pltpu.make_async_copy(scratch, outs[0], sem).start()
        return
    count = COUNTS[name]
    piece = outs[0].shape[-1]
    for b in range(2):
        c = me[2] ^ b
        for y in range(2):
            for p in range(count):
                if name == "shrink":
                    src = scratch.at[:, :, c, p, :, pl.ds(y * piece, piece)]
                else:
                    src = scratch.at[:, :, c, :, pl.ds((y * count + p) * piece, piece)]
                out, place = outs[b], start + p
                if split is not None and p >= split:
                    out, place = outs[2 + b], p - split
                pltpu.make_async_copy(src, out.at[:, :, y, place], sem).start()


def flat(block):
    return block.reshape(-1, block.shape[-1])


def put_rows(scratch, value, cols):
    scratch[:, :, :, :, cols] = value.reshape(scratch.shape[:4] + (value.shape[-1],))


def normed(values, gain):
    r = lax.rsqrt(jnp.mean(values * values, axis=-1, keepdims=True) + EPS)
    return values * r * gain


def norm_back(values, gain, grad):
    r = lax.rsqrt(jnp.mean(values * values, axis=-1, keepdims=True) + EPS)
    inner = jnp.mean(values * gain * grad, axis=-1, keepdims=True)
    back = r * gain * grad - values * (r * r * r * inner)
    return back, jnp.sum(grad * values * r, axis=0, keepdims=True)


def prepare_kernel(lens, x, cot, gains, buckets, table, n1, kept, bias):
    rows = cot.shape[1]
    for s in range(x.shape[0]):
        values = x[s].astype(F32)
        n1[s * rows : (s + 1) * rows, :] = normed(values, gains[0:1, :]).astype(BF)
        keep = lax.broadcasted_iota(jnp.int32, (rows, 1), 0) < lens[s]
        kept[s * rows : (s + 1) * rows, :] = jnp.where(keep, cot[s].astype(F32), 0.0).astype(BF)
    half = 128
    heads = 2 * bias.shape[0]

    @pl.loop(0, rows // 8)
    def _(step):
        start = pl.multiple_of(step * 8, 8)
        for side in range(rows // half):
            which = buckets[pl.ds(start, 8), side * half : (side + 1) * half]
            key = start + lax.broadcasted_iota(jnp.int32, (8, half), 0)
            query = side * half + lax.broadcasted_iota(jnp.int32, (8, half), 1)
            for h in range(heads):
                row = jnp.broadcast_to(table[h : h + 1, :], (8, half))
                found = jnp.take_along_axis(row, which, axis=1)
                at = (h % 2) * rows + side * half
                bias[h // 2, pl.ds(start, 8), at : at + half] = jnp.where(
                    key <= query, found, NEGATIVE
                )


CHUNK = 32


def stacked(block):
    lane = lax.broadcasted_iota(jnp.int32, block.shape, 1)
    zero = jnp.zeros_like(block)
    return jnp.concatenate((jnp.where(lane < DH, block, zero), jnp.where(lane < DH, zero, block)))


def unstacked(block):
    queries = block.shape[1] // 2
    return jnp.concatenate((block[:DH, :queries], block[DH:, queries:]), axis=0).T


def folded(block, by):
    return by(block.reshape(block.shape[0] // 8, 8, block.shape[1]), axis=0)


def chunks(size):
    return [slice(at, at + CHUNK) for at in range(0, size, CHUNK)]


def forward_units(units, size, fix):
    for query, keys, values, scores, probs, mixed, logsum, which in units:
        scores[:size] = nt(keys, stacked(query * jnp.asarray(SCALE, BF)))
    for query, keys, values, scores, probs, mixed, logsum, which in units:
        top = None
        for part in chunks(size):
            block, changed = fix(scores[part], part, which)
            if changed:
                scores[part] = block
            block = folded(block, jnp.max)
            top = block if top is None else jnp.maximum(top, block)
        highest = jnp.max(top, axis=0, keepdims=True)
        total = jnp.zeros((8, highest.shape[1]), F32)
        for part in chunks(size):
            weights = jnp.exp(scores[part] - highest)
            total = total + folded(weights, jnp.sum)
            probs[part] = weights.astype(BF)
        total = jnp.sum(total, axis=0, keepdims=True)
        logsum[...] = highest + jnp.log(total)
        mixed[...] = unstacked(tn(values, probs[:size]) * (1.0 / total)).astype(BF)


def backward_units(units, size, fix):
    for query, keys, values, grad, mixed, logsum, scores, slopes, probs, grads, outs, which in units:
        scores[:size] = nt(keys, stacked(query * jnp.asarray(SCALE, BF)))
        slopes[:size] = nt(values, stacked(grad))
    for query, keys, values, grad, mixed, logsum, scores, slopes, probs, grads, outs, which in units:
        product = stacked(grad.astype(F32) * mixed.astype(F32))
        high = product.astype(BF)
        low = (product - high.astype(F32)).astype(BF)
        ones = jnp.ones((8, product.shape[1]), BF)
        inner = (nt(ones, high) + nt(ones, low))[0:1]
        for part in chunks(size):
            block, keep = fix(scores[part], part, which)
            weights = jnp.exp(block - logsum[...])
            if keep is not None:
                weights = jnp.where(keep, weights, 0.0)
            probs[part] = weights.astype(BF)
            grads[part] = (weights * (slopes[part] - inner)).astype(BF)
        left = grads[:size]
        outs[0][...] = (unstacked(tn(keys, left)) * SCALE).astype(BF)
        outs[1][...] = nn(left, stacked(query * jnp.asarray(SCALE, BF))).astype(BF)
        outs[2][...] = nn(probs[:size], stacked(grad)).astype(BF)


def self_units(length):
    return [(slice(s * length, (s + 1) * length), slice(j * 128, (j + 1) * 128), s, j) for s in range(2) for j in range(2)]


def self_forward_kernel(query, keys, values, bias, mixed, logsum, scores, probs):
    length = bias.shape[1]
    units = []
    for rows, cols, s, j in self_units(length):
        u = s * 2 + j
        units.append(
            (
                query[rows, cols],
                keys[rows, cols],
                values[rows, cols],
                scores.at[u],
                probs.at[u],
                mixed.at[rows, cols],
                logsum.at[j, s],
                j,
            )
        )
    forward_units(units, length, lambda block, part, j: (block + bias[j, part, :], True))


def self_backward_kernel(
    query, keys, values, grad, mixed, bias, logsum, gq, gk, gv, grad_bias, scores, slopes, probs, grads
):
    length = bias.shape[1]
    units = []
    for rows, cols, s, j in self_units(length):
        u = s * 2 + j
        units.append(
            (
                query[rows, cols],
                keys[rows, cols],
                values[rows, cols],
                grad[rows, cols],
                mixed[rows, cols],
                logsum.at[j, s],
                scores.at[u],
                slopes.at[u],
                probs.at[u],
                grads.at[u],
                (gq.at[rows, cols], gk.at[rows, cols], gv.at[rows, cols]),
                j,
            )
        )
    backward_units(units, length, lambda block, part, j: (block + bias[j, part, :], None))
    for j in range(2):
        for part in chunks(length):
            grad_bias[j, part, :] = grads[j, part, :].astype(F32) + grads[2 + j, part, :].astype(F32)


def last_tile(valid, size, part, block):
    if part.start < size - KEY_TILE:
        return None
    return part.start + lax.broadcasted_iota(jnp.int32, block.shape, 0) < valid


def cross_forward_kernel(lens, query, keys, values, mixed, logsum, scores, probs):
    valid = lens[pl.program_id(0)]
    for tiles in range(1, keys.shape[0] // KEY_TILE + 1):

        @pl.when((valid + KEY_TILE - 1) // KEY_TILE == tiles)
        def _():
            size = tiles * KEY_TILE

            def fix(block, part, which):
                keep = last_tile(valid, size, part, block)
                if keep is None:
                    return block, False
                return jnp.where(keep, block, NEGATIVE), True

            units = []
            for j in range(2):
                cols = slice(j * 128, (j + 1) * 128)
                units.append(
                    (
                        query[:, cols],
                        keys[:size, cols],
                        values[:size, cols],
                        scores.at[j],
                        probs.at[j],
                        mixed.at[:, cols],
                        logsum.at[j, 0],
                        None,
                    )
                )
            forward_units(units, size, fix)


def cross_backward_kernel(
    lens, query, keys, values, grad, mixed, logsum, gq, gk, gv, scores, slopes, probs, grads
):
    valid = lens[pl.program_id(0)]
    for tiles in range(1, keys.shape[0] // KEY_TILE + 1):

        @pl.when((valid + KEY_TILE - 1) // KEY_TILE == tiles)
        def _():
            size = tiles * KEY_TILE
            units = []
            for j in range(2):
                cols = slice(j * 128, (j + 1) * 128)
                units.append(
                    (
                        query[:, cols],
                        keys[:size, cols],
                        values[:size, cols],
                        grad[:, cols],
                        mixed[:, cols],
                        logsum.at[j, 0],
                        scores.at[j],
                        slopes.at[j],
                        probs.at[j],
                        grads.at[j],
                        (gq.at[:, cols], gk.at[:size, cols], gv.at[:size, cols]),
                        None,
                    )
                )
            backward_units(
                units,
                size,
                lambda block, part, which: (block, last_tile(valid, size, part, block)),
            )


def attend_scratch(units, keys, queries, backward):
    wide = pltpu.VMEM((units, keys, 2 * queries), F32)
    thin = pltpu.VMEM((units, keys, 2 * queries), BF)
    return [wide, wide, thin, thin] if backward else [wide, thin]


def pair_spec(rows, base=0):
    return pl.BlockSpec((rows, 256), lambda s, p: (s, base + p))


def both_spec(rows, base=0):
    return pl.BlockSpec((rows, 256), lambda p: (0, base + p))


def inward_kernel(held, me, n1, *rest):
    refs, (packed, weight, sem) = rest[: len(held.arrays)], rest[len(held.arrays) :]
    load("inward", held, refs, weight, me, sem)
    arrived(weight, sem)
    size = n1.shape[1]
    left = n1[...]
    for block in range(3):
        cols = slice(block * size, (block + 1) * size)
        packed[:, cols] = nn(left, flat(weight[..., cols])).astype(BF)


def outward_kernel(held, me, x, mixed, gains, *rest):
    refs, (after, n2, weight, sem) = rest[: len(held.arrays)], rest[len(held.arrays) :]
    load("outward", held, refs, weight, me, sem)
    arrived(weight, sem)
    values = x[...].astype(F32) + nn(mixed[...], flat(weight[...]))
    after[...] = values
    n2[...] = normed(values, gains[1:2, :]).astype(BF)


def memory_kernel(held_query, held_reader, me, lens, n2, encoded, *rest):
    k, both = len(held_query.arrays), len(held_query.arrays) + len(held_reader.arrays)
    refs_query, refs_reader = rest[:k], rest[k:both]
    asks, pairs, weight_query, weight_reader, sems = rest[both:]
    step = pl.program_id(0)
    tiles = pl.num_programs(0) // lens.shape[0]

    @pl.when(step == 0)
    def _():
        load("query", held_query, refs_query, weight_query, me, sems.at[0])
        load("reader", held_reader, refs_reader, weight_reader, me, sems.at[1])
        arrived(weight_query, sems.at[0])
        asks[...] = nn(n2[...], flat(weight_query[...])).astype(BF)
        arrived(weight_reader, sems.at[1])

    @pl.when(lax.rem(step, tiles) * KEY_TILE < lens[step // tiles])
    def _():
        size = encoded.shape[1]
        left = encoded[...]
        for block in range(2):
            cols = slice(block * size, (block + 1) * size)
            pairs[:, cols] = nn(left, flat(weight_reader[..., cols])).astype(BF)


def gelu_parts(v):
    phi = 0.5 * (1.0 + lax.erf(v * (0.5**0.5)))
    density = jnp.exp(-0.5 * v * v) * 0.3989422804014327
    return v * phi, phi + v * density


def widen_kernel(held_writer, held_expand, me, after_self, mixed, gains, kept, *rest):
    k, both = len(held_writer.arrays), len(held_writer.arrays) + len(held_expand.arrays)
    refs_writer, refs_expand = rest[:k], rest[k:both]
    outs = rest[both:]
    after_cross, n3, hidden, slope = outs[:4]
    grads, (weight_writer, weight_expand, shrink_grad, sems) = outs[4:-4], outs[-4:]
    load("writer", held_writer, refs_writer, weight_writer, me, sems.at[0])
    load("expand", held_expand, refs_expand, weight_expand, me, sems.at[1])
    arrived(weight_writer, sems.at[0])
    values = after_self[...] + nn(mixed[...], flat(weight_writer[...]))
    after_cross[...] = values
    n3[...] = normed(values, gains[2:3, :]).astype(BF)
    arrived(weight_expand, sems.at[1])
    size = n3.shape[1]

    for z in range(4):
        cols = slice(z * size, (z + 1) * size)
        before = nn(n3[...], flat(weight_expand[:, :, :, :, cols]))
        active, gate = gelu_parts(before)
        active = active.astype(BF)
        hidden[:, cols] = active
        slope[:, cols] = gate.astype(BF)
        grad = tn(active, kept[...]).astype(BF)
        shrink_grad[z] = grad.reshape(shrink_grad.shape[1:])

    store("shrink", shrink_grad, grads, 0, me, sems.at[2])
    arrived(shrink_grad, sems.at[2])


def narrow_kernel(
    held_shrink, held_expand, me, lens, after_cross, n3, hidden, slope, kept, gains, *rest
):
    k, both = len(held_shrink.arrays), len(held_shrink.arrays) + len(held_expand.arrays)
    refs_shrink, refs_expand = rest[:k], rest[k:both]
    outs = rest[both:]
    layer_out, grad_cross, gain_part = outs[:3]
    grads, (weight_shrink, weight_expand, expand_grad, grad_norm, total, sems) = (
        outs[3:-6],
        outs[-6:],
    )
    load("shrink", held_shrink, refs_shrink, weight_shrink, me, sems.at[0])
    load("expand", held_expand, refs_expand, weight_expand, me, sems.at[1])
    size = n3.shape[1]
    total[...] = after_cross[...]
    grad_norm[...] = jnp.zeros_like(grad_norm)
    arrived(weight_shrink, sems.at[0])
    arrived(weight_expand, sems.at[1])

    for z in range(4):
        cols = slice(z * size, (z + 1) * size)
        shrink_rows = flat(weight_shrink[z])
        grad = (slope[:, cols].astype(F32) * nt(kept[...], shrink_rows)).astype(BF)
        put_rows(expand_grad, tn(n3[...], grad).astype(BF), cols)
        grad_norm[...] += nt(grad, flat(weight_expand[:, :, :, :, cols]))
        total[...] += nn(hidden[:, cols], shrink_rows)

    store("expand", expand_grad, grads, 0, me, sems.at[2])
    rows = total.shape[0] // lens.shape[0]
    for s in range(lens.shape[0]):
        part = slice(s * rows, (s + 1) * rows)
        keep = lax.broadcasted_iota(jnp.int32, (rows, 1), 0) < lens[s]
        layer_out[s] = jnp.where(keep, total[part, :], 0.0).astype(BF)
    back, gain = norm_back(after_cross[...], gains[2:3, :], grad_norm[...])
    grad_cross[...] = kept[...].astype(F32) + back
    gain_part[...] = gain
    arrived(expand_grad, sems.at[2])


def writer_back_kernel(held, me, grad_cross, mixed, *rest):
    k = len(held.arrays)
    refs, outs = rest[:k], rest[k:]
    grad_mixed, grads, (weight, grad_scratch, sems) = outs[0], outs[1:-3], outs[-3:]
    load("writer", held, refs, weight, me, sems.at[0])
    branch = grad_cross[...].astype(BF)
    put_rows(grad_scratch, tn(mixed[...], branch).astype(BF), slice(None))
    store("writer", grad_scratch, grads, 0, me, sems.at[1])
    arrived(weight, sems.at[0])
    grad_mixed[...] = nt(branch, flat(weight[...])).astype(BF)
    arrived(grad_scratch, sems.at[1])


def query_back_kernel(
    packed_mode,
    held_query,
    held_out,
    me,
    grad_asks,
    n2,
    after_self,
    grad_cross,
    mixed,
    gains,
    *rest,
):
    k, both = len(held_query.arrays), len(held_query.arrays) + len(held_out.arrays)
    refs_query, refs_out = rest[:k], rest[k:both]
    rest = rest[both:]
    if packed_mode:
        rest = rest[2:]
    grad_self, grad_mixed, gain_part = rest[:3]
    weight_query, weight_out, query_grad, out_grad, sems = rest[-5:]
    grads = rest[3:-5]
    load("query", held_query, refs_query, weight_query, me, sems.at[0])
    load("outward", held_out, refs_out, weight_out, me, sems.at[1])
    put_rows(query_grad, tn(n2[...], grad_asks[...]).astype(BF), slice(None))
    store("query", query_grad, grads if packed_mode else grads[:1], 1, me, sems.at[2])
    arrived(weight_query, sems.at[0])
    back, gain = norm_back(
        after_self[...], gains[1:2, :], nt(grad_asks[...], flat(weight_query[...]))
    )
    total = grad_cross[...] + back
    grad_self[...] = total
    gain_part[...] = gain
    branch = total.astype(BF)
    arrived(weight_out, sems.at[1])
    grad_mixed[...] = nt(branch, flat(weight_out[...])).astype(BF)
    put_rows(out_grad, tn(mixed[...], branch).astype(BF), slice(None))
    store("outward", out_grad, grads if packed_mode else grads[1:], 2, me, sems.at[3])
    arrived(query_grad, sems.at[2])
    arrived(out_grad, sems.at[3])


def inward_grad_kernel(me, n1, gq, gk, gv, *rest):
    grads, (scratch, sem) = rest[:-2], rest[-2:]
    size = n1.shape[1]
    for block, grad in enumerate((gq, gk, gv)):
        cols = slice(block * size, (block + 1) * size)
        put_rows(scratch, tn(n1[...], grad[...]).astype(BF), cols)
    store("inward", scratch, grads, 0, me, sem, 2)
    arrived(scratch, sem)


def inputs_grad_kernel(held, me, x, gq, gk, gv, grad_self, gains, *rest):
    k = len(held.arrays)
    refs, (out, gain_part, weight, sem) = rest[:k], rest[k:]
    load("inward", held, refs, weight, me, sem)
    arrived(weight, sem)
    size = x.shape[1]
    total = 0.0
    for block, grad in enumerate((gq, gk, gv)):
        cols = slice(block * size, (block + 1) * size)
        total = total + nt(grad[...], flat(weight[..., cols]))
    back, gain = norm_back(x[...].astype(F32), gains[0:1, :], total)
    out[...] = grad_self[...] + back
    gain_part[...] = gain


def reader_grad_kernel(me, lens, encoded, gk, gv, *rest):
    grads, (scratch, total, sem) = rest[:-3], rest[-3:]
    step = pl.program_id(0)
    steps = pl.num_programs(0)
    tiles = steps // lens.shape[0]
    size = encoded.shape[1]

    @pl.when(step == 0)
    def _():
        total[...] = jnp.zeros_like(total)

    @pl.when(lax.rem(step, tiles) * KEY_TILE < lens[step // tiles])
    def _():
        left = encoded[...]
        total[:, :size] += tn(left, gk[...])
        total[:, size:] += tn(left, gv[...])

    @pl.when(step == steps - 1)
    def _():
        put_rows(scratch, total[...].astype(BF), slice(None))
        store("reader", scratch, grads, 0, me, sem)
        arrived(scratch, sem)


def encoded_grad_kernel(held, me, lens, gk, gv, *rest):
    refs, (out, weight, sem) = rest[: len(held.arrays)], rest[len(held.arrays) :]
    step = pl.program_id(0)
    tiles = pl.num_programs(0) // lens.shape[0]
    valid = lax.rem(step, tiles) * KEY_TILE < lens[step // tiles]
    size = gk.shape[1]

    @pl.when(step == 0)
    def _():
        load("reader", held, refs, weight, me, sem)
        arrived(weight, sem)

    @pl.when(valid)
    def _():
        out[...] = nt(gk[...], flat(weight[..., :size])) + nt(gv[...], flat(weight[..., size:]))

    @pl.when(jnp.logical_not(valid))
    def _():
        out[...] = jnp.zeros_like(out)


def table_kernel(count, buckets, grad_bias, out):
    pairs, length = grad_bias.shape[:2]
    group = 4
    lane = lax.broadcasted_iota(jnp.int32, out.shape, 1)

    def one(step, total):
        rows = [[] for _ in range(group)]
        for h in range(2 * pairs):
            cols = slice((h % 2) * length, (h % 2 + 1) * length)
            sums = [jnp.zeros((8, length), F32) for _ in range(group)]
            for part in chunks(length):
                value, which = grad_bias[h // 2, part, cols], buckets[part, :]
                for k in range(group):
                    hit = jnp.where(which == step * group + k, value, 0.0)
                    sums[k] = sums[k] + folded(hit, jnp.sum)
            for k in range(group):
                rows[k].append(jnp.sum(sums[k], axis=0, keepdims=True))
        for k in range(group):
            value = jnp.sum(jnp.concatenate(rows[k], axis=0), axis=1, keepdims=True)
            total = total + jnp.where(lane == step * group + k, value, 0.0)
        return total

    out[...] = lax.fori_loop(0, count // group, one, jnp.zeros(out.shape, F32))


GAINS_AT = 8
TABLE_AT = 12


def statistics_kernel(*refs):
    grads, gains, table, rows, shared = refs[:7], refs[7:10], refs[10], refs[11], refs[12]
    rows[...] = jnp.zeros_like(rows)
    shared[...] = jnp.zeros_like(shared)
    lane = lax.broadcasted_iota(jnp.int32, (1, 128), 1)
    totals = jnp.zeros((1, 128), F32)
    for j, grad in enumerate(grads):
        square = grad[...] * grad[...]
        count, width = square.shape
        sums = jnp.sum(square, axis=1, keepdims=True)
        rows[:count, :] += jnp.where(lane == j, sums, 0.0)
        columns = jnp.sum(square, axis=0, keepdims=True)
        shared[j : j + 1, :width] = columns
        totals = totals + jnp.where(lane == j, jnp.sum(sums, axis=0, keepdims=True), 0.0)
    shared[7:8, :128] = totals
    for k in range(3):
        shared[GAINS_AT + k : GAINS_AT + k + 1, : gains[k].shape[1]] = gains[k][...]
    shared[TABLE_AT : TABLE_AT + table.shape[0], :128] = table[...]


def steps_kernel(wide, narrow, *refs):
    grads, rows, shared = refs[:7], refs[7], refs[8]
    outs = refs[9:]
    turned = rows[...].T
    for j, grad in enumerate(grads):
        step, row_out, col_out = outs[3 * j : 3 * j + 3]
        count, width = grad.shape
        full_rows, full_cols = count * wide, width * narrow
        row = rows[:count, j : j + 1] / full_cols + TINY
        col = shared[j : j + 1, :width] / full_rows + TINY
        mean = shared[7:8, j : j + 1] / (full_rows * full_cols) + TINY
        step[...] = grad[...] * lax.rsqrt(row * col / mean)
        row_out[...] = (turned[j : j + 1, :count] / full_cols + TINY).reshape(count)
        col_out[...] = col.reshape(width)


def tie(value, after):
    after = tuple(after)
    return lax.optimization_barrier((value,) + after)[0] if after else value


def join(gathers, arrays=()):
    keys = [(g, key) for g in gathers for key in g.live]
    flat_values, tree = jax.tree.flatten(([g.live[key] for g, key in keys], list(arrays)))
    values, arrays = jax.tree.unflatten(tree, lax.optimization_barrier(tuple(flat_values)))
    for (g, key), value in zip(keys, values):
        g.live[key] = value
    return arrays


class Hyper:
    MASKS = {"y": 1, "c": 2, "x": 4, "z1": 8, "z2": 16}

    def __init__(self):
        wide = lax.axis_index("wide")
        self.z, self.x, self.c = wide // 4, (wide // 2) % 2, wide % 2
        self.y = lax.axis_index("narrow")
        self.me = jnp.stack((self.z, self.x, self.c, self.y)).astype(jnp.int32)

    def swap(self, value, bit, after=()):
        mask = self.MASKS[bit]
        return lax.ppermute(tie(value, after), BOTH, [(i, i ^ mask) for i in range(32)])


class Gather:
    def __init__(self, hyper, shards, plan, width):
        self.hyper, self.plan = hyper, plan
        pieces = [cut(name, shards[name], width)[p] for half in plan for name, p in half]
        self.live = {"own": jnp.stack(pieces)}

    def z1(self):
        self.live["other"] = self.hyper.swap(self.live["own"], "z1")

    def z2(self):
        h = self.hyper
        own, other = self.live.pop("own"), self.live.pop("other")
        pair = jnp.where(h.z % 2 == 0, jnp.stack((own, other)), jnp.stack((other, own)))
        self.live["own"], self.live["other"] = pair, h.swap(pair, "z2")

    def p1(self):
        h = self.hyper
        own, other = self.live.pop("own"), self.live.pop("other")
        quad = jnp.where(
            h.z // 2 == 0, jnp.concatenate((own, other)), jnp.concatenate((other, own))
        )
        cutting = len(self.plan[0])
        halves = [quad[:, :cutting], quad[:, cutting:]]
        self.live["halves"] = halves
        self.live["others"] = [h.swap(half, bit) for half, bit in zip(halves, "xy")]

    def pair_up(self):
        two = zip(self.live.pop("halves"), self.live.pop("others"))
        self.live["near"] = [jnp.stack(pair) for pair in two]

    def p2(self):
        self.pair_up()
        near = self.live["near"]
        self.live["far"] = [self.hyper.swap(half, bit) for half, bit in zip(near, "yx")]

    def near_core(self):
        self.live["near_c"] = [self.hyper.swap(half, "c") for half in self.live["near"]]

    def far_core(self):
        self.live["far_c"] = [self.hyper.swap(half, "c") for half in self.live["far"]]

    def held(self, name):
        groups, places, seen = [], [], {}
        for p in range(COUNTS[name]):
            for half in range(2):
                if (name, p) in self.plan[half]:
                    if half not in seen:
                        seen[half] = len(groups)
                        arrays = [self.live[key][half] for key in ("near", "near_c", "far", "far_c")]
                        groups.append((arrays, "xy"[half]))
                    places.append((seen[half], self.plan[half].index((name, p))))
        return Held(groups, places)


def fold_kernel(counts, joint, names, me, *refs):
    na, nb, nj = counts
    first, second, both, outs = refs[:na], refs[na : na + nb], refs[na + nb : na + nb + nj], refs[na + nb + nj :]
    pa = first[0].shape[3]

    def add(parts, part):
        return sum([r[...].astype(F32) for r in parts] + [r[:, :, :, part].astype(F32) for r in both])

    one = add(first, slice(0, pa))
    two = add(second, slice(pa, None))
    if names:
        pieces = [one[0, 0, 0, p] for p in range(one.shape[3])]
        pieces += [two[0, 0, 0, p] for p in range(two.shape[3])]
        for out, (name, start) in zip(outs, names):
            for p in range(COUNTS[name]):
                piece = pieces[start + p]
                if name == "shrink":
                    out[p * piece.shape[0] : (p + 1) * piece.shape[0], :] = piece
                else:
                    out[:, p * piece.shape[1] : (p + 1) * piece.shape[1]] = piece
    elif joint:
        outs[0][:, :, :, :pa] = one.astype(outs[0].dtype)
        outs[0][:, :, :, pa:] = two.astype(outs[0].dtype)
    else:
        outs[0][...] = one.astype(outs[0].dtype)
        outs[1][...] = two.astype(outs[1].dtype)


class Scatter:
    def __init__(self, hyper, first, second, name):
        self.hyper, self.halves, self.name = hyper, (first, second), name
        self.parts = [[], []]
        self.joint = []
        self.sizes = [half[0].shape[3] for half in (first, second)]
        self.block = first[0].shape[4:]

    def core(self, half, after=()):
        keep, send = self.halves[half]
        recv = self.hyper.swap(send, "c", after)
        self.parts[half] = [keep, recv]
        return [recv]

    def fold(self, picks, out_dims, joint, after, step):
        ins = []
        for half in range(2):
            p = self.sizes[half]
            for array, (dims, index) in zip(self.parts[half], picks[half]):
                spec = pl.BlockSpec(
                    tuple(dims) + (p,) + self.block,
                    lambda i, me, index=index: tuple(index(me)) + (0, 0, 0),
                )
                ins.append((array, spec))
        whole = sum(self.sizes)
        for array, index in zip(self.joint, picks[2]):
            spec = pl.BlockSpec(
                (1, 1, 1, whole) + self.block,
                lambda i, me, index=index: (index(me), 0, 0, 0, 0, 0),
            )
            ins.append((array, spec))
        outs = []
        rows, cols = self.block
        for dims, kind in out_dims:
            if isinstance(dims, str):
                count = COUNTS[dims]
                full = (count * rows, cols) if dims == "shrink" else (rows, count * cols)
                outs.append((shape(full, F32), pl.BlockSpec(full, lambda i, me: (0, 0))))
                continue
            p = whole if joint else self.sizes[len(outs)]
            full = tuple(dims) + (p,) + self.block
            outs.append((shape(full, kind), pl.BlockSpec(full, lambda i, me: (0,) * 6)))
        counts = (len(self.parts[0]), len(self.parts[1]), len(self.joint))
        names = out_dims if step == "last" else None
        self.sent = launch(
            functools.partial(fold_kernel, counts, joint, names),
            ins,
            outs,
            grid=(1,),
            gflop=1.0,
            name=f"{self.name}_{step}",
            after=after,
            prefetch=(self.hyper.me,),
        )
        return self.sent

    def p1(self, after=()):
        a = [((4, 2, 1), lambda me: (0, 0, 1 - me[3]))] * 2
        b = [((4, 1, 2), lambda me: (0, 1 - me[1], 0))] * 2
        sent = self.fold((a, b, ()), (((4, 2, 1), BF), ((4, 1, 2), BF)), False, after, "p1")
        recv = [self.hyper.swap(value, bit) for value, bit in zip(sent, "yx")]
        for half in range(2):
            self.parts[half].append(recv[half])
        return recv

    def p2(self, after=()):
        four = (4, 1, 1)
        a = [(four, lambda me: (0, 1 - me[1], me[3]))] * 2
        a += [(four, lambda me: (0, 1 - me[1], 0))]
        b = [(four, lambda me: (0, me[1], 1 - me[3]))] * 2
        b += [(four, lambda me: (0, 0, 1 - me[3]))]
        sent = self.fold((a, b, ()), ((four, BF), (four, BF)), False, after, "p2")
        recv = [self.hyper.swap(value, bit) for value, bit in zip(sent, "xy")]
        for half in range(2):
            self.parts[half].append(recv[half])
        return recv

    def own(self, count, place):
        dims = (count, 1, 1)
        a = [(dims, lambda me: (place(me), me[1], me[3]))] * 2
        a += [(dims, lambda me: (place(me), me[1], 0)), (dims, lambda me: (place(me), 0, 0))]
        b = [(dims, lambda me: (place(me), me[1], me[3]))] * 2
        b += [(dims, lambda me: (place(me), 0, me[3])), (dims, lambda me: (place(me), 0, 0))]
        return a, b

    def z2(self, after=()):
        a, b = self.own(2, lambda me: 1 - me[0] // 2)
        (sent,) = self.fold((a, b, ()), (((2, 1, 1), BF),), True, after, "z2")
        recv = self.hyper.swap(sent, "z2")
        self.joint.append(recv)
        return [recv]

    def z1(self, after=()):
        a, b = self.own(1, lambda me: (me[0] // 2) * 2 + 1 - lax.rem(me[0], 2))
        j = [lambda me: 1 - lax.rem(me[0], 2)]
        (sent,) = self.fold((a, b, j), (((1, 1, 1), BF),), True, after, "z1")
        recv = self.hyper.swap(sent, "z1")
        self.joint.append(recv)
        return [recv]

    def last(self, weights, after=()):
        a, b = self.own(1, lambda me: me[0])
        j = [lambda me: lax.rem(me[0], 2), lambda me: 0]
        return self.fold((a, b, j), weights, True, after, "last")


def cut(name, shard, width):
    count = COUNTS[name]
    if name == "shrink":
        return shard.reshape(count, shard.shape[0] // count, shard.shape[1])
    rows, cols = shard.shape
    return jnp.transpose(shard.reshape(rows, count, cols // count), (1, 0, 2))


def whole_shape(name, width):
    if name == "shrink":
        return (4, 2, 2, 4, width // 16, width)
    return (4, 2, 2, width // 16, width * COUNTS[name])


def local(
    inputs,
    encoded,
    target_lengths,
    memory_lengths,
    buckets,
    cotangent,
    self_inward,
    self_outward,
    cross_query,
    cross_reader,
    cross_writer,
    expand_weight,
    shrink_weight,
    norm_gains,
    bias_table,
):
    wide_count = lax.axis_size("wide")
    narrow_count = lax.axis_size("narrow")
    fast = (wide_count, narrow_count) == (16, 2)
    seqs, length, width = inputs.shape
    memory_size = encoded.shape[1]
    rows, mem_rows = seqs * length, seqs * memory_size
    wide_hidden = expand_weight.shape[1] * narrow_count
    shards = dict(
        zip(
            NAMES,
            (
                self_inward,
                self_outward,
                cross_query,
                cross_reader,
                cross_writer,
                expand_weight,
                shrink_weight,
            ),
        )
    )
    hyper = Hyper() if fast else None
    me = hyper.me if fast else jnp.zeros((4,), jnp.int32)
    none = []

    def grad_outs(name, count):
        if fast:
            block = shape((4, 2, 2, count, width // 16, width // 2), BF)
            return [(block, HB), (block, HB)]
        return [(shape(whole_shape(name, width), BF), HB)]

    dma = pltpu.SemaphoreType.DMA
    x_rows = inputs.reshape(rows, width)
    mem_flat = encoded.reshape(mem_rows, width)
    heads = HEADS
    pairs_count = heads // 2
    turned = buckets.T
    table = jnp.pad(bias_table.T, ((0, 0), (0, 128 - bias_table.shape[0])))

    def weights(*names):
        return [entry for name in names for entry in held[name].ins()]

    held = {}
    if fast:
        ga, gb, gc, gd = [Gather(hyper, shards, plan, width) for plan in GATHERS]
        ga.z1()
        gb.z1()
        join((ga, gb))
        ga.z2()
        gc.z1()
        gd.z1()
    else:
        for name in NAMES:
            full = lax.all_gather(shards[name], "narrow", axis=1, tiled=True)
            full = lax.all_gather(full, "wide", axis=0, tiled=True)
            full = full.reshape(whole_shape(name, width))
            held[name] = Held([((full,), "x")], [(0, 0)] * COUNTS[name])

    n1, kept, bias = launch(
        prepare_kernel,
        [
            (target_lengths, SM),
            (inputs, VM),
            (cotangent, VM),
            (norm_gains, VM),
            (turned, VM),
            (table, VM),
        ],
        [
            (shape((rows, width), BF), VM),
            (shape((rows, width), BF), VM),
            (shape((pairs_count, length, 2 * length), F32), VM),
        ],
        name="prepare",
    )

    if fast:
        n1, kept, bias = join((ga, gc, gd), (n1, kept, bias))
        ga.p1()
        join((ga,))
        ga.p2()
        ga.near_core()
        gb.z2()
        join((ga, gb))
        ga.far_core()
        gb.p1()
        gc.z2()
        for name in ("inward", "outward"):
            held[name] = ga.held(name)

    (packed,) = launch(
        functools.partial(inward_kernel, held["inward"]),
        [(me, SM), (n1, VM)] + weights("inward"),
        [(shape((rows, 3 * width), BF), VM)],
        [weight_scratch("inward", width), dma],
        gflop=2.0,
        name="inward",
    )

    if fast:
        (packed,) = join((ga, gb, gc), (packed,))
        gb.p2()
        gb.near_core()
        gd.z2()

    bias_spec = pl.BlockSpec((2, length, 2 * length), lambda p: (p, 0, 0))
    log_both = pl.BlockSpec((2, seqs, 1, 2 * length), lambda p: (p, 0, 0, 0))
    log_spec = pl.BlockSpec((2, 1, 1, 2 * length), lambda s, p: (p, s, 0, 0))
    log_shape = shape((pairs_count, seqs, 1, 2 * length), F32)
    blocks = pairs_count // 2
    self_mixed, self_log = launch(
        self_forward_kernel,
        [
            (packed, both_spec(rows)),
            (packed, both_spec(rows, blocks)),
            (packed, both_spec(rows, 2 * blocks)),
            (bias, bias_spec),
        ],
        [(shape((rows, width), BF), both_spec(rows)), (log_shape, log_both)],
        attend_scratch(4, length, length, False),
        grid=(blocks,),
        gflop=5.0,
        name="self_forward",
    )

    after_self, n2 = launch(
        functools.partial(outward_kernel, held["outward"]),
        [(me, SM), (x_rows, VM), (self_mixed, VM), (norm_gains, VM)] + weights("outward"),
        [(shape((rows, width), F32), VM), (shape((rows, width), BF), VM)],
        [weight_scratch("outward", width), dma],
        gflop=2.0,
        name="outward",
    )

    if fast:
        after_self, n2 = join((gb, gd), (after_self, n2))
        gb.far_core()
        for name in ("query", "writer", "reader"):
            held[name] = gb.held(name)
        gc.p1()
        gd.p1()

    tile_spec = pl.BlockSpec((KEY_TILE, width), lambda i: (i, 0))
    asks, pairs = launch(
        functools.partial(memory_kernel, held["query"], held["reader"]),
        [(me, SM), (memory_lengths, SM), (n2, VM), (mem_flat, tile_spec)]
        + weights("query", "reader"),
        [
            (shape((rows, width), BF), pl.BlockSpec((rows, width), lambda i: (0, 0))),
            (
                shape((mem_rows, 2 * width), BF),
                pl.BlockSpec((KEY_TILE, 2 * width), lambda i: (i, 0)),
            ),
        ],
        [weight_scratch("query", width), weight_scratch("reader", width), dma((2,))],
        grid=(mem_rows // KEY_TILE,),
        gflop=6.0,
        name="memory",
    )

    if fast:
        asks, pairs = join((gb, gc, gd), (asks, pairs))
        gc.p2()
        gc.near_core()

    cross_mixed, cross_log = launch(
        cross_forward_kernel,
        [
            (memory_lengths, SM),
            (asks, pair_spec(length)),
            (pairs, pair_spec(memory_size)),
            (pairs, pair_spec(memory_size, blocks)),
        ],
        [(shape((rows, width), BF), pair_spec(length)), (log_shape, log_spec)],
        attend_scratch(2, memory_size, length, False),
        grid=(seqs, blocks),
        gflop=10.0,
        name="cross_forward",
    )

    if fast:
        cross_mixed, cross_log = join((gc,), (cross_mixed, cross_log))
        gc.far_core()
        held["expand"] = gc.held("expand")
        gd.p2()
        gd.near_core()

    after_cross, n3, hidden, slope, *shrink_parts = launch(
        functools.partial(widen_kernel, held["writer"], held["expand"]),
        [(me, SM), (after_self, VM), (cross_mixed, VM), (norm_gains, VM), (kept, VM)]
        + weights("writer", "expand"),
        [
            (shape((rows, width), F32), VM),
            (shape((rows, width), BF), VM),
            (shape((rows, wide_hidden), BF), VM),
            (shape((rows, wide_hidden), BF), VM),
        ]
        + grad_outs("shrink", 4),
        [
            weight_scratch("writer", width),
            weight_scratch("expand", width),
            weight_scratch("shrink", width),
            dma((3,)),
        ],
        gflop=10.0,
        name="widen",
    )

    if fast:
        after_cross, n3, hidden, slope, *shrink_parts = join(
            (gd,), [after_cross, n3, hidden, slope] + shrink_parts
        )
        gd.far_core()
        held["shrink"] = gd.held("shrink")

    layer_out, grad_cross, gain_third, *expand_parts = launch(
        functools.partial(narrow_kernel, held["shrink"], held["expand"]),
        [
            (me, SM),
            (target_lengths, SM),
            (after_cross, VM),
            (n3, VM),
            (hidden, VM),
            (slope, VM),
            (kept, VM),
            (norm_gains, VM),
        ]
        + weights("shrink", "expand"),
        [
            (shape((seqs, length, width), BF), VM),
            (shape((rows, width), F32), VM),
            (shape((1, width), F32), VM),
        ]
        + grad_outs("expand", 4),
        [
            weight_scratch("shrink", width),
            weight_scratch("expand", width),
            weight_scratch("expand", width),
            pltpu.VMEM((rows, width), F32),
            pltpu.VMEM((rows, width), F32),
            dma((3,)),
        ],
        gflop=14.0,
        name="narrow",
    )

    if fast:
        sf = Scatter(hyper, shrink_parts, expand_parts, "ffn")
        f0 = sf.core(0) + sf.core(1)

    grad_mixed, *rest_parts = launch(
        functools.partial(writer_back_kernel, held["writer"]),
        [(me, SM), (grad_cross, VM), (cross_mixed, VM)] + weights("writer"),
        [(shape((rows, width), BF), VM)] + grad_outs("writer", 3),
        [weight_scratch("writer", width), weight_scratch("writer", width), dma((2,))],
        gflop=2.0,
        name="writer_back",
    )
    writer_parts = rest_parts

    if fast:
        f1 = sf.p1([grad_mixed])

    grad_asks, grad_mem_keys, grad_mem_values = launch(
        cross_backward_kernel,
        [
            (memory_lengths, SM),
            (asks, pair_spec(length)),
            (pairs, pair_spec(memory_size)),
            (pairs, pair_spec(memory_size, blocks)),
            (grad_mixed, pair_spec(length)),
            (cross_mixed, pair_spec(length)),
            (cross_log, log_spec),
        ],
        [
            (shape((rows, width), BF), pair_spec(length)),
            (shape((mem_rows, width), BF), pair_spec(memory_size)),
            (shape((mem_rows, width), BF), pair_spec(memory_size)),
        ],
        attend_scratch(2, memory_size, length, True),
        grid=(seqs, blocks),
        gflop=20.0,
        name="cross_backward",
        after=sf.sent if fast else none,
    )

    reader_parts = launch(
        reader_grad_kernel,
        [
            (me, SM),
            (memory_lengths, SM),
            (mem_flat, tile_spec),
            (grad_mem_keys, tile_spec),
            (grad_mem_values, tile_spec),
        ],
        grad_outs("reader", 2),
        [weight_scratch("reader", width), pltpu.VMEM((width, 2 * width), F32), dma],
        grid=(mem_rows // KEY_TILE,),
        gflop=5.0,
        name="reader_grad",
    )

    if fast:
        f2 = sf.p2([reader_parts[0]])

    into = [(a, HB) for a in rest_parts] if fast else []
    base = 7 + len(weights("query", "outward"))
    grad_self, grad_mixed, gain_second, *rest_parts = launch(
        functools.partial(query_back_kernel, fast, held["query"], held["outward"]),
        [
            (me, SM),
            (grad_asks, VM),
            (n2, VM),
            (after_self, VM),
            (grad_cross, VM),
            (self_mixed, VM),
            (norm_gains, VM),
        ]
        + weights("query", "outward")
        + into,
        [
            (shape((rows, width), F32), VM),
            (shape((rows, width), BF), VM),
            (shape((1, width), F32), VM),
        ]
        + (grad_outs("query", 3) if fast else grad_outs("query", 1) + grad_outs("outward", 1)),
        [
            weight_scratch("query", width),
            weight_scratch("outward", width),
            weight_scratch("query", width),
            weight_scratch("outward", width),
            dma((4,)),
        ],
        alias={base: 3, base + 1: 4} if fast else None,
        gflop=4.0,
        name="query_back",
        after=sf.sent if fast else none,
    )

    if fast:
        sm = Scatter(hyper, rest_parts, reader_parts, "mid")
        sm.core(0)
        sm.core(1)

    grad_query, grad_keys, grad_values, grad_bias = launch(
        self_backward_kernel,
        [
            (packed, both_spec(rows)),
            (packed, both_spec(rows, blocks)),
            (packed, both_spec(rows, 2 * blocks)),
            (grad_mixed, both_spec(rows)),
            (self_mixed, both_spec(rows)),
            (bias, bias_spec),
            (self_log, log_both),
        ],
        [(shape((rows, width), BF), both_spec(rows))] * 3
        + [(shape((pairs_count, length, 2 * length), F32), bias_spec)],
        attend_scratch(4, length, length, True),
        grid=(blocks,),
        gflop=6.0,
        name="self_backward",
    )

    if fast:
        f3 = sf.z2([grad_query])
        m1 = sm.p1(sf.sent)

    inward_outs = grad_outs("inward", 2) + grad_outs("inward", 1) if fast else grad_outs("inward", 3)
    inward_parts = launch(
        inward_grad_kernel,
        [(me, SM), (n1, VM), (grad_query, VM), (grad_keys, VM), (grad_values, VM)],
        inward_outs,
        [weight_scratch("inward", width), dma],
        gflop=2.0,
        name="inward_grad",
        after=sm.sent if fast else none,
    )

    if fast:
        si = Scatter(hyper, inward_parts[:2], inward_parts[2:], "inward")
        i0 = si.core(0) + si.core(1)

    inputs_grad, gain_first = launch(
        functools.partial(inputs_grad_kernel, held["inward"]),
        [
            (me, SM),
            (x_rows, VM),
            (grad_query, VM),
            (grad_keys, VM),
            (grad_values, VM),
            (grad_self, VM),
            (norm_gains, VM),
        ]
        + weights("inward"),
        [(shape((rows, width), F32), VM), (shape((1, width), F32), VM)],
        [weight_scratch("inward", width), dma],
        gflop=2.0,
        name="inputs_grad",
        after=[inward_parts[0]] if fast else none,
    )

    if fast:
        i1 = si.p1([inputs_grad])

    (encoded_grad,) = launch(
        functools.partial(encoded_grad_kernel, held["reader"]),
        [(me, SM), (memory_lengths, SM), (grad_mem_keys, tile_spec), (grad_mem_values, tile_spec)]
        + weights("reader"),
        [(shape((mem_rows, width), F32), tile_spec)],
        [weight_scratch("reader", width), dma],
        grid=(mem_rows // KEY_TILE,),
        gflop=5.0,
        name="encoded_grad",
        after=si.sent if fast else none,
    )

    if fast:
        m2 = sm.p2([encoded_grad])
        i2 = si.p2(sm.sent)
        f4 = sf.z1(si.sent)

    (table_part,) = launch(
        functools.partial(table_kernel, bias_table.shape[0]),
        [(turned, VM), (grad_bias, VM)],
        [(shape((heads, 128), F32), VM)],
        gflop=6.0,
        name="table",
        after=sf.sent if fast else none,
    )

    sums = {}
    if fast:
        m3 = sm.z2([table_part])
        i3 = si.z2(sm.sent)
        sums["shrink"], sums["expand"] = sf.last((("shrink", 0), ("expand", 4)), si.sent)
        m4 = sm.z1()
        i4 = si.z1(sm.sent)
        mids = ("writer", "query", "outward", "reader")
        for name, total in zip(mids, sm.last([(name, at) for at, name in enumerate(mids)])):
            sums[name] = total
        (sums["inward"],) = si.last((("inward", 0),))
    else:
        parts = {
            "shrink": shrink_parts[0],
            "expand": expand_parts[0],
            "writer": writer_parts[0],
            "reader": reader_parts[0],
            "query": rest_parts[0],
            "outward": rest_parts[1],
            "inward": inward_parts[0],
        }
        for name in NAMES:
            full = parts[name].reshape(-1, parts[name].shape[-1]).astype(F32)
            full = lax.psum_scatter(full, "wide", scatter_dimension=0, tiled=True)
            sums[name] = lax.psum_scatter(full, "narrow", scatter_dimension=1, tiled=True)

    grads = [sums[name] for name in NAMES]
    tallest = max(g.shape[0] for g in grads)
    widest = max([g.shape[1] for g in grads] + [width])
    row_sums, shared = launch(
        statistics_kernel,
        [(g, VM) for g in grads]
        + [(gain_first, VM), (gain_second, VM), (gain_third, VM), (table_part, VM)],
        [(shape((tallest, 128), F32), VM), (shape((TABLE_AT + heads, widest), F32), VM)],
        name="statistics",
    )
    add_y = lax.broadcasted_iota(jnp.int32, shared.shape, 0) >= 7
    if fast:
        other = hyper.swap(row_sums, "y")
        shared = shared + jnp.where(add_y, hyper.swap(shared, "y"), 0.0)
        row_sums = row_sums + other
        shared = tie(shared, [other])
        for bit in ("c", "x", "z1", "z2"):
            shared = shared + hyper.swap(shared, bit)
    else:
        row_sums = lax.psum(row_sums, "narrow")
        shared = lax.psum(jnp.where(add_y, lax.psum(shared, "narrow"), shared), "wide")

    step_outs = []
    for g in grads:
        step_outs.append((shape(g.shape, F32), VM))
        step_outs.append((shape((g.shape[0],), F32), VM))
        step_outs.append((shape((g.shape[1],), F32), VM))
    made = launch(
        functools.partial(steps_kernel, wide_count, narrow_count),
        [(g, VM) for g in grads] + [(row_sums, VM), (shared, VM)],
        step_outs,
        name="steps",
    )
    results = []
    for j, grad in enumerate(grads):
        step, row_stat, col_stat = made[3 * j : 3 * j + 3]
        results.extend([grad, step, row_stat, col_stat])
    gains_grad = shared[GAINS_AT : GAINS_AT + 3, :width]
    table_grad = shared[TABLE_AT : TABLE_AT + heads, : bias_table.shape[0]].T
    return (
        (
            layer_out,
            inputs_grad.reshape(inputs.shape),
            encoded_grad.reshape(encoded.shape),
        )
        + tuple(results)
        + (gains_grad, table_grad)
    )


def solution(mesh):
    tokens = P(BOTH, None, None)
    weight = P("wide", "narrow")
    per_weight = (weight, weight, P("wide"), P("narrow"))
    return jax.shard_map(
        local,
        mesh=mesh,
        in_specs=(tokens, tokens, P(BOTH), P(BOTH), P(), tokens) + (weight,) * 7 + (P(), P()),
        out_specs=(tokens, tokens, tokens) + per_weight * 7 + (P(), P()),
        check_vma=False,
    )
```

```python
import functools

import jax
import jax.numpy as jnp
from jax import lax
from jax.experimental import pallas as pl
from jax.experimental.pallas import tpu as pltpu
from jax.sharding import PartitionSpec as P

HEADS = 12
DH = 64
EPS = 1e-06
TINY = 1e-30
NEGATIVE = -1e30
SCALE = DH ** (-0.5)

BF = jnp.bfloat16
F32 = jnp.float32
BOTH = ("wide", "narrow")
VMEM_LIMIT = 63 * 1024 * 1024
KEY_TILE = 256

COUNTS = {
    "inward": 3,
    "outward": 1,
    "query": 1,
    "reader": 2,
    "writer": 1,
    "expand": 4,
    "shrink": 4,
}
NAMES = ("inward", "outward", "query", "reader", "writer", "expand", "shrink")
GATHERS = (
    (("inward", 0), ("inward", 1), ("inward", 2), ("outward", 0)),
    (("query", 0), ("writer", 0), ("reader", 0), ("reader", 1)),
    (("expand", 0), ("expand", 1), ("expand", 2), ("expand", 3)),
    (("shrink", 0), ("shrink", 1), ("shrink", 2), ("shrink", 3)),
)


def nn(left, right):
    return lax.dot_general(left, right, (((1,), (0,)), ((), ())), preferred_element_type=F32)


def nt(left, right):
    return lax.dot_general(left, right, (((1,), (1,)), ((), ())), preferred_element_type=F32)


def tn(left, right):
    return lax.dot_general(left, right, (((0,), (0,)), ((), ())), preferred_element_type=F32)


VM = pl.BlockSpec(memory_space=pltpu.VMEM)
SM = pl.BlockSpec(memory_space=pltpu.SMEM)
HB = pl.BlockSpec(memory_space=pl.ANY)


def launch(
    body, ins, outs, scratch=(), grid=None, alias=None, gflop=1.0, name=None, after=(), prefetch=()
):
    ahead, count, extra = len(prefetch), len(ins), len(after)

    def trimmed(*refs):
        body(*refs[: ahead + count], *refs[ahead + count + extra :])

    params = dict(
        out_shape=[o for o, _ in outs],
        input_output_aliases={ahead + k: v for k, v in (alias or {}).items()},
        compiler_params=pltpu.CompilerParams(vmem_limit_bytes=VMEM_LIMIT),
        cost_estimate=pl.CostEstimate(
            flops=int(gflop * 1e10), bytes_accessed=1 << 22, transcendentals=0
        ),
        name=name,
    )
    specs = dict(
        grid=grid if grid is not None else (),
        in_specs=[s for _, s in ins] + [HB] * extra,
        out_specs=[s for _, s in outs],
        scratch_shapes=list(scratch),
    )
    if ahead:
        specs = dict(grid_spec=pltpu.PrefetchScalarGridSpec(num_scalar_prefetch=ahead, **specs))
    return pl.pallas_call(trimmed, **params, **specs)(*prefetch, *[a for a, _ in ins], *after)


def shape(dims, dtype):
    return jax.ShapeDtypeStruct(tuple(dims), dtype)


def weight_scratch(name, width):
    if name == "shrink":
        return pltpu.VMEM((4, 2, 2, 4, width // 16, width), BF)
    return pltpu.VMEM((4, 2, 2, width // 16, width * COUNTS[name]), BF)


class Held:
    def __init__(self, arrays, start=0):
        self.arrays, self.start = list(arrays), start

    def ins(self):
        return [(a, HB) for a in self.arrays]


def load(name, held, refs, scratch, me, sem):
    if len(refs) == 1 and refs[0].shape == scratch.shape:
        pltpu.make_async_copy(refs[0], scratch, sem).start()
        return
    count = COUNTS[name]
    piece = refs[0].shape[-1]

    def columns(y, p):
        if name == "shrink":
            return pl.ds(pl.multiple_of(y * piece, 128), piece)
        return pl.ds(pl.multiple_of((y * count + p) * piece, 128), piece)

    for p in range(count):
        if len(refs) == 1:
            for y in range(2):
                src = refs[0].at[:, :, :, y, held.start + p]
                cols = columns(y, p)
                dst = scratch.at[:, :, :, p, :, cols] if name == "shrink" else scratch.at[:, :, :, :, cols]
                pltpu.make_async_copy(src, dst, sem).start()
            continue
        for k in range(4):
            for b in range(2):
                x, y, c = me[1] ^ (k & 1), me[3] ^ (k >> 1), me[2] ^ b
                src = refs[k * 2 + b].at[:, held.start + p]
                cols = columns(y, p)
                dst = scratch.at[:, x, c, p, :, cols] if name == "shrink" else scratch.at[:, x, c, :, cols]
                pltpu.make_async_copy(src, dst, sem).start()


def arrived(scratch, sem):
    pltpu.make_async_copy(scratch, scratch, sem).wait()


def store(name, scratch, outs, start, me, sem):
    if len(outs) == 1 and outs[0].shape == scratch.shape:
        pltpu.make_async_copy(scratch, outs[0], sem).start()
        return
    count = COUNTS[name]
    piece = outs[0].shape[-1]
    if len(outs) == 1:
        for y in range(2):
            for p in range(count):
                src = scratch.at[:, :, :, p, :, pl.ds(y * piece, piece)]
                pltpu.make_async_copy(src, outs[0].at[:, :, :, y, p], sem).start()
        return
    for b in range(2):
        c = me[2] ^ b
        for y in range(2):
            for p in range(count):
                if name == "shrink":
                    src = scratch.at[:, :, c, p, :, pl.ds(y * piece, piece)]
                else:
                    src = scratch.at[:, :, c, :, pl.ds((y * count + p) * piece, piece)]
                pltpu.make_async_copy(src, outs[b].at[:, :, y, start + p], sem).start()


def flat(block):
    return block.reshape(-1, block.shape[-1])


def put_rows(scratch, value, cols):
    scratch[:, :, :, :, cols] = value.reshape(scratch.shape[:4] + (value.shape[-1],))


def normed(values, gain):
    r = lax.rsqrt(jnp.mean(values * values, axis=-1, keepdims=True) + EPS)
    return values * r * gain


def norm_back(values, gain, grad):
    r = lax.rsqrt(jnp.mean(values * values, axis=-1, keepdims=True) + EPS)
    inner = jnp.mean(values * gain * grad, axis=-1, keepdims=True)
    back = r * gain * grad - values * (r * r * r * inner)
    return back, jnp.sum(grad * values * r, axis=0, keepdims=True)


def prepare_kernel(lens, x, cot, gains, buckets, table, n1, kept, bias):
    rows = cot.shape[1]
    for s in range(x.shape[0]):
        values = x[s].astype(F32)
        n1[s * rows : (s + 1) * rows, :] = normed(values, gains[0:1, :]).astype(BF)
        keep = lax.broadcasted_iota(jnp.int32, (rows, 1), 0) < lens[s]
        kept[s * rows : (s + 1) * rows, :] = jnp.where(keep, cot[s].astype(F32), 0.0).astype(BF)
    half = 128
    heads = 2 * bias.shape[0]

    @pl.loop(0, rows // 8)
    def _(step):
        start = pl.multiple_of(step * 8, 8)
        for side in range(rows // half):
            which = buckets[pl.ds(start, 8), side * half : (side + 1) * half]
            key = start + lax.broadcasted_iota(jnp.int32, (8, half), 0)
            query = side * half + lax.broadcasted_iota(jnp.int32, (8, half), 1)
            for h in range(heads):
                row = jnp.broadcast_to(table[h : h + 1, :], (8, half))
                found = jnp.take_along_axis(row, which, axis=1)
                at = (h % 2) * rows + side * half
                bias[h // 2, pl.ds(start, 8), at : at + half] = jnp.where(
                    key <= query, found, NEGATIVE
                )


CHUNK = 32


def stacked(block):
    lane = lax.broadcasted_iota(jnp.int32, block.shape, 1)
    zero = jnp.zeros_like(block)
    return jnp.concatenate((jnp.where(lane < DH, block, zero), jnp.where(lane < DH, zero, block)))


def unstacked(block):
    queries = block.shape[1] // 2
    return jnp.concatenate((block[:DH, :queries], block[DH:, queries:]), axis=0).T


def folded(block, by):
    return by(block.reshape(block.shape[0] // 8, 8, block.shape[1]), axis=0)


def chunks(size):
    return [slice(at, at + CHUNK) for at in range(0, size, CHUNK)]


def forward_units(units, size, fix):
    for query, keys, values, scores, probs, mixed, logsum, which in units:
        scores[:size] = nt(keys, stacked(query * jnp.asarray(SCALE, BF)))
    for query, keys, values, scores, probs, mixed, logsum, which in units:
        top = None
        for part in chunks(size):
            block, changed = fix(scores[part], part, which)
            if changed:
                scores[part] = block
            block = folded(block, jnp.max)
            top = block if top is None else jnp.maximum(top, block)
        highest = jnp.max(top, axis=0, keepdims=True)
        total = jnp.zeros((8, highest.shape[1]), F32)
        for part in chunks(size):
            weights = jnp.exp(scores[part] - highest)
            total = total + folded(weights, jnp.sum)
            probs[part] = weights.astype(BF)
        total = jnp.sum(total, axis=0, keepdims=True)
        logsum[...] = highest + jnp.log(total)
        mixed[...] = unstacked(tn(values, probs[:size]) * (1.0 / total)).astype(BF)


def backward_units(units, size, fix):
    for query, keys, values, grad, mixed, logsum, scores, slopes, probs, grads, outs, which in units:
        scores[:size] = nt(keys, stacked(query * jnp.asarray(SCALE, BF)))
        slopes[:size] = nt(values, stacked(grad))
    for query, keys, values, grad, mixed, logsum, scores, slopes, probs, grads, outs, which in units:
        product = stacked(grad.astype(F32) * mixed.astype(F32))
        high = product.astype(BF)
        low = (product - high.astype(F32)).astype(BF)
        ones = jnp.ones((8, product.shape[1]), BF)
        inner = (nt(ones, high) + nt(ones, low))[0:1]
        for part in chunks(size):
            block, keep = fix(scores[part], part, which)
            weights = jnp.exp(block - logsum[...])
            if keep is not None:
                weights = jnp.where(keep, weights, 0.0)
            probs[part] = weights.astype(BF)
            grads[part] = (weights * (slopes[part] - inner)).astype(BF)
        left = grads[:size]
        outs[0][...] = (unstacked(tn(keys, left)) * SCALE).astype(BF)
        outs[1][...] = nn(left, stacked(query * jnp.asarray(SCALE, BF))).astype(BF)
        outs[2][...] = nn(probs[:size], stacked(grad)).astype(BF)


def self_units(length):
    return [(slice(s * length, (s + 1) * length), slice(j * 128, (j + 1) * 128), s, j) for s in range(2) for j in range(2)]


def self_forward_kernel(query, keys, values, bias, mixed, logsum, scores, probs):
    length = bias.shape[1]
    units = []
    for rows, cols, s, j in self_units(length):
        u = s * 2 + j
        units.append(
            (
                query[rows, cols],
                keys[rows, cols],
                values[rows, cols],
                scores.at[u],
                probs.at[u],
                mixed.at[rows, cols],
                logsum.at[j, s],
                j,
            )
        )
    forward_units(units, length, lambda block, part, j: (block + bias[j, part, :], True))


def self_backward_kernel(
    query, keys, values, grad, mixed, bias, logsum, gq, gk, gv, grad_bias, scores, slopes, probs, grads
):
    length = bias.shape[1]
    units = []
    for rows, cols, s, j in self_units(length):
        u = s * 2 + j
        units.append(
            (
                query[rows, cols],
                keys[rows, cols],
                values[rows, cols],
                grad[rows, cols],
                mixed[rows, cols],
                logsum.at[j, s],
                scores.at[u],
                slopes.at[u],
                probs.at[u],
                grads.at[u],
                (gq.at[rows, cols], gk.at[rows, cols], gv.at[rows, cols]),
                j,
            )
        )
    backward_units(units, length, lambda block, part, j: (block + bias[j, part, :], None))
    for j in range(2):
        for part in chunks(length):
            grad_bias[j, part, :] = grads[j, part, :].astype(F32) + grads[2 + j, part, :].astype(F32)


def last_tile(valid, size, part, block):
    if part.start < size - KEY_TILE:
        return None
    return part.start + lax.broadcasted_iota(jnp.int32, block.shape, 0) < valid


def cross_forward_kernel(lens, query, keys, values, mixed, logsum, scores, probs):
    valid = lens[pl.program_id(0)]
    for tiles in range(1, keys.shape[0] // KEY_TILE + 1):

        @pl.when((valid + KEY_TILE - 1) // KEY_TILE == tiles)
        def _():
            size = tiles * KEY_TILE

            def fix(block, part, which):
                keep = last_tile(valid, size, part, block)
                if keep is None:
                    return block, False
                return jnp.where(keep, block, NEGATIVE), True

            units = []
            for j in range(2):
                cols = slice(j * 128, (j + 1) * 128)
                units.append(
                    (
                        query[:, cols],
                        keys[:size, cols],
                        values[:size, cols],
                        scores.at[j],
                        probs.at[j],
                        mixed.at[:, cols],
                        logsum.at[j, 0],
                        None,
                    )
                )
            forward_units(units, size, fix)


def cross_backward_kernel(
    lens, query, keys, values, grad, mixed, logsum, gq, gk, gv, scores, slopes, probs, grads
):
    valid = lens[pl.program_id(0)]
    for tiles in range(1, keys.shape[0] // KEY_TILE + 1):

        @pl.when((valid + KEY_TILE - 1) // KEY_TILE == tiles)
        def _():
            size = tiles * KEY_TILE
            units = []
            for j in range(2):
                cols = slice(j * 128, (j + 1) * 128)
                units.append(
                    (
                        query[:, cols],
                        keys[:size, cols],
                        values[:size, cols],
                        grad[:, cols],
                        mixed[:, cols],
                        logsum.at[j, 0],
                        scores.at[j],
                        slopes.at[j],
                        probs.at[j],
                        grads.at[j],
                        (gq.at[:, cols], gk.at[:size, cols], gv.at[:size, cols]),
                        None,
                    )
                )
            backward_units(
                units,
                size,
                lambda block, part, which: (block, last_tile(valid, size, part, block)),
            )


def attend_scratch(units, keys, queries, backward):
    wide = pltpu.VMEM((units, keys, 2 * queries), F32)
    thin = pltpu.VMEM((units, keys, 2 * queries), BF)
    return [wide, wide, thin, thin] if backward else [wide, thin]


def pair_spec(rows, base=0):
    return pl.BlockSpec((rows, 256), lambda s, p: (s, base + p))


def both_spec(rows, base=0):
    return pl.BlockSpec((rows, 256), lambda p: (0, base + p))


def inward_kernel(held, me, n1, *rest):
    refs, (packed, weight, sem) = rest[: len(held.arrays)], rest[len(held.arrays) :]
    load("inward", held, refs, weight, me, sem)
    arrived(weight, sem)
    size = n1.shape[1]
    left = n1[...]
    for block in range(3):
        cols = slice(block * size, (block + 1) * size)
        packed[:, cols] = nn(left, flat(weight[..., cols])).astype(BF)


def outward_kernel(held, me, x, mixed, gains, *rest):
    refs, (after, n2, weight, sem) = rest[: len(held.arrays)], rest[len(held.arrays) :]
    load("outward", held, refs, weight, me, sem)
    arrived(weight, sem)
    values = x[...].astype(F32) + nn(mixed[...], flat(weight[...]))
    after[...] = values
    n2[...] = normed(values, gains[1:2, :]).astype(BF)


def memory_kernel(held_query, held_reader, me, lens, n2, encoded, *rest):
    k, both = len(held_query.arrays), len(held_query.arrays) + len(held_reader.arrays)
    refs_query, refs_reader = rest[:k], rest[k:both]
    asks, pairs, weight_query, weight_reader, sems = rest[both:]
    step = pl.program_id(0)
    tiles = pl.num_programs(0) // lens.shape[0]

    @pl.when(step == 0)
    def _():
        load("query", held_query, refs_query, weight_query, me, sems.at[0])
        load("reader", held_reader, refs_reader, weight_reader, me, sems.at[1])
        arrived(weight_query, sems.at[0])
        asks[...] = nn(n2[...], flat(weight_query[...])).astype(BF)
        arrived(weight_reader, sems.at[1])

    @pl.when(lax.rem(step, tiles) * KEY_TILE < lens[step // tiles])
    def _():
        size = encoded.shape[1]
        left = encoded[...]
        for block in range(2):
            cols = slice(block * size, (block + 1) * size)
            pairs[:, cols] = nn(left, flat(weight_reader[..., cols])).astype(BF)


def gelu_parts(v):
    phi = 0.5 * (1.0 + lax.erf(v * (0.5**0.5)))
    density = jnp.exp(-0.5 * v * v) * 0.3989422804014327
    return v * phi, phi + v * density


def widen_kernel(held_writer, held_expand, me, after_self, mixed, gains, kept, *rest):
    k, both = len(held_writer.arrays), len(held_writer.arrays) + len(held_expand.arrays)
    refs_writer, refs_expand = rest[:k], rest[k:both]
    outs = rest[both:]
    after_cross, n3, hidden, slope = outs[:4]
    grads, (weight_writer, weight_expand, shrink_grad, sems) = outs[4:-4], outs[-4:]
    load("writer", held_writer, refs_writer, weight_writer, me, sems.at[0])
    load("expand", held_expand, refs_expand, weight_expand, me, sems.at[1])
    arrived(weight_writer, sems.at[0])
    values = after_self[...] + nn(mixed[...], flat(weight_writer[...]))
    after_cross[...] = values
    n3[...] = normed(values, gains[2:3, :]).astype(BF)
    arrived(weight_expand, sems.at[1])
    size = n3.shape[1]

    for z in range(4):
        cols = slice(z * size, (z + 1) * size)
        before = nn(n3[...], flat(weight_expand[:, :, :, :, cols]))
        active, gate = gelu_parts(before)
        active = active.astype(BF)
        hidden[:, cols] = active
        slope[:, cols] = gate.astype(BF)
        grad = tn(active, kept[...]).astype(BF)
        shrink_grad[z] = grad.reshape(shrink_grad.shape[1:])

    store("shrink", shrink_grad, grads, 0, me, sems.at[2])
    arrived(shrink_grad, sems.at[2])


def narrow_kernel(
    held_shrink, held_expand, me, lens, after_cross, n3, hidden, slope, kept, gains, *rest
):
    k, both = len(held_shrink.arrays), len(held_shrink.arrays) + len(held_expand.arrays)
    refs_shrink, refs_expand = rest[:k], rest[k:both]
    outs = rest[both:]
    layer_out, grad_cross, gain_part = outs[:3]
    grads, (weight_shrink, weight_expand, expand_grad, grad_norm, total, sems) = (
        outs[3:-6],
        outs[-6:],
    )
    load("shrink", held_shrink, refs_shrink, weight_shrink, me, sems.at[0])
    load("expand", held_expand, refs_expand, weight_expand, me, sems.at[1])
    size = n3.shape[1]
    total[...] = after_cross[...]
    grad_norm[...] = jnp.zeros_like(grad_norm)
    arrived(weight_shrink, sems.at[0])
    arrived(weight_expand, sems.at[1])

    for z in range(4):
        cols = slice(z * size, (z + 1) * size)
        shrink_rows = flat(weight_shrink[z])
        grad = (slope[:, cols].astype(F32) * nt(kept[...], shrink_rows)).astype(BF)
        put_rows(expand_grad, tn(n3[...], grad).astype(BF), cols)
        grad_norm[...] += nt(grad, flat(weight_expand[:, :, :, :, cols]))
        total[...] += nn(hidden[:, cols], shrink_rows)

    store("expand", expand_grad, grads, 0, me, sems.at[2])
    rows = total.shape[0] // lens.shape[0]
    for s in range(lens.shape[0]):
        part = slice(s * rows, (s + 1) * rows)
        keep = lax.broadcasted_iota(jnp.int32, (rows, 1), 0) < lens[s]
        layer_out[s] = jnp.where(keep, total[part, :], 0.0).astype(BF)
    back, gain = norm_back(after_cross[...], gains[2:3, :], grad_norm[...])
    grad_cross[...] = kept[...].astype(F32) + back
    gain_part[...] = gain
    arrived(expand_grad, sems.at[2])


def writer_back_kernel(held, me, grad_cross, mixed, *rest):
    k = len(held.arrays)
    refs, outs = rest[:k], rest[k:]
    grad_mixed, grads, (weight, grad_scratch, sems) = outs[0], outs[1:-3], outs[-3:]
    load("writer", held, refs, weight, me, sems.at[0])
    branch = grad_cross[...].astype(BF)
    put_rows(grad_scratch, tn(mixed[...], branch).astype(BF), slice(None))
    store("writer", grad_scratch, grads, 0, me, sems.at[1])
    arrived(weight, sems.at[0])
    grad_mixed[...] = nt(branch, flat(weight[...])).astype(BF)
    arrived(grad_scratch, sems.at[1])


def query_back_kernel(
    packed_mode,
    held_query,
    held_out,
    me,
    grad_asks,
    n2,
    after_self,
    grad_cross,
    mixed,
    gains,
    *rest,
):
    k, both = len(held_query.arrays), len(held_query.arrays) + len(held_out.arrays)
    refs_query, refs_out = rest[:k], rest[k:both]
    rest = rest[both:]
    grad_self, grad_mixed, gain_part = rest[:3]
    weight_query, weight_out, query_grad, out_grad, sems = rest[-5:]
    grads = rest[3:-5]
    load("query", held_query, refs_query, weight_query, me, sems.at[0])
    load("outward", held_out, refs_out, weight_out, me, sems.at[1])
    put_rows(query_grad, tn(n2[...], grad_asks[...]).astype(BF), slice(None))
    store("query", query_grad, grads if packed_mode else grads[:1], 0, me, sems.at[2])
    arrived(weight_query, sems.at[0])
    back, gain = norm_back(
        after_self[...], gains[1:2, :], nt(grad_asks[...], flat(weight_query[...]))
    )
    total = grad_cross[...] + back
    grad_self[...] = total
    gain_part[...] = gain
    branch = total.astype(BF)
    arrived(weight_out, sems.at[1])
    grad_mixed[...] = nt(branch, flat(weight_out[...])).astype(BF)
    put_rows(out_grad, tn(mixed[...], branch).astype(BF), slice(None))
    store("outward", out_grad, grads if packed_mode else grads[1:], 1, me, sems.at[3])
    arrived(query_grad, sems.at[2])
    arrived(out_grad, sems.at[3])


def inward_grad_kernel(me, n1, gq, gk, gv, *rest):
    grads, (scratch, sem) = rest[:-2], rest[-2:]
    size = n1.shape[1]
    for block, grad in enumerate((gq, gk, gv)):
        cols = slice(block * size, (block + 1) * size)
        put_rows(scratch, tn(n1[...], grad[...]).astype(BF), cols)
    store("inward", scratch, grads, 0, me, sem)
    arrived(scratch, sem)


def inputs_grad_kernel(held, me, x, gq, gk, gv, grad_self, gains, *rest):
    k = len(held.arrays)
    refs, (out, gain_part, weight, sem) = rest[:k], rest[k:]
    load("inward", held, refs, weight, me, sem)
    arrived(weight, sem)
    size = x.shape[1]
    total = 0.0
    for block, grad in enumerate((gq, gk, gv)):
        cols = slice(block * size, (block + 1) * size)
        total = total + nt(grad[...], flat(weight[..., cols]))
    back, gain = norm_back(x[...].astype(F32), gains[0:1, :], total)
    out[...] = grad_self[...] + back
    gain_part[...] = gain


def reader_grad_kernel(me, lens, encoded, gk, gv, *rest):
    grads, (scratch, total, sem) = rest[:-3], rest[-3:]
    step = pl.program_id(0)
    steps = pl.num_programs(0)
    tiles = steps // lens.shape[0]
    size = encoded.shape[1]

    @pl.when(step == 0)
    def _():
        total[...] = jnp.zeros_like(total)

    @pl.when(lax.rem(step, tiles) * KEY_TILE < lens[step // tiles])
    def _():
        left = encoded[...]
        total[:, :size] += tn(left, gk[...])
        total[:, size:] += tn(left, gv[...])

    @pl.when(step == steps - 1)
    def _():
        put_rows(scratch, total[...].astype(BF), slice(None))
        store("reader", scratch, grads, 0, me, sem)
        arrived(scratch, sem)


def encoded_grad_kernel(held, me, lens, gk, gv, *rest):
    refs, (out, weight, sem) = rest[: len(held.arrays)], rest[len(held.arrays) :]
    step = pl.program_id(0)
    tiles = pl.num_programs(0) // lens.shape[0]
    valid = lax.rem(step, tiles) * KEY_TILE < lens[step // tiles]
    size = gk.shape[1]

    @pl.when(step == 0)
    def _():
        load("reader", held, refs, weight, me, sem)
        arrived(weight, sem)

    @pl.when(valid)
    def _():
        out[...] = nt(gk[...], flat(weight[..., :size])) + nt(gv[...], flat(weight[..., size:]))

    @pl.when(jnp.logical_not(valid))
    def _():
        out[...] = jnp.zeros_like(out)


def table_kernel(count, buckets, grad_bias, out):
    pairs, length = grad_bias.shape[:2]
    group = 4
    lane = lax.broadcasted_iota(jnp.int32, out.shape, 1)

    def one(step, total):
        rows = [[] for _ in range(group)]
        for h in range(2 * pairs):
            cols = slice((h % 2) * length, (h % 2 + 1) * length)
            sums = [jnp.zeros((8, length), F32) for _ in range(group)]
            for part in chunks(length):
                value, which = grad_bias[h // 2, part, cols], buckets[part, :]
                for k in range(group):
                    hit = jnp.where(which == step * group + k, value, 0.0)
                    sums[k] = sums[k] + folded(hit, jnp.sum)
            for k in range(group):
                rows[k].append(jnp.sum(sums[k], axis=0, keepdims=True))
        for k in range(group):
            value = jnp.sum(jnp.concatenate(rows[k], axis=0), axis=1, keepdims=True)
            total = total + jnp.where(lane == step * group + k, value, 0.0)
        return total

    out[...] = lax.fori_loop(0, count // group, one, jnp.zeros(out.shape, F32))


def shared_places(widths, piece, width):
    starts = [0]
    for w in widths:
        starts.append(starts[-1] + w // piece)
    return starts[:-1], starts[-1], starts[-1] + 1, starts[-1] + 1 + 3 * (width // piece)


def statistics_kernel(piece, *refs):
    grads, gains, table, rows, shared = refs[:7], refs[7:10], refs[10], refs[11], refs[12]
    width = gains[0].shape[1]
    starts, totals_at, gains_at, table_at = shared_places([g.shape[1] for g in grads], piece, width)
    rows[...] = jnp.zeros_like(rows)
    shared[...] = jnp.zeros_like(shared)
    lane = lax.broadcasted_iota(jnp.int32, (1, 128), 1)
    lane_piece = lax.broadcasted_iota(jnp.int32, (1, piece), 1)
    totals = jnp.zeros((1, piece), F32)
    for j, grad in enumerate(grads):
        square = grad[...] * grad[...]
        count, wide = square.shape
        sums = jnp.sum(square, axis=1, keepdims=True)
        rows[:count, :] += jnp.where(lane == j, sums, 0.0)
        columns = jnp.sum(square, axis=0, keepdims=True)
        for p in range(wide // piece):
            at = starts[j] + p
            shared[at : at + 1, :] = columns[:, p * piece : (p + 1) * piece]
        totals = totals + jnp.where(lane_piece == j, jnp.sum(sums, axis=0, keepdims=True), 0.0)
    shared[totals_at : totals_at + 1, :] = totals
    for k in range(3):
        for p in range(width // piece):
            at = gains_at + k * (width // piece) + p
            shared[at : at + 1, :] = gains[k][:, p * piece : (p + 1) * piece]
    keep = min(piece, table.shape[1])
    shared[table_at : table_at + table.shape[0], :keep] = table[:, :keep]


def steps_kernel(wide, narrow, *refs):
    grads, rows, shared = refs[:7], refs[7], refs[8]
    outs = refs[9:]
    piece = shared.shape[1]
    starts, totals_at, _, _ = shared_places([g.shape[1] for g in grads], piece, piece)
    turned = rows[...].T
    for j, grad in enumerate(grads):
        step, row_out, col_out = outs[3 * j : 3 * j + 3]
        count, width = grad.shape
        full_rows, full_cols = count * wide, width * narrow
        row = rows[:count, j : j + 1] / full_cols + TINY
        mean = shared[totals_at : totals_at + 1, j : j + 1] / (full_rows * full_cols) + TINY
        cols = []
        for p in range(width // piece):
            at = starts[j] + p
            part = slice(p * piece, (p + 1) * piece)
            col = shared[at : at + 1, :] / full_rows + TINY
            step[:, part] = grad[:, part] * lax.rsqrt(row * col / mean)
            cols.append(col)
        row_out[...] = (turned[j : j + 1, :count] / full_cols + TINY).reshape(count)
        col = cols[0] if len(cols) == 1 else jnp.concatenate(cols, axis=1)
        col_out[...] = col.reshape(width)


def tie(value, after):
    after = tuple(after)
    return lax.optimization_barrier((value,) + after)[0] if after else value


def join(gathers, arrays=()):
    keys = [(g, key) for g in gathers for key in g.live]
    flat_values, tree = jax.tree.flatten(([g.live[key] for g, key in keys], list(arrays)))
    values, arrays = jax.tree.unflatten(tree, lax.optimization_barrier(tuple(flat_values)))
    for (g, key), value in zip(keys, values):
        g.live[key] = value
    return arrays


class Hyper:
    MASKS = {"y": 1, "c": 2, "x": 4, "xy": 5, "z1": 8, "z2": 16, "z3": 24}

    def __init__(self):
        wide = lax.axis_index("wide")
        self.z, self.x, self.c = wide // 4, (wide // 2) % 2, wide % 2
        self.y = lax.axis_index("narrow")
        self.me = jnp.stack((self.z, self.x, self.c, self.y)).astype(jnp.int32)

    def swap(self, value, bit, after=()):
        mask = self.MASKS[bit]
        return lax.ppermute(tie(value, after), BOTH, [(i, i ^ mask) for i in range(32)])


class Gather:
    def __init__(self, hyper, shards, plan, width):
        self.hyper, self.plan = hyper, plan
        self.live = {"own": jnp.stack([cut(name, shards[name], width)[p] for name, p in plan])}

    def z(self):
        own = self.live["own"]
        self.live["others"] = [self.hyper.swap(own, bit) for bit in ("z1", "z2", "z3")]

    def z1(self):
        self.live["other"] = self.hyper.swap(self.live["own"], "z1")

    def z2(self):
        h = self.hyper
        own, other = self.live.pop("own"), self.live.pop("other")
        pair = jnp.where(h.z % 2 == 0, jnp.stack((own, other)), jnp.stack((other, own)))
        self.live["own"], self.live["other"] = pair, h.swap(pair, "z2")

    def plane(self):
        h = self.hyper
        own = self.live.pop("own")
        if "others" in self.live:
            one, two, three = self.live.pop("others")
            even = h.z % 2 == 0
            own = jnp.where(even, jnp.stack((own, one)), jnp.stack((one, own)))
            other = jnp.where(even, jnp.stack((two, three)), jnp.stack((three, two)))
        else:
            other = self.live.pop("other")
        quad = jnp.where(
            h.z // 2 == 0, jnp.concatenate((own, other)), jnp.concatenate((other, own))
        )
        self.live["quads"] = [quad] + [h.swap(quad, bit) for bit in ("x", "y", "xy")]

    def core_own(self):
        self.live["first"] = self.hyper.swap(self.live["quads"][0], "c")

    def core(self):
        self.live["cores"] = [self.live.pop("first")] + [
            self.hyper.swap(quad, "c") for quad in self.live["quads"][1:]
        ]

    def held(self, name):
        arrays = [a for two in zip(self.live["quads"], self.live["cores"]) for a in two]
        return Held(arrays, self.plan.index((name, 0)))


def fold_kernel(counts, joint, names, me, *refs):
    na, nb, nj = counts
    first, second, both, outs = refs[:na], refs[na : na + nb], refs[na + nb : na + nb + nj], refs[na + nb + nj :]
    pa = first[0].shape[3]

    def add(parts, part):
        return sum([r[...].astype(F32) for r in parts] + [r[:, :, :, part].astype(F32) for r in both])

    one = add(first, slice(0, pa))
    two = add(second, slice(pa, None))
    if names:
        pieces = [one[0, 0, 0, p] for p in range(one.shape[3])]
        pieces += [two[0, 0, 0, p] for p in range(two.shape[3])]
        for out, (name, start) in zip(outs, names):
            for p in range(COUNTS[name]):
                piece = pieces[start + p]
                if name == "shrink":
                    out[p * piece.shape[0] : (p + 1) * piece.shape[0], :] = piece
                else:
                    out[:, p * piece.shape[1] : (p + 1) * piece.shape[1]] = piece
    elif joint:
        outs[0][:, :, :, :pa] = one.astype(outs[0].dtype)
        outs[0][:, :, :, pa:] = two.astype(outs[0].dtype)
    else:
        outs[0][...] = one.astype(outs[0].dtype)
        outs[1][...] = two.astype(outs[1].dtype)


class HalvedScatter:
    def __init__(self, hyper, first, second, name):
        self.hyper, self.halves, self.name = hyper, (first, second), name
        self.parts = [[], []]
        self.joint = []
        self.sizes = [half[0].shape[3] for half in (first, second)]
        self.block = first[0].shape[4:]

    def core(self, half, after=()):
        keep, send = self.halves[half]
        recv = self.hyper.swap(send, "c", after)
        self.parts[half] = [keep, recv]
        return [recv]

    def fold(self, picks, out_dims, joint, after, step):
        ins = []
        for half in range(2):
            p = self.sizes[half]
            for array, (dims, index) in zip(self.parts[half], picks[half]):
                spec = pl.BlockSpec(
                    tuple(dims) + (p,) + self.block,
                    lambda i, me, index=index: tuple(index(me)) + (0, 0, 0),
                )
                ins.append((array, spec))
        whole = sum(self.sizes)
        for array, index in zip(self.joint, picks[2]):
            spec = pl.BlockSpec(
                (1, 1, 1, whole) + self.block,
                lambda i, me, index=index: (index(me), 0, 0, 0, 0, 0),
            )
            ins.append((array, spec))
        outs = []
        rows, cols = self.block
        for dims, kind in out_dims:
            if isinstance(dims, str):
                count = COUNTS[dims]
                full = (count * rows, cols) if dims == "shrink" else (rows, count * cols)
                outs.append((shape(full, F32), pl.BlockSpec(full, lambda i, me: (0, 0))))
                continue
            p = whole if joint else self.sizes[len(outs)]
            full = tuple(dims) + (p,) + self.block
            outs.append((shape(full, kind), pl.BlockSpec(full, lambda i, me: (0,) * 6)))
        counts = (len(self.parts[0]), len(self.parts[1]), len(self.joint))
        names = out_dims if step == "last" else None
        self.sent = launch(
            functools.partial(fold_kernel, counts, joint, names),
            ins,
            outs,
            grid=(1,),
            gflop=1.0,
            name=f"{self.name}_{step}",
            after=after,
            prefetch=(self.hyper.me,),
        )
        return self.sent

    def p1(self, after=()):
        a = [((4, 2, 1), lambda me: (0, 0, 1 - me[3]))] * 2
        b = [((4, 1, 2), lambda me: (0, 1 - me[1], 0))] * 2
        sent = self.fold((a, b, ()), (((4, 2, 1), BF), ((4, 1, 2), BF)), False, after, "p1")
        recv = [self.hyper.swap(value, bit) for value, bit in zip(sent, "yx")]
        for half in range(2):
            self.parts[half].append(recv[half])
        return recv

    def p2(self, after=()):
        four = (4, 1, 1)
        a = [(four, lambda me: (0, 1 - me[1], me[3]))] * 2
        a += [(four, lambda me: (0, 1 - me[1], 0))]
        b = [(four, lambda me: (0, me[1], 1 - me[3]))] * 2
        b += [(four, lambda me: (0, 0, 1 - me[3]))]
        sent = self.fold((a, b, ()), ((four, BF), (four, BF)), False, after, "p2")
        recv = [self.hyper.swap(value, bit) for value, bit in zip(sent, "xy")]
        for half in range(2):
            self.parts[half].append(recv[half])
        return recv

    def own(self, count, place):
        dims = (count, 1, 1)
        a = [(dims, lambda me: (place(me), me[1], me[3]))] * 2
        a += [(dims, lambda me: (place(me), me[1], 0)), (dims, lambda me: (place(me), 0, 0))]
        b = [(dims, lambda me: (place(me), me[1], me[3]))] * 2
        b += [(dims, lambda me: (place(me), 0, me[3])), (dims, lambda me: (place(me), 0, 0))]
        return a, b

    def z2(self, after=()):
        a, b = self.own(2, lambda me: 1 - me[0] // 2)
        (sent,) = self.fold((a, b, ()), (((2, 1, 1), BF),), True, after, "z2")
        recv = self.hyper.swap(sent, "z2")
        self.joint.append(recv)
        return [recv]

    def z1(self, after=()):
        a, b = self.own(1, lambda me: (me[0] // 2) * 2 + 1 - lax.rem(me[0], 2))
        j = [lambda me: 1 - lax.rem(me[0], 2)]
        (sent,) = self.fold((a, b, j), (((1, 1, 1), BF),), True, after, "z1")
        recv = self.hyper.swap(sent, "z1")
        self.joint.append(recv)
        return [recv]

    def last(self, weights, after=()):
        a, b = self.own(1, lambda me: me[0])
        j = [lambda me: lax.rem(me[0], 2), lambda me: 0]
        return self.fold((a, b, j), weights, True, after, "last")


def plane_kernel(me, *refs):
    groups, outs = refs[:-4], refs[-4:]
    for k, out in enumerate(outs):
        x, y = me[1] ^ (k & 1), me[3] ^ (k >> 1)
        at = 0
        for keep, recv in zip(groups[::2], groups[1::2]):
            total = keep[:, x, y].astype(F32) + recv[:, x, y].astype(F32)
            out[:, at : at + total.shape[1]] = total.astype(out.dtype)
            at += total.shape[1]


def line_kernel(me, own, one, two, three, *outs):
    for k, out in enumerate(outs):
        z = me[0] ^ k
        total = own[z] + one[z].astype(F32) + two[z].astype(F32) + three[z].astype(F32)
        out[...] = total.astype(out.dtype)


def last_kernel(names, own, one, two, three, *outs):
    total = own[...] + one[...].astype(F32) + two[...].astype(F32) + three[...].astype(F32)
    at = 0
    for out, name in zip(outs, names):
        for p in range(COUNTS[name]):
            piece = total[at + p]
            if name == "shrink":
                out[p * piece.shape[0] : (p + 1) * piece.shape[0], :] = piece
            else:
                out[:, p * piece.shape[1] : (p + 1) * piece.shape[1]] = piece
        at += COUNTS[name]


class Scatter:
    def __init__(self, hyper, name, weights):
        self.hyper, self.name, self.weights = hyper, name, weights
        self.groups = []

    def core(self, keep, send):
        self.groups.append((keep, self.hyper.swap(send, "c")))

    def plane(self, after=()):
        count = sum(keep.shape[3] for keep, _ in self.groups)
        block = self.groups[0][0].shape[4:]
        dims = (4, count) + block
        self.own, *sent = launch(
            plane_kernel,
            [(self.hyper.me, SM)] + [(a, VM) for group in self.groups for a in group],
            [(shape(dims, F32), VM)] + [(shape(dims, BF), VM)] * 3,
            name=self.name + "_plane",
            after=after,
        )
        self.sent = sent
        self.got = [self.hyper.swap(a, bit) for a, bit in zip(sent, ("x", "y", "xy"))]

    def line(self, after=()):
        dims = self.own.shape[1:]
        self.own, *sent = launch(
            line_kernel,
            [(self.hyper.me, SM), (self.own, VM)] + [(a, VM) for a in self.got],
            [(shape(dims, F32), VM)] + [(shape(dims, BF), VM)] * 3,
            name=self.name + "_line",
            after=after,
        )
        self.sent = sent
        self.got = [self.hyper.swap(a, bit) for a, bit in zip(sent, ("z1", "z2", "z3"))]

    def last(self, after=()):
        rows, cols = self.own.shape[1:]
        outs = []
        for name in self.weights:
            count = COUNTS[name]
            full = (count * rows, cols) if name == "shrink" else (rows, count * cols)
            outs.append((shape(full, F32), VM))
        totals = launch(
            functools.partial(last_kernel, self.weights),
            [(self.own, VM)] + [(a, VM) for a in self.got],
            outs,
            name=self.name + "_last",
            after=after,
        )
        self.sent = totals
        return dict(zip(self.weights, totals))


def cut(name, shard, width):
    count = COUNTS[name]
    if name == "shrink":
        return shard.reshape(count, shard.shape[0] // count, shard.shape[1])
    rows, cols = shard.shape
    return jnp.transpose(shard.reshape(rows, count, cols // count), (1, 0, 2))


def whole_shape(name, width):
    if name == "shrink":
        return (4, 2, 2, 4, width // 16, width)
    return (4, 2, 2, width // 16, width * COUNTS[name])


def local(
    inputs,
    encoded,
    target_lengths,
    memory_lengths,
    buckets,
    cotangent,
    self_inward,
    self_outward,
    cross_query,
    cross_reader,
    cross_writer,
    expand_weight,
    shrink_weight,
    norm_gains,
    bias_table,
):
    wide_count = lax.axis_size("wide")
    narrow_count = lax.axis_size("narrow")
    fast = (wide_count, narrow_count) == (16, 2)
    seqs, length, width = inputs.shape
    memory_size = encoded.shape[1]
    rows, mem_rows = seqs * length, seqs * memory_size
    wide_hidden = expand_weight.shape[1] * narrow_count
    shards = dict(
        zip(
            NAMES,
            (
                self_inward,
                self_outward,
                cross_query,
                cross_reader,
                cross_writer,
                expand_weight,
                shrink_weight,
            ),
        )
    )
    hyper = Hyper() if fast else None
    me = hyper.me if fast else jnp.zeros((4,), jnp.int32)
    none = []

    def grad_outs(name, count):
        if fast:
            block = shape((4, 2, 2, count, width // 16, width // 2), BF)
            return [(block, HB), (block, HB)]
        return [(shape(whole_shape(name, width), BF), HB)]

    dma = pltpu.SemaphoreType.DMA
    x_rows = inputs.reshape(rows, width)
    mem_flat = encoded.reshape(mem_rows, width)
    heads = HEADS
    pairs_count = heads // 2
    turned = buckets.T
    table = jnp.pad(bias_table.T, ((0, 0), (0, 128 - bias_table.shape[0])))

    def weights(*names):
        return [entry for name in names for entry in held[name].ins()]

    held = {}
    if fast:
        ga, gb, gc, gd = [Gather(hyper, shards, plan, width) for plan in GATHERS]
        ga.z()
    else:
        for name in NAMES:
            full = lax.all_gather(shards[name], "narrow", axis=1, tiled=True)
            full = lax.all_gather(full, "wide", axis=0, tiled=True)
            full = full.reshape(whole_shape(name, width))
            held[name] = Held((full,))

    n1, kept, bias = launch(
        prepare_kernel,
        [
            (target_lengths, SM),
            (inputs, VM),
            (cotangent, VM),
            (norm_gains, VM),
            (turned, VM),
            (table, VM),
        ],
        [
            (shape((rows, width), BF), VM),
            (shape((rows, width), BF), VM),
            (shape((pairs_count, length, 2 * length), F32), VM),
        ],
        name="prepare",
    )

    if fast:
        n1, kept, bias = join((ga,), (n1, kept, bias))
        ga.plane()
        ga.core_own()
        gb.z1()
        gb.z2()
        join((ga, gb))
        ga.core()
        gb.plane()
        gc.z1()
        for name in ("inward", "outward"):
            held[name] = ga.held(name)

    (packed,) = launch(
        functools.partial(inward_kernel, held["inward"]),
        [(me, SM), (n1, VM)] + weights("inward"),
        [(shape((rows, 3 * width), BF), VM)],
        [weight_scratch("inward", width), dma],
        gflop=2.0,
        name="inward",
    )

    bias_spec = pl.BlockSpec((2, length, 2 * length), lambda p: (p, 0, 0))
    log_both = pl.BlockSpec((2, seqs, 1, 2 * length), lambda p: (p, 0, 0, 0))
    log_spec = pl.BlockSpec((2, 1, 1, 2 * length), lambda s, p: (p, s, 0, 0))
    log_shape = shape((pairs_count, seqs, 1, 2 * length), F32)
    blocks = pairs_count // 2
    self_mixed, self_log = launch(
        self_forward_kernel,
        [
            (packed, both_spec(rows)),
            (packed, both_spec(rows, blocks)),
            (packed, both_spec(rows, 2 * blocks)),
            (bias, bias_spec),
        ],
        [(shape((rows, width), BF), both_spec(rows)), (log_shape, log_both)],
        attend_scratch(4, length, length, False),
        grid=(blocks,),
        gflop=5.0,
        name="self_forward",
    )

    if fast:
        self_mixed, self_log = join((gc,), (self_mixed, self_log))
        gc.z2()

    after_self, n2 = launch(
        functools.partial(outward_kernel, held["outward"]),
        [(me, SM), (x_rows, VM), (self_mixed, VM), (norm_gains, VM)] + weights("outward"),
        [(shape((rows, width), F32), VM), (shape((rows, width), BF), VM)],
        [weight_scratch("outward", width), dma],
        gflop=2.0,
        name="outward",
    )

    if fast:
        after_self, n2 = join((gb, gc), (after_self, n2))
        gb.core_own()
        gb.core()
        gc.plane()
        gd.z1()
        for name in ("query", "writer", "reader"):
            held[name] = gb.held(name)

    tile_spec = pl.BlockSpec((KEY_TILE, width), lambda i: (i, 0))
    asks, pairs = launch(
        functools.partial(memory_kernel, held["query"], held["reader"]),
        [(me, SM), (memory_lengths, SM), (n2, VM), (mem_flat, tile_spec)]
        + weights("query", "reader"),
        [
            (shape((rows, width), BF), pl.BlockSpec((rows, width), lambda i: (0, 0))),
            (
                shape((mem_rows, 2 * width), BF),
                pl.BlockSpec((KEY_TILE, 2 * width), lambda i: (i, 0)),
            ),
        ],
        [weight_scratch("query", width), weight_scratch("reader", width), dma((2,))],
        grid=(mem_rows // KEY_TILE,),
        gflop=6.0,
        name="memory",
    )

    if fast:
        asks, pairs = join((gd,), (asks, pairs))
        gc.core_own()
        gd.z2()

    cross_mixed, cross_log = launch(
        cross_forward_kernel,
        [
            (memory_lengths, SM),
            (asks, pair_spec(length)),
            (pairs, pair_spec(memory_size)),
            (pairs, pair_spec(memory_size, blocks)),
        ],
        [(shape((rows, width), BF), pair_spec(length)), (log_shape, log_spec)],
        attend_scratch(2, memory_size, length, False),
        grid=(seqs, blocks),
        gflop=10.0,
        name="cross_forward",
    )

    if fast:
        cross_mixed, cross_log = join((gc, gd), (cross_mixed, cross_log))
        gc.core()
        held["expand"] = gc.held("expand")
        gd.plane()
        gd.core_own()

    after_cross, n3, hidden, slope, *shrink_parts = launch(
        functools.partial(widen_kernel, held["writer"], held["expand"]),
        [(me, SM), (after_self, VM), (cross_mixed, VM), (norm_gains, VM), (kept, VM)]
        + weights("writer", "expand"),
        [
            (shape((rows, width), F32), VM),
            (shape((rows, width), BF), VM),
            (shape((rows, wide_hidden), BF), VM),
            (shape((rows, wide_hidden), BF), VM),
        ]
        + grad_outs("shrink", 4),
        [
            weight_scratch("writer", width),
            weight_scratch("expand", width),
            weight_scratch("shrink", width),
            dma((3,)),
        ],
        gflop=10.0,
        name="widen",
    )

    if fast:
        after_cross, n3, hidden, slope = join((gd,), (after_cross, n3, hidden, slope))
        gd.core()
        held["shrink"] = gd.held("shrink")

    layer_out, grad_cross, gain_third, *expand_parts = launch(
        functools.partial(narrow_kernel, held["shrink"], held["expand"]),
        [
            (me, SM),
            (target_lengths, SM),
            (after_cross, VM),
            (n3, VM),
            (hidden, VM),
            (slope, VM),
            (kept, VM),
            (norm_gains, VM),
        ]
        + weights("shrink", "expand"),
        [
            (shape((seqs, length, width), BF), VM),
            (shape((rows, width), F32), VM),
            (shape((1, width), F32), VM),
        ]
        + grad_outs("expand", 4),
        [
            weight_scratch("shrink", width),
            weight_scratch("expand", width),
            weight_scratch("expand", width),
            pltpu.VMEM((rows, width), F32),
            pltpu.VMEM((rows, width), F32),
            dma((3,)),
        ],
        gflop=14.0,
        name="narrow",
    )

    if fast:
        sf = HalvedScatter(hyper, shrink_parts, expand_parts, "ffn")
        sf.core(0)
        sf.core(1)

    grad_mixed, *writer_parts = launch(
        functools.partial(writer_back_kernel, held["writer"]),
        [(me, SM), (grad_cross, VM), (cross_mixed, VM)] + weights("writer"),
        [(shape((rows, width), BF), VM)] + grad_outs("writer", 1),
        [weight_scratch("writer", width), weight_scratch("writer", width), dma((2,))],
        gflop=2.0,
        name="writer_back",
    )

    if fast:
        sf.p1([grad_mixed])

    grad_asks, grad_mem_keys, grad_mem_values = launch(
        cross_backward_kernel,
        [
            (memory_lengths, SM),
            (asks, pair_spec(length)),
            (pairs, pair_spec(memory_size)),
            (pairs, pair_spec(memory_size, blocks)),
            (grad_mixed, pair_spec(length)),
            (cross_mixed, pair_spec(length)),
            (cross_log, log_spec),
        ],
        [
            (shape((rows, width), BF), pair_spec(length)),
            (shape((mem_rows, width), BF), pair_spec(memory_size)),
            (shape((mem_rows, width), BF), pair_spec(memory_size)),
        ],
        attend_scratch(2, memory_size, length, True),
        grid=(seqs, blocks),
        gflop=20.0,
        name="cross_backward",
        after=sf.sent if fast else none,
    )

    reader_parts = launch(
        reader_grad_kernel,
        [
            (me, SM),
            (memory_lengths, SM),
            (mem_flat, tile_spec),
            (grad_mem_keys, tile_spec),
            (grad_mem_values, tile_spec),
        ],
        grad_outs("reader", 2),
        [weight_scratch("reader", width), pltpu.VMEM((width, 2 * width), F32), dma],
        grid=(mem_rows // KEY_TILE,),
        gflop=5.0,
        name="reader_grad",
    )

    if fast:
        sf.p2([reader_parts[0]])
        sm = Scatter(hyper, "middle", ("writer", "reader", "query", "outward"))
        sm.core(*writer_parts)
        sm.core(*reader_parts)

    grad_self, grad_mixed, gain_second, *rest_parts = launch(
        functools.partial(query_back_kernel, fast, held["query"], held["outward"]),
        [
            (me, SM),
            (grad_asks, VM),
            (n2, VM),
            (after_self, VM),
            (grad_cross, VM),
            (self_mixed, VM),
            (norm_gains, VM),
        ]
        + weights("query", "outward"),
        [
            (shape((rows, width), F32), VM),
            (shape((rows, width), BF), VM),
            (shape((1, width), F32), VM),
        ]
        + (grad_outs("query", 2) if fast else grad_outs("query", 1) + grad_outs("outward", 1)),
        [
            weight_scratch("query", width),
            weight_scratch("outward", width),
            weight_scratch("query", width),
            weight_scratch("outward", width),
            dma((4,)),
        ],
        gflop=4.0,
        name="query_back",
        after=sf.sent if fast else none,
    )

    if fast:
        sm.core(*rest_parts)
        sf.z2([grad_mixed])
        sm.plane(sf.sent)

    grad_query, grad_keys, grad_values, grad_bias = launch(
        self_backward_kernel,
        [
            (packed, both_spec(rows)),
            (packed, both_spec(rows, blocks)),
            (packed, both_spec(rows, 2 * blocks)),
            (grad_mixed, both_spec(rows)),
            (self_mixed, both_spec(rows)),
            (bias, bias_spec),
            (self_log, log_both),
        ],
        [(shape((rows, width), BF), both_spec(rows))] * 3
        + [(shape((pairs_count, length, 2 * length), F32), bias_spec)],
        attend_scratch(4, length, length, True),
        grid=(blocks,),
        gflop=6.0,
        name="self_backward",
        after=sm.sent if fast else none,
    )

    inward_parts = launch(
        inward_grad_kernel,
        [(me, SM), (n1, VM), (grad_query, VM), (grad_keys, VM), (grad_values, VM)],
        grad_outs("inward", 3),
        [weight_scratch("inward", width), dma],
        gflop=2.0,
        name="inward_grad",
    )

    if fast:
        si = Scatter(hyper, "inward", ("inward",))
        si.core(*inward_parts)
        sf.z1([inward_parts[0]])

    inputs_grad, gain_first = launch(
        functools.partial(inputs_grad_kernel, held["inward"]),
        [
            (me, SM),
            (x_rows, VM),
            (grad_query, VM),
            (grad_keys, VM),
            (grad_values, VM),
            (grad_self, VM),
            (norm_gains, VM),
        ]
        + weights("inward"),
        [(shape((rows, width), F32), VM), (shape((1, width), F32), VM)],
        [weight_scratch("inward", width), dma],
        gflop=2.0,
        name="inputs_grad",
        after=sf.sent if fast else none,
    )

    if fast:
        si.plane([inputs_grad])
        sm.line(si.sent)
        sums = dict(zip(("shrink", "expand"), sf.last((("shrink", 0), ("expand", 4)), sm.sent)))

    (encoded_grad,) = launch(
        functools.partial(encoded_grad_kernel, held["reader"]),
        [(me, SM), (memory_lengths, SM), (grad_mem_keys, tile_spec), (grad_mem_values, tile_spec)]
        + weights("reader"),
        [(shape((mem_rows, width), F32), tile_spec)],
        [weight_scratch("reader", width), dma],
        grid=(mem_rows // KEY_TILE,),
        gflop=5.0,
        name="encoded_grad",
        after=sf.sent if fast else none,
    )

    if fast:
        si.line([encoded_grad])

    (table_part,) = launch(
        functools.partial(table_kernel, bias_table.shape[0]),
        [(turned, VM), (grad_bias, VM)],
        [(shape((heads, 128), F32), VM)],
        gflop=6.0,
        name="table",
        after=si.sent if fast else none,
    )

    if fast:
        sums.update(sm.last([table_part]))
        sums.update(si.last(sm.sent))
    else:
        sums = {}
        parts = {
            "shrink": shrink_parts[0],
            "expand": expand_parts[0],
            "writer": writer_parts[0],
            "reader": reader_parts[0],
            "query": rest_parts[0],
            "outward": rest_parts[1],
            "inward": inward_parts[0],
        }
        for name in NAMES:
            full = parts[name].reshape(-1, parts[name].shape[-1]).astype(F32)
            full = lax.psum_scatter(full, "wide", scatter_dimension=0, tiled=True)
            sums[name] = lax.psum_scatter(full, "narrow", scatter_dimension=1, tiled=True)

    grads = [sums[name] for name in NAMES]
    tallest = max(g.shape[0] for g in grads)
    piece = width // narrow_count
    _, totals_at, gains_at, table_at = shared_places([g.shape[1] for g in grads], piece, width)
    row_sums, shared = launch(
        functools.partial(statistics_kernel, piece),
        [(g, VM) for g in grads]
        + [(gain_first, VM), (gain_second, VM), (gain_third, VM), (table_part, VM)],
        [(shape((tallest, 128), F32), VM), (shape((-(-(table_at + heads) // 8) * 8, piece), F32), VM)],
        name="statistics",
    )
    add_y = lax.broadcasted_iota(jnp.int32, shared.shape, 0) >= totals_at
    if fast:
        other = hyper.swap(row_sums, "y")
        shared = shared + jnp.where(add_y, hyper.swap(shared, "y"), 0.0)
        row_sums = row_sums + other
        shared = tie(shared, [other])
        for bit in ("c", "x", "z1", "z2"):
            shared = shared + hyper.swap(shared, bit)
    else:
        row_sums = lax.psum(row_sums, "narrow")
        shared = lax.psum(jnp.where(add_y, lax.psum(shared, "narrow"), shared), "wide")

    step_outs = []
    for g in grads:
        step_outs.append((shape(g.shape, F32), VM))
        step_outs.append((shape((g.shape[0],), F32), VM))
        step_outs.append((shape((g.shape[1],), F32), VM))
    made = launch(
        functools.partial(steps_kernel, wide_count, narrow_count),
        [(g, VM) for g in grads] + [(row_sums, VM), (shared, VM)],
        step_outs,
        name="steps",
    )
    results = []
    for j, grad in enumerate(grads):
        step, row_stat, col_stat = made[3 * j : 3 * j + 3]
        results.extend([grad, step, row_stat, col_stat])
    gains_grad = shared[gains_at:table_at].reshape(3, width)
    table_grad = shared[table_at : table_at + heads, : bias_table.shape[0]].T
    return (
        (
            layer_out,
            inputs_grad.reshape(inputs.shape),
            encoded_grad.reshape(encoded.shape),
        )
        + tuple(results)
        + (gains_grad, table_grad)
    )


def solution(mesh):
    tokens = P(BOTH, None, None)
    weight = P("wide", "narrow")
    per_weight = (weight, weight, P("wide"), P("narrow"))
    return jax.shard_map(
        local,
        mesh=mesh,
        in_specs=(tokens, tokens, P(BOTH), P(BOTH), P(), tokens) + (weight,) * 7 + (P(), P()),
        out_specs=(tokens, tokens, tokens) + per_weight * 7 + (P(), P()),
        check_vma=False,
    )
```

```python
import functools

import jax
import jax.numpy as jnp
from jax import lax
from jax.experimental import pallas as pl
from jax.experimental.pallas import tpu as pltpu
from jax.sharding import PartitionSpec as P

HEADS = 12
DH = 64
EPS = 1e-06
TINY = 1e-30
NEGATIVE = -1e30
SCALE = DH ** (-0.5)

BF = jnp.bfloat16
F32 = jnp.float32
BOTH = ("wide", "narrow")
VMEM_LIMIT = 63 * 1024 * 1024
KEY_TILE = 256

COUNTS = {
    "inward": 3,
    "outward": 1,
    "query": 1,
    "reader": 2,
    "writer": 1,
    "expand": 4,
    "shrink": 4,
}
NAMES = ("inward", "outward", "query", "reader", "writer", "expand", "shrink")
GATHERS = (
    (("inward", 0), ("inward", 1), ("inward", 2), ("outward", 0)),
    (("query", 0), ("writer", 0), ("reader", 0), ("reader", 1)),
    (("expand", 0), ("expand", 1), ("expand", 2), ("expand", 3)),
    (("shrink", 0), ("shrink", 1), ("shrink", 2), ("shrink", 3)),
)


def nn(left, right):
    return lax.dot_general(left, right, (((1,), (0,)), ((), ())), preferred_element_type=F32)


def nt(left, right):
    return lax.dot_general(left, right, (((1,), (1,)), ((), ())), preferred_element_type=F32)


def tn(left, right):
    return lax.dot_general(left, right, (((0,), (0,)), ((), ())), preferred_element_type=F32)


VM = pl.BlockSpec(memory_space=pltpu.VMEM)
SM = pl.BlockSpec(memory_space=pltpu.SMEM)
HB = pl.BlockSpec(memory_space=pl.ANY)


def launch(
    body, ins, outs, scratch=(), grid=None, alias=None, gflop=1.0, name=None, after=(), prefetch=()
):
    ahead, count, extra = len(prefetch), len(ins), len(after)

    def trimmed(*refs):
        body(*refs[: ahead + count], *refs[ahead + count + extra :])

    params = dict(
        out_shape=[o for o, _ in outs],
        input_output_aliases={ahead + k: v for k, v in (alias or {}).items()},
        compiler_params=pltpu.CompilerParams(vmem_limit_bytes=VMEM_LIMIT),
        cost_estimate=pl.CostEstimate(
            flops=int(gflop * 1e10), bytes_accessed=1 << 22, transcendentals=0
        ),
        name=name,
    )
    specs = dict(
        grid=grid if grid is not None else (),
        in_specs=[s for _, s in ins] + [HB] * extra,
        out_specs=[s for _, s in outs],
        scratch_shapes=list(scratch),
    )
    if ahead:
        specs = dict(grid_spec=pltpu.PrefetchScalarGridSpec(num_scalar_prefetch=ahead, **specs))
    return pl.pallas_call(trimmed, **params, **specs)(*prefetch, *[a for a, _ in ins], *after)


def shape(dims, dtype):
    return jax.ShapeDtypeStruct(tuple(dims), dtype)


def weight_scratch(name, width):
    if name == "shrink":
        return pltpu.VMEM((4, 2, 2, 4, width // 16, width), BF)
    return pltpu.VMEM((4, 2, 2, width // 16, width * COUNTS[name]), BF)


class Held:
    def __init__(self, arrays, start=0):
        self.arrays, self.start = list(arrays), start

    def ins(self):
        return [(a, HB) for a in self.arrays]


def load(name, held, refs, scratch, me, sem):
    if len(refs) == 1 and refs[0].shape == scratch.shape:
        pltpu.make_async_copy(refs[0], scratch, sem).start()
        return
    count = COUNTS[name]
    piece = refs[0].shape[-1]

    def columns(y, p):
        if name == "shrink":
            return pl.ds(pl.multiple_of(y * piece, 128), piece)
        return pl.ds(pl.multiple_of((y * count + p) * piece, 128), piece)

    for p in range(count):
        if len(refs) == 1:
            for y in range(2):
                src = refs[0].at[:, :, :, y, held.start + p]
                cols = columns(y, p)
                dst = scratch.at[:, :, :, p, :, cols] if name == "shrink" else scratch.at[:, :, :, :, cols]
                pltpu.make_async_copy(src, dst, sem).start()
            continue
        for k in range(4):
            for b in range(2):
                x, y, c = me[1] ^ (k & 1), me[3] ^ (k >> 1), me[2] ^ b
                src = refs[k * 2 + b].at[:, held.start + p]
                cols = columns(y, p)
                dst = scratch.at[:, x, c, p, :, cols] if name == "shrink" else scratch.at[:, x, c, :, cols]
                pltpu.make_async_copy(src, dst, sem).start()


def arrived(scratch, sem):
    pltpu.make_async_copy(scratch, scratch, sem).wait()


def store(name, scratch, outs, start, me, sem):
    if len(outs) == 1 and outs[0].shape == scratch.shape:
        pltpu.make_async_copy(scratch, outs[0], sem).start()
        return
    count = COUNTS[name]
    piece = outs[0].shape[-1]
    if len(outs) == 1:
        for y in range(2):
            for p in range(count):
                src = scratch.at[:, :, :, p, :, pl.ds(y * piece, piece)]
                pltpu.make_async_copy(src, outs[0].at[:, :, :, y, p], sem).start()
        return
    for b in range(2):
        c = me[2] ^ b
        for y in range(2):
            for p in range(count):
                if name == "shrink":
                    src = scratch.at[:, :, c, p, :, pl.ds(y * piece, piece)]
                else:
                    src = scratch.at[:, :, c, :, pl.ds((y * count + p) * piece, piece)]
                pltpu.make_async_copy(src, outs[b].at[:, :, y, start + p], sem).start()


def flat(block):
    return block.reshape(-1, block.shape[-1])


def put_rows(scratch, value, cols):
    scratch[:, :, :, :, cols] = value.reshape(scratch.shape[:4] + (value.shape[-1],))


def normed(values, gain):
    r = lax.rsqrt(jnp.mean(values * values, axis=-1, keepdims=True) + EPS)
    return values * r * gain


def norm_back(values, gain, grad):
    r = lax.rsqrt(jnp.mean(values * values, axis=-1, keepdims=True) + EPS)
    inner = jnp.mean(values * gain * grad, axis=-1, keepdims=True)
    back = r * gain * grad - values * (r * r * r * inner)
    return back, jnp.sum(grad * values * r, axis=0, keepdims=True)


def prepare_kernel(lens, x, cot, gains, buckets, table, n1, kept, bias):
    rows = cot.shape[1]
    for s in range(x.shape[0]):
        values = x[s].astype(F32)
        n1[s * rows : (s + 1) * rows, :] = normed(values, gains[0:1, :]).astype(BF)
        keep = lax.broadcasted_iota(jnp.int32, (rows, 1), 0) < lens[s]
        kept[s * rows : (s + 1) * rows, :] = jnp.where(keep, cot[s].astype(F32), 0.0).astype(BF)
    half = 128
    heads = 2 * bias.shape[0]

    @pl.loop(0, rows // 8)
    def _(step):
        start = pl.multiple_of(step * 8, 8)
        for side in range(rows // half):
            which = buckets[pl.ds(start, 8), side * half : (side + 1) * half]
            key = start + lax.broadcasted_iota(jnp.int32, (8, half), 0)
            query = side * half + lax.broadcasted_iota(jnp.int32, (8, half), 1)
            for h in range(heads):
                row = jnp.broadcast_to(table[h : h + 1, :], (8, half))
                found = jnp.take_along_axis(row, which, axis=1)
                at = (h % 2) * rows + side * half
                bias[h // 2, pl.ds(start, 8), at : at + half] = jnp.where(
                    key <= query, found, NEGATIVE
                )


CHUNK = 32


def stacked(block):
    lane = lax.broadcasted_iota(jnp.int32, block.shape, 1)
    zero = jnp.zeros_like(block)
    return jnp.concatenate((jnp.where(lane < DH, block, zero), jnp.where(lane < DH, zero, block)))


def unstacked(block):
    queries = block.shape[1] // 2
    return jnp.concatenate((block[:DH, :queries], block[DH:, queries:]), axis=0).T


def folded(block, by):
    return by(block.reshape(block.shape[0] // 8, 8, block.shape[1]), axis=0)


def chunks(size):
    return [slice(at, at + CHUNK) for at in range(0, size, CHUNK)]


def forward_units(units, size, fix):
    for query, keys, values, scores, probs, mixed, logsum, which in units:
        scores[:size] = nt(keys, stacked(query * jnp.asarray(SCALE, BF)))
    for query, keys, values, scores, probs, mixed, logsum, which in units:
        top = None
        for part in chunks(size):
            block, changed = fix(scores[part], part, which)
            if changed:
                scores[part] = block
            block = folded(block, jnp.max)
            top = block if top is None else jnp.maximum(top, block)
        highest = jnp.max(top, axis=0, keepdims=True)
        total = jnp.zeros((8, highest.shape[1]), F32)
        for part in chunks(size):
            weights = jnp.exp(scores[part] - highest)
            total = total + folded(weights, jnp.sum)
            probs[part] = weights.astype(BF)
        total = jnp.sum(total, axis=0, keepdims=True)
        logsum[...] = highest + jnp.log(total)
        mixed[...] = unstacked(tn(values, probs[:size]) * (1.0 / total)).astype(BF)


def backward_units(units, size, fix):
    for query, keys, values, grad, mixed, logsum, scores, slopes, probs, grads, outs, which in units:
        scores[:size] = nt(keys, stacked(query * jnp.asarray(SCALE, BF)))
        slopes[:size] = nt(values, stacked(grad))
    for query, keys, values, grad, mixed, logsum, scores, slopes, probs, grads, outs, which in units:
        product = stacked(grad.astype(F32) * mixed.astype(F32))
        high = product.astype(BF)
        low = (product - high.astype(F32)).astype(BF)
        ones = jnp.ones((8, product.shape[1]), BF)
        inner = (nt(ones, high) + nt(ones, low))[0:1]
        for part in chunks(size):
            block, keep = fix(scores[part], part, which)
            weights = jnp.exp(block - logsum[...])
            if keep is not None:
                weights = jnp.where(keep, weights, 0.0)
            probs[part] = weights.astype(BF)
            grads[part] = (weights * (slopes[part] - inner)).astype(BF)
        left = grads[:size]
        outs[0][...] = (unstacked(tn(keys, left)) * SCALE).astype(BF)
        outs[1][...] = nn(left, stacked(query * jnp.asarray(SCALE, BF))).astype(BF)
        outs[2][...] = nn(probs[:size], stacked(grad)).astype(BF)


def self_units(length):
    return [(slice(s * length, (s + 1) * length), slice(j * 128, (j + 1) * 128), s, j) for s in range(2) for j in range(2)]


def self_forward_kernel(query, keys, values, bias, mixed, logsum, scores, probs):
    length = bias.shape[1]
    units = []
    for rows, cols, s, j in self_units(length):
        u = s * 2 + j
        units.append(
            (
                query[rows, cols],
                keys[rows, cols],
                values[rows, cols],
                scores.at[u],
                probs.at[u],
                mixed.at[rows, cols],
                logsum.at[j, s],
                j,
            )
        )
    forward_units(units, length, lambda block, part, j: (block + bias[j, part, :], True))


def self_backward_kernel(
    query, keys, values, grad, mixed, bias, logsum, gq, gk, gv, grad_bias, scores, slopes, probs, grads
):
    length = bias.shape[1]
    units = []
    for rows, cols, s, j in self_units(length):
        u = s * 2 + j
        units.append(
            (
                query[rows, cols],
                keys[rows, cols],
                values[rows, cols],
                grad[rows, cols],
                mixed[rows, cols],
                logsum.at[j, s],
                scores.at[u],
                slopes.at[u],
                probs.at[u],
                grads.at[u],
                (gq.at[rows, cols], gk.at[rows, cols], gv.at[rows, cols]),
                j,
            )
        )
    backward_units(units, length, lambda block, part, j: (block + bias[j, part, :], None))
    for j in range(2):
        for part in chunks(length):
            grad_bias[j, part, :] = grads[j, part, :].astype(F32) + grads[2 + j, part, :].astype(F32)


def last_tile(valid, size, part, block):
    if part.start < size - KEY_TILE:
        return None
    return part.start + lax.broadcasted_iota(jnp.int32, block.shape, 0) < valid


def cross_forward_kernel(lens, query, keys, values, mixed, logsum, scores, probs):
    valid = lens[pl.program_id(0)]
    for tiles in range(1, keys.shape[0] // KEY_TILE + 1):

        @pl.when((valid + KEY_TILE - 1) // KEY_TILE == tiles)
        def _():
            size = tiles * KEY_TILE

            def fix(block, part, which):
                keep = last_tile(valid, size, part, block)
                if keep is None:
                    return block, False
                return jnp.where(keep, block, NEGATIVE), True

            units = []
            for j in range(2):
                cols = slice(j * 128, (j + 1) * 128)
                units.append(
                    (
                        query[:, cols],
                        keys[:size, cols],
                        values[:size, cols],
                        scores.at[j],
                        probs.at[j],
                        mixed.at[:, cols],
                        logsum.at[j, 0],
                        None,
                    )
                )
            forward_units(units, size, fix)


def cross_backward_kernel(
    lens, query, keys, values, grad, mixed, logsum, gq, gk, gv, scores, slopes, probs, grads
):
    valid = lens[pl.program_id(0)]
    for tiles in range(1, keys.shape[0] // KEY_TILE + 1):

        @pl.when((valid + KEY_TILE - 1) // KEY_TILE == tiles)
        def _():
            size = tiles * KEY_TILE
            units = []
            for j in range(2):
                cols = slice(j * 128, (j + 1) * 128)
                units.append(
                    (
                        query[:, cols],
                        keys[:size, cols],
                        values[:size, cols],
                        grad[:, cols],
                        mixed[:, cols],
                        logsum.at[j, 0],
                        scores.at[j],
                        slopes.at[j],
                        probs.at[j],
                        grads.at[j],
                        (gq.at[:, cols], gk.at[:size, cols], gv.at[:size, cols]),
                        None,
                    )
                )
            backward_units(
                units,
                size,
                lambda block, part, which: (block, last_tile(valid, size, part, block)),
            )


def attend_scratch(units, keys, queries, backward):
    wide = pltpu.VMEM((units, keys, 2 * queries), F32)
    thin = pltpu.VMEM((units, keys, 2 * queries), BF)
    return [wide, wide, thin, thin] if backward else [wide, thin]


def pair_spec(rows, base=0):
    return pl.BlockSpec((rows, 256), lambda s, p: (s, base + p))


def both_spec(rows, base=0):
    return pl.BlockSpec((rows, 256), lambda p: (0, base + p))


def inward_kernel(held, me, n1, *rest):
    refs, (packed, weight, sem) = rest[: len(held.arrays)], rest[len(held.arrays) :]
    load("inward", held, refs, weight, me, sem)
    arrived(weight, sem)
    size = n1.shape[1]
    left = n1[...]
    for block in range(3):
        cols = slice(block * size, (block + 1) * size)
        packed[:, cols] = nn(left, flat(weight[..., cols])).astype(BF)


def outward_kernel(held, me, x, mixed, gains, *rest):
    refs, (after, n2, weight, sem) = rest[: len(held.arrays)], rest[len(held.arrays) :]
    load("outward", held, refs, weight, me, sem)
    arrived(weight, sem)
    values = x[...].astype(F32) + nn(mixed[...], flat(weight[...]))
    after[...] = values
    n2[...] = normed(values, gains[1:2, :]).astype(BF)


def memory_kernel(held_query, held_reader, me, lens, n2, encoded, *rest):
    k, both = len(held_query.arrays), len(held_query.arrays) + len(held_reader.arrays)
    refs_query, refs_reader = rest[:k], rest[k:both]
    asks, pairs, weight_query, weight_reader, sems = rest[both:]
    step = pl.program_id(0)
    tiles = pl.num_programs(0) // lens.shape[0]

    @pl.when(step == 0)
    def _():
        load("query", held_query, refs_query, weight_query, me, sems.at[0])
        load("reader", held_reader, refs_reader, weight_reader, me, sems.at[1])
        arrived(weight_query, sems.at[0])
        asks[...] = nn(n2[...], flat(weight_query[...])).astype(BF)
        arrived(weight_reader, sems.at[1])

    @pl.when(lax.rem(step, tiles) * encoded.shape[0] < lens[step // tiles])
    def _():
        size = encoded.shape[1]
        left = encoded[...]
        for block in range(2):
            cols = slice(block * size, (block + 1) * size)
            pairs[:, cols] = nn(left, flat(weight_reader[..., cols])).astype(BF)


def gelu_parts(v):
    phi = 0.5 * (1.0 + lax.erf(v * (0.5**0.5)))
    density = jnp.exp(-0.5 * v * v) * 0.3989422804014327
    return v * phi, phi + v * density


def widen_kernel(held_writer, held_expand, me, after_self, mixed, gains, kept, *rest):
    k, both = len(held_writer.arrays), len(held_writer.arrays) + len(held_expand.arrays)
    refs_writer, refs_expand = rest[:k], rest[k:both]
    outs = rest[both:]
    after_cross, n3, hidden, slope = outs[:4]
    grads, (weight_writer, weight_expand, shrink_grad, sems) = outs[4:-4], outs[-4:]
    load("writer", held_writer, refs_writer, weight_writer, me, sems.at[0])
    load("expand", held_expand, refs_expand, weight_expand, me, sems.at[1])
    arrived(weight_writer, sems.at[0])
    values = after_self[...] + nn(mixed[...], flat(weight_writer[...]))
    after_cross[...] = values
    n3[...] = normed(values, gains[2:3, :]).astype(BF)
    arrived(weight_expand, sems.at[1])
    size = n3.shape[1]

    for z in range(4):
        cols = slice(z * size, (z + 1) * size)
        before = nn(n3[...], flat(weight_expand[:, :, :, :, cols]))
        active, gate = gelu_parts(before)
        active = active.astype(BF)
        hidden[:, cols] = active
        slope[:, cols] = gate.astype(BF)
        grad = tn(active, kept[...]).astype(BF)
        shrink_grad[z] = grad.reshape(shrink_grad.shape[1:])

    store("shrink", shrink_grad, grads, 0, me, sems.at[2])
    arrived(shrink_grad, sems.at[2])


def narrow_kernel(
    held_shrink, held_expand, me, lens, after_cross, n3, hidden, slope, kept, gains, *rest
):
    k, both = len(held_shrink.arrays), len(held_shrink.arrays) + len(held_expand.arrays)
    refs_shrink, refs_expand = rest[:k], rest[k:both]
    outs = rest[both:]
    layer_out, grad_cross, gain_part = outs[:3]
    grads, (weight_shrink, weight_expand, expand_grad, grad_wide, sems) = outs[3:-5], outs[-5:]
    load("shrink", held_shrink, refs_shrink, weight_shrink, me, sems.at[0])
    load("expand", held_expand, refs_expand, weight_expand, me, sems.at[1])
    size = n3.shape[1]
    arrived(weight_shrink, sems.at[0])
    for z in range(4):
        cols = slice(z * size, (z + 1) * size)
        grad_wide[:, cols] = (
            slope[:, cols].astype(F32) * nt(kept[...], flat(weight_shrink[z]))
        ).astype(BF)
    turned = n3[...].T
    for z in range(4):
        cols = slice(z * size, (z + 1) * size)
        put_rows(expand_grad, nn(turned, grad_wide[:, cols]).astype(BF), cols)
    store("expand", expand_grad, grads, 0, me, sems.at[2])
    total = after_cross[...] + nn(hidden[...], flat(weight_shrink[...]))
    rows = total.shape[0] // lens.shape[0]
    for s in range(lens.shape[0]):
        part = slice(s * rows, (s + 1) * rows)
        keep = lax.broadcasted_iota(jnp.int32, (rows, 1), 0) < lens[s]
        layer_out[s] = jnp.where(keep, total[part, :], 0.0).astype(BF)
    arrived(weight_expand, sems.at[1])
    grad_norm = nt(grad_wide[...], flat(weight_expand[...]))
    back, gain = norm_back(after_cross[...], gains[2:3, :], grad_norm)
    grad_cross[...] = kept[...].astype(F32) + back
    gain_part[...] = gain
    arrived(expand_grad, sems.at[2])


def writer_back_kernel(held, me, grad_cross, mixed, *rest):
    k = len(held.arrays)
    refs, outs = rest[:k], rest[k:]
    grad_mixed, grads, (weight, grad_scratch, sems) = outs[0], outs[1:-3], outs[-3:]
    load("writer", held, refs, weight, me, sems.at[0])
    branch = grad_cross[...].astype(BF)
    put_rows(grad_scratch, tn(mixed[...], branch).astype(BF), slice(None))
    store("writer", grad_scratch, grads, 0, me, sems.at[1])
    arrived(weight, sems.at[0])
    grad_mixed[...] = nt(branch, flat(weight[...])).astype(BF)
    arrived(grad_scratch, sems.at[1])


def query_back_kernel(
    packed_mode,
    held_query,
    held_out,
    me,
    grad_asks,
    n2,
    after_self,
    grad_cross,
    mixed,
    gains,
    *rest,
):
    k, both = len(held_query.arrays), len(held_query.arrays) + len(held_out.arrays)
    refs_query, refs_out = rest[:k], rest[k:both]
    rest = rest[both:]
    grad_self, grad_mixed, gain_part = rest[:3]
    weight_query, weight_out, query_grad, out_grad, sems = rest[-5:]
    grads = rest[3:-5]
    load("query", held_query, refs_query, weight_query, me, sems.at[0])
    load("outward", held_out, refs_out, weight_out, me, sems.at[1])
    put_rows(query_grad, tn(n2[...], grad_asks[...]).astype(BF), slice(None))
    store("query", query_grad, grads if packed_mode else grads[:1], 0, me, sems.at[2])
    arrived(weight_query, sems.at[0])
    back, gain = norm_back(
        after_self[...], gains[1:2, :], nt(grad_asks[...], flat(weight_query[...]))
    )
    total = grad_cross[...] + back
    grad_self[...] = total
    gain_part[...] = gain
    branch = total.astype(BF)
    arrived(weight_out, sems.at[1])
    grad_mixed[...] = nt(branch, flat(weight_out[...])).astype(BF)
    put_rows(out_grad, tn(mixed[...], branch).astype(BF), slice(None))
    store("outward", out_grad, grads if packed_mode else grads[1:], 1, me, sems.at[3])
    arrived(query_grad, sems.at[2])
    arrived(out_grad, sems.at[3])


def inward_grad_kernel(me, n1, gq, gk, gv, *rest):
    grads, (scratch, sem) = rest[:-2], rest[-2:]
    size = n1.shape[1]
    turned = n1[...].T
    for block, grad in enumerate((gq, gk, gv)):
        cols = slice(block * size, (block + 1) * size)
        put_rows(scratch, nn(turned, grad[...]).astype(BF), cols)
    store("inward", scratch, grads, 0, me, sem)
    arrived(scratch, sem)


def inputs_grad_kernel(held, me, x, gq, gk, gv, grad_self, gains, *rest):
    k = len(held.arrays)
    refs, (out, gain_part, weight, sem) = rest[:k], rest[k:]
    load("inward", held, refs, weight, me, sem)
    arrived(weight, sem)
    size = x.shape[1]
    total = 0.0
    for block, grad in enumerate((gq, gk, gv)):
        cols = slice(block * size, (block + 1) * size)
        total = total + nt(grad[...], flat(weight[..., cols]))
    back, gain = norm_back(x[...].astype(F32), gains[0:1, :], total)
    out[...] = grad_self[...] + back
    gain_part[...] = gain


def reader_grad_kernel(me, lens, encoded, gk, gv, *rest):
    grads, (scratch, total, sem) = rest[:-3], rest[-3:]
    step = pl.program_id(0)
    size = encoded.shape[1]
    valid = lens[step]
    for tiles in range(1, encoded.shape[0] // KEY_TILE + 1):

        @pl.when((valid + KEY_TILE - 1) // KEY_TILE == tiles)
        def _():
            rows = tiles * KEY_TILE
            turned = encoded[:rows].T
            for block, grad in enumerate((gk, gv)):
                cols = slice(block * size, (block + 1) * size)
                before = jnp.where(step == 0, 0.0, total[:, cols])
                total[:, cols] = before + nn(turned, grad[:rows])

    @pl.when(step == pl.num_programs(0) - 1)
    def _():
        put_rows(scratch, total[...].astype(BF), slice(None))
        store("reader", scratch, grads, 0, me, sem)
        arrived(scratch, sem)


def encoded_grad_kernel(held, me, lens, gk, gv, *rest):
    refs, (out, weight, sem) = rest[: len(held.arrays)], rest[len(held.arrays) :]
    step = pl.program_id(0)
    steps = pl.num_programs(0) // lens.shape[0]
    height, size = gk.shape
    left = lens[step // steps] - lax.rem(step, steps) * height

    @pl.when(step == 0)
    def _():
        load("reader", held, refs, weight, me, sem)
        arrived(weight, sem)

    for tiles in range(1, height // KEY_TILE + 1):
        rows = tiles * KEY_TILE
        last = tiles == height // KEY_TILE
        fits = left > rows - KEY_TILE

        @pl.when(fits if last else jnp.logical_and(fits, left <= rows))
        def _():
            out[:rows] = nt(gk[:rows], flat(weight[..., :size])) + nt(
                gv[:rows], flat(weight[..., size:])
            )
            if rows < height:
                out[rows:] = jnp.zeros((height - rows, size), F32)

    @pl.when(left <= 0)
    def _():
        out[...] = jnp.zeros_like(out)


def table_kernel(count, buckets, grad_bias, out, hot):
    pairs, length = grad_bias.shape[:2]
    group = hot.shape[0]
    lane = lax.broadcasted_iota(jnp.int32, out.shape, 1)

    def one(step, total):
        for k in range(group):
            hot[k] = jnp.where(buckets[...] == step * group + k, 1.0, 0.0)
        rows = [[] for _ in range(group)]
        for h in range(2 * pairs):
            cols = slice((h % 2) * length, (h % 2 + 1) * length)
            sums = [jnp.zeros((8, length), F32) for _ in range(group)]
            for part in chunks(length):
                value = grad_bias[h // 2, part, cols]
                for k in range(group):
                    sums[k] = sums[k] + folded(hot[k, part] * value, jnp.sum)
            for k in range(group):
                rows[k].append(jnp.sum(sums[k], axis=0, keepdims=True))
        for k in range(group):
            value = jnp.sum(jnp.concatenate(rows[k], axis=0), axis=1, keepdims=True)
            total = total + jnp.where(lane == step * group + k, value, 0.0)
        return total

    out[...] = lax.fori_loop(0, count // group, one, jnp.zeros(out.shape, F32))


def shared_places(widths, piece, width):
    starts = [0]
    for w in widths:
        starts.append(starts[-1] + w // piece)
    return starts[:-1], starts[-1], starts[-1] + 1, starts[-1] + 1 + 3 * (width // piece)


def statistics_kernel(piece, *refs):
    grads, gains, table, rows, shared = refs[:7], refs[7:10], refs[10], refs[11], refs[12]
    width = gains[0].shape[1]
    starts, totals_at, gains_at, table_at = shared_places([g.shape[1] for g in grads], piece, width)
    rows[...] = jnp.zeros_like(rows)
    shared[...] = jnp.zeros_like(shared)
    lane = lax.broadcasted_iota(jnp.int32, (1, 128), 1)
    lane_piece = lax.broadcasted_iota(jnp.int32, (1, piece), 1)
    totals = jnp.zeros((1, piece), F32)
    for j, grad in enumerate(grads):
        square = grad[...] * grad[...]
        count, wide = square.shape
        sums = jnp.sum(square, axis=1, keepdims=True)
        rows[:count, :] += jnp.where(lane == j, sums, 0.0)
        columns = jnp.sum(square, axis=0, keepdims=True)
        for p in range(wide // piece):
            at = starts[j] + p
            shared[at : at + 1, :] = columns[:, p * piece : (p + 1) * piece]
        totals = totals + jnp.where(lane_piece == j, jnp.sum(sums, axis=0, keepdims=True), 0.0)
    shared[totals_at : totals_at + 1, :] = totals
    for k in range(3):
        for p in range(width // piece):
            at = gains_at + k * (width // piece) + p
            shared[at : at + 1, :] = gains[k][:, p * piece : (p + 1) * piece]
    keep = min(piece, table.shape[1])
    shared[table_at : table_at + table.shape[0], :keep] = table[:, :keep]


def steps_kernel(wide, narrow, *refs):
    grads, rows, shared = refs[:7], refs[7], refs[8]
    outs = refs[9:]
    piece = shared.shape[1]
    starts, totals_at, _, _ = shared_places([g.shape[1] for g in grads], piece, piece)
    turned = rows[...].T
    for j, grad in enumerate(grads):
        step, row_out, col_out = outs[3 * j : 3 * j + 3]
        count, width = grad.shape
        full_rows, full_cols = count * wide, width * narrow
        row = rows[:count, j : j + 1] / full_cols + TINY
        mean = shared[totals_at : totals_at + 1, j : j + 1] / (full_rows * full_cols) + TINY
        cols = []
        for p in range(width // piece):
            at = starts[j] + p
            part = slice(p * piece, (p + 1) * piece)
            col = shared[at : at + 1, :] / full_rows + TINY
            step[:, part] = grad[:, part] * lax.rsqrt(row * col / mean)
            cols.append(col)
        row_out[...] = (turned[j : j + 1, :count] / full_cols + TINY).reshape(count)
        col = cols[0] if len(cols) == 1 else jnp.concatenate(cols, axis=1)
        col_out[...] = col.reshape(width)


def tie(value, after):
    after = tuple(after)
    return lax.optimization_barrier((value,) + after)[0] if after else value


def join(gathers, arrays=()):
    keys = [(g, key) for g in gathers for key in g.live]
    flat_values, tree = jax.tree.flatten(([g.live[key] for g, key in keys], list(arrays)))
    values, arrays = jax.tree.unflatten(tree, lax.optimization_barrier(tuple(flat_values)))
    for (g, key), value in zip(keys, values):
        g.live[key] = value
    return arrays


class Hyper:
    MASKS = {"y": 1, "c": 2, "x": 4, "xy": 5, "z1": 8, "z2": 16, "z3": 24}

    def __init__(self):
        wide = lax.axis_index("wide")
        self.z, self.x, self.c = wide // 4, (wide // 2) % 2, wide % 2
        self.y = lax.axis_index("narrow")
        self.me = jnp.stack((self.z, self.x, self.c, self.y)).astype(jnp.int32)

    def swap(self, value, bit, after=()):
        mask = self.MASKS[bit]
        return lax.ppermute(tie(value, after), BOTH, [(i, i ^ mask) for i in range(32)])


class Gather:
    def __init__(self, hyper, shards, plan, width):
        self.hyper, self.plan = hyper, plan
        self.live = {"own": jnp.stack([cut(name, shards[name], width)[p] for name, p in plan])}

    def z(self):
        own = self.live["own"]
        self.live["others"] = [self.hyper.swap(own, bit) for bit in ("z1", "z2", "z3")]

    def z1(self):
        self.live["other"] = self.hyper.swap(self.live["own"], "z1")

    def z2(self):
        h = self.hyper
        own, other = self.live.pop("own"), self.live.pop("other")
        pair = jnp.where(h.z % 2 == 0, jnp.stack((own, other)), jnp.stack((other, own)))
        self.live["own"], self.live["other"] = pair, h.swap(pair, "z2")

    def plane(self):
        h = self.hyper
        own = self.live.pop("own")
        if "others" in self.live:
            one, two, three = self.live.pop("others")
            even = h.z % 2 == 0
            own = jnp.where(even, jnp.stack((own, one)), jnp.stack((one, own)))
            other = jnp.where(even, jnp.stack((two, three)), jnp.stack((three, two)))
        else:
            other = self.live.pop("other")
        quad = jnp.where(
            h.z // 2 == 0, jnp.concatenate((own, other)), jnp.concatenate((other, own))
        )
        self.live["quads"] = [quad] + [h.swap(quad, bit) for bit in ("x", "y", "xy")]

    def core_own(self):
        self.live["first"] = self.hyper.swap(self.live["quads"][0], "c")

    def core(self):
        self.live["cores"] = [self.live.pop("first")] + [
            self.hyper.swap(quad, "c") for quad in self.live["quads"][1:]
        ]

    def held(self, name):
        arrays = [a for two in zip(self.live["quads"], self.live["cores"]) for a in two]
        return Held(arrays, self.plan.index((name, 0)))


def fold_kernel(counts, joint, names, me, *refs):
    na, nb, nj = counts
    first, second, both, outs = refs[:na], refs[na : na + nb], refs[na + nb : na + nb + nj], refs[na + nb + nj :]
    pa = first[0].shape[3]

    def add(parts, part):
        return sum([r[...].astype(F32) for r in parts] + [r[:, :, :, part].astype(F32) for r in both])

    one = add(first, slice(0, pa))
    two = add(second, slice(pa, None))
    if names:
        pieces = [one[0, 0, 0, p] for p in range(one.shape[3])]
        pieces += [two[0, 0, 0, p] for p in range(two.shape[3])]
        for out, (name, start) in zip(outs, names):
            for p in range(COUNTS[name]):
                piece = pieces[start + p]
                if name == "shrink":
                    out[p * piece.shape[0] : (p + 1) * piece.shape[0], :] = piece
                else:
                    out[:, p * piece.shape[1] : (p + 1) * piece.shape[1]] = piece
    elif joint:
        outs[0][:, :, :, :pa] = one.astype(outs[0].dtype)
        outs[0][:, :, :, pa:] = two.astype(outs[0].dtype)
    else:
        outs[0][...] = one.astype(outs[0].dtype)
        outs[1][...] = two.astype(outs[1].dtype)


class HalvedScatter:
    def __init__(self, hyper, first, second, name):
        self.hyper, self.halves, self.name = hyper, (first, second), name
        self.parts = [[], []]
        self.joint = []
        self.sizes = [half[0].shape[3] for half in (first, second)]
        self.block = first[0].shape[4:]

    def core(self, half, after=()):
        keep, send = self.halves[half]
        recv = self.hyper.swap(send, "c", after)
        self.parts[half] = [keep, recv]
        return [recv]

    def fold(self, picks, out_dims, joint, after, step):
        ins = []
        for half in range(2):
            p = self.sizes[half]
            for array, (dims, index) in zip(self.parts[half], picks[half]):
                spec = pl.BlockSpec(
                    tuple(dims) + (p,) + self.block,
                    lambda i, me, index=index: tuple(index(me)) + (0, 0, 0),
                )
                ins.append((array, spec))
        whole = sum(self.sizes)
        for array, index in zip(self.joint, picks[2]):
            spec = pl.BlockSpec(
                (1, 1, 1, whole) + self.block,
                lambda i, me, index=index: (index(me), 0, 0, 0, 0, 0),
            )
            ins.append((array, spec))
        outs = []
        rows, cols = self.block
        for dims, kind in out_dims:
            if isinstance(dims, str):
                count = COUNTS[dims]
                full = (count * rows, cols) if dims == "shrink" else (rows, count * cols)
                outs.append((shape(full, F32), pl.BlockSpec(full, lambda i, me: (0, 0))))
                continue
            p = whole if joint else self.sizes[len(outs)]
            full = tuple(dims) + (p,) + self.block
            outs.append((shape(full, kind), pl.BlockSpec(full, lambda i, me: (0,) * 6)))
        counts = (len(self.parts[0]), len(self.parts[1]), len(self.joint))
        names = out_dims if step == "last" else None
        self.sent = launch(
            functools.partial(fold_kernel, counts, joint, names),
            ins,
            outs,
            grid=(1,),
            gflop=1.0,
            name=f"{self.name}_{step}",
            after=after,
            prefetch=(self.hyper.me,),
        )
        return self.sent

    def p1(self, after=()):
        a = [((4, 2, 1), lambda me: (0, 0, 1 - me[3]))] * 2
        b = [((4, 1, 2), lambda me: (0, 1 - me[1], 0))] * 2
        sent = self.fold((a, b, ()), (((4, 2, 1), BF), ((4, 1, 2), BF)), False, after, "p1")
        recv = [self.hyper.swap(value, bit) for value, bit in zip(sent, "yx")]
        for half in range(2):
            self.parts[half].append(recv[half])
        return recv

    def p2(self, after=()):
        four = (4, 1, 1)
        a = [(four, lambda me: (0, 1 - me[1], me[3]))] * 2
        a += [(four, lambda me: (0, 1 - me[1], 0))]
        b = [(four, lambda me: (0, me[1], 1 - me[3]))] * 2
        b += [(four, lambda me: (0, 0, 1 - me[3]))]
        sent = self.fold((a, b, ()), ((four, BF), (four, BF)), False, after, "p2")
        recv = [self.hyper.swap(value, bit) for value, bit in zip(sent, "xy")]
        for half in range(2):
            self.parts[half].append(recv[half])
        return recv

    def own(self, count, place):
        dims = (count, 1, 1)
        a = [(dims, lambda me: (place(me), me[1], me[3]))] * 2
        a += [(dims, lambda me: (place(me), me[1], 0)), (dims, lambda me: (place(me), 0, 0))]
        b = [(dims, lambda me: (place(me), me[1], me[3]))] * 2
        b += [(dims, lambda me: (place(me), 0, me[3])), (dims, lambda me: (place(me), 0, 0))]
        return a, b

    def z2(self, after=()):
        a, b = self.own(2, lambda me: 1 - me[0] // 2)
        (sent,) = self.fold((a, b, ()), (((2, 1, 1), BF),), True, after, "z2")
        recv = self.hyper.swap(sent, "z2")
        self.joint.append(recv)
        return [recv]

    def z1(self, after=()):
        a, b = self.own(1, lambda me: (me[0] // 2) * 2 + 1 - lax.rem(me[0], 2))
        j = [lambda me: 1 - lax.rem(me[0], 2)]
        (sent,) = self.fold((a, b, j), (((1, 1, 1), BF),), True, after, "z1")
        recv = self.hyper.swap(sent, "z1")
        self.joint.append(recv)
        return [recv]

    def last(self, weights, after=()):
        a, b = self.own(1, lambda me: me[0])
        j = [lambda me: lax.rem(me[0], 2), lambda me: 0]
        return self.fold((a, b, j), weights, True, after, "last")


def plane_kernel(me, *refs):
    groups, outs = refs[:-4], refs[-4:]
    for k, out in enumerate(outs):
        x, y = me[1] ^ (k & 1), me[3] ^ (k >> 1)
        at = 0
        for keep, recv in zip(groups[::2], groups[1::2]):
            total = keep[:, x, y].astype(F32) + recv[:, x, y].astype(F32)
            out[:, at : at + total.shape[1]] = total.astype(out.dtype)
            at += total.shape[1]


def line_kernel(me, own, one, two, three, *outs):
    for k, out in enumerate(outs):
        z = me[0] ^ k
        total = own[z] + one[z].astype(F32) + two[z].astype(F32) + three[z].astype(F32)
        out[...] = total.astype(out.dtype)


def last_kernel(names, own, one, two, three, *outs):
    total = own[...] + one[...].astype(F32) + two[...].astype(F32) + three[...].astype(F32)
    at = 0
    for out, name in zip(outs, names):
        for p in range(COUNTS[name]):
            piece = total[at + p]
            if name == "shrink":
                out[p * piece.shape[0] : (p + 1) * piece.shape[0], :] = piece
            else:
                out[:, p * piece.shape[1] : (p + 1) * piece.shape[1]] = piece
        at += COUNTS[name]


class Scatter:
    def __init__(self, hyper, name, weights):
        self.hyper, self.name, self.weights = hyper, name, weights
        self.groups = []

    def core(self, keep, send):
        self.groups.append((keep, self.hyper.swap(send, "c")))

    def plane(self, after=()):
        count = sum(keep.shape[3] for keep, _ in self.groups)
        block = self.groups[0][0].shape[4:]
        dims = (4, count) + block
        self.own, *sent = launch(
            plane_kernel,
            [(self.hyper.me, SM)] + [(a, VM) for group in self.groups for a in group],
            [(shape(dims, F32), VM)] + [(shape(dims, BF), VM)] * 3,
            name=self.name + "_plane",
            after=after,
        )
        self.sent = sent
        self.got = [self.hyper.swap(a, bit) for a, bit in zip(sent, ("x", "y", "xy"))]

    def line(self, after=()):
        dims = self.own.shape[1:]
        self.own, *sent = launch(
            line_kernel,
            [(self.hyper.me, SM), (self.own, VM)] + [(a, VM) for a in self.got],
            [(shape(dims, F32), VM)] + [(shape(dims, BF), VM)] * 3,
            name=self.name + "_line",
            after=after,
        )
        self.sent = sent
        self.got = [self.hyper.swap(a, bit) for a, bit in zip(sent, ("z1", "z2", "z3"))]

    def last(self, after=()):
        rows, cols = self.own.shape[1:]
        outs = []
        for name in self.weights:
            count = COUNTS[name]
            full = (count * rows, cols) if name == "shrink" else (rows, count * cols)
            outs.append((shape(full, F32), VM))
        totals = launch(
            functools.partial(last_kernel, self.weights),
            [(self.own, VM)] + [(a, VM) for a in self.got],
            outs,
            name=self.name + "_last",
            after=after,
        )
        self.sent = totals
        return dict(zip(self.weights, totals))


def cut(name, shard, width):
    count = COUNTS[name]
    if name == "shrink":
        return shard.reshape(count, shard.shape[0] // count, shard.shape[1])
    rows, cols = shard.shape
    return jnp.transpose(shard.reshape(rows, count, cols // count), (1, 0, 2))


def whole_shape(name, width):
    if name == "shrink":
        return (4, 2, 2, 4, width // 16, width)
    return (4, 2, 2, width // 16, width * COUNTS[name])


def local(
    inputs,
    encoded,
    target_lengths,
    memory_lengths,
    buckets,
    cotangent,
    self_inward,
    self_outward,
    cross_query,
    cross_reader,
    cross_writer,
    expand_weight,
    shrink_weight,
    norm_gains,
    bias_table,
):
    wide_count = lax.axis_size("wide")
    narrow_count = lax.axis_size("narrow")
    fast = (wide_count, narrow_count) == (16, 2)
    seqs, length, width = inputs.shape
    memory_size = encoded.shape[1]
    rows, mem_rows = seqs * length, seqs * memory_size
    wide_hidden = expand_weight.shape[1] * narrow_count
    shards = dict(
        zip(
            NAMES,
            (
                self_inward,
                self_outward,
                cross_query,
                cross_reader,
                cross_writer,
                expand_weight,
                shrink_weight,
            ),
        )
    )
    hyper = Hyper() if fast else None
    me = hyper.me if fast else jnp.zeros((4,), jnp.int32)
    none = []

    def grad_outs(name, count):
        if fast:
            block = shape((4, 2, 2, count, width // 16, width // 2), BF)
            return [(block, HB), (block, HB)]
        return [(shape(whole_shape(name, width), BF), HB)]

    dma = pltpu.SemaphoreType.DMA
    x_rows = inputs.reshape(rows, width)
    mem_flat = encoded.reshape(mem_rows, width)
    heads = HEADS
    pairs_count = heads // 2
    turned = buckets.T
    table = jnp.pad(bias_table.T, ((0, 0), (0, 128 - bias_table.shape[0])))

    def weights(*names):
        return [entry for name in names for entry in held[name].ins()]

    held = {}
    if fast:
        ga, gb, gc, gd = [Gather(hyper, shards, plan, width) for plan in GATHERS]
        ga.z()
    else:
        for name in NAMES:
            full = lax.all_gather(shards[name], "narrow", axis=1, tiled=True)
            full = lax.all_gather(full, "wide", axis=0, tiled=True)
            full = full.reshape(whole_shape(name, width))
            held[name] = Held((full,))

    n1, kept, bias = launch(
        prepare_kernel,
        [
            (target_lengths, SM),
            (inputs, VM),
            (cotangent, VM),
            (norm_gains, VM),
            (turned, VM),
            (table, VM),
        ],
        [
            (shape((rows, width), BF), VM),
            (shape((rows, width), BF), VM),
            (shape((pairs_count, length, 2 * length), F32), VM),
        ],
        name="prepare",
    )

    if fast:
        n1, kept, bias = join((ga,), (n1, kept, bias))
        ga.plane()
        ga.core_own()
        gb.z1()
        gb.z2()
        join((ga, gb))
        ga.core()
        gb.plane()
        gc.z1()
        for name in ("inward", "outward"):
            held[name] = ga.held(name)

    (packed,) = launch(
        functools.partial(inward_kernel, held["inward"]),
        [(me, SM), (n1, VM)] + weights("inward"),
        [(shape((rows, 3 * width), BF), VM)],
        [weight_scratch("inward", width), dma],
        gflop=2.0,
        name="inward",
    )

    bias_spec = pl.BlockSpec((2, length, 2 * length), lambda p: (p, 0, 0))
    log_both = pl.BlockSpec((2, seqs, 1, 2 * length), lambda p: (p, 0, 0, 0))
    log_spec = pl.BlockSpec((2, 1, 1, 2 * length), lambda s, p: (p, s, 0, 0))
    log_shape = shape((pairs_count, seqs, 1, 2 * length), F32)
    blocks = pairs_count // 2
    self_mixed, self_log = launch(
        self_forward_kernel,
        [
            (packed, both_spec(rows)),
            (packed, both_spec(rows, blocks)),
            (packed, both_spec(rows, 2 * blocks)),
            (bias, bias_spec),
        ],
        [(shape((rows, width), BF), both_spec(rows)), (log_shape, log_both)],
        attend_scratch(4, length, length, False),
        grid=(blocks,),
        gflop=5.0,
        name="self_forward",
    )

    if fast:
        self_mixed, self_log = join((gc,), (self_mixed, self_log))
        gc.z2()

    after_self, n2 = launch(
        functools.partial(outward_kernel, held["outward"]),
        [(me, SM), (x_rows, VM), (self_mixed, VM), (norm_gains, VM)] + weights("outward"),
        [(shape((rows, width), F32), VM), (shape((rows, width), BF), VM)],
        [weight_scratch("outward", width), dma],
        gflop=2.0,
        name="outward",
    )

    if fast:
        after_self, n2 = join((gb, gc), (after_self, n2))
        gb.core_own()
        gb.core()
        gc.plane()
        gd.z1()
        for name in ("query", "writer", "reader"):
            held[name] = gb.held(name)

    tile_spec = pl.BlockSpec((KEY_TILE, width), lambda i: (i, 0))
    asks, pairs = launch(
        functools.partial(memory_kernel, held["query"], held["reader"]),
        [(me, SM), (memory_lengths, SM), (n2, VM), (mem_flat, pl.BlockSpec((2 * KEY_TILE, width), lambda i: (i, 0)))]
        + weights("query", "reader"),
        [
            (shape((rows, width), BF), pl.BlockSpec((rows, width), lambda i: (0, 0))),
            (
                shape((mem_rows, 2 * width), BF),
                pl.BlockSpec((2 * KEY_TILE, 2 * width), lambda i: (i, 0)),
            ),
        ],
        [weight_scratch("query", width), weight_scratch("reader", width), dma((2,))],
        grid=(mem_rows // (2 * KEY_TILE),),
        gflop=6.0,
        name="memory",
    )

    if fast:
        asks, pairs = join((gd,), (asks, pairs))
        gc.core_own()
        gd.z2()

    cross_mixed, cross_log = launch(
        cross_forward_kernel,
        [
            (memory_lengths, SM),
            (asks, pair_spec(length)),
            (pairs, pair_spec(memory_size)),
            (pairs, pair_spec(memory_size, blocks)),
        ],
        [(shape((rows, width), BF), pair_spec(length)), (log_shape, log_spec)],
        attend_scratch(2, memory_size, length, False),
        grid=(seqs, blocks),
        gflop=10.0,
        name="cross_forward",
    )

    if fast:
        cross_mixed, cross_log = join((gc, gd), (cross_mixed, cross_log))
        gc.core()
        held["expand"] = gc.held("expand")
        gd.plane()
        gd.core_own()

    after_cross, n3, hidden, slope, *shrink_parts = launch(
        functools.partial(widen_kernel, held["writer"], held["expand"]),
        [(me, SM), (after_self, VM), (cross_mixed, VM), (norm_gains, VM), (kept, VM)]
        + weights("writer", "expand"),
        [
            (shape((rows, width), F32), VM),
            (shape((rows, width), BF), VM),
            (shape((rows, wide_hidden), BF), VM),
            (shape((rows, wide_hidden), BF), VM),
        ]
        + grad_outs("shrink", 4),
        [
            weight_scratch("writer", width),
            weight_scratch("expand", width),
            weight_scratch("shrink", width),
            dma((3,)),
        ],
        gflop=10.0,
        name="widen",
    )

    if fast:
        after_cross, n3, hidden, slope = join((gd,), (after_cross, n3, hidden, slope))
        gd.core()
        held["shrink"] = gd.held("shrink")

    layer_out, grad_cross, gain_third, *expand_parts = launch(
        functools.partial(narrow_kernel, held["shrink"], held["expand"]),
        [
            (me, SM),
            (target_lengths, SM),
            (after_cross, VM),
            (n3, VM),
            (hidden, VM),
            (slope, VM),
            (kept, VM),
            (norm_gains, VM),
        ]
        + weights("shrink", "expand"),
        [
            (shape((seqs, length, width), BF), VM),
            (shape((rows, width), F32), VM),
            (shape((1, width), F32), VM),
        ]
        + grad_outs("expand", 4),
        [
            weight_scratch("shrink", width),
            weight_scratch("expand", width),
            weight_scratch("expand", width),
            pltpu.VMEM((rows, wide_hidden), BF),
            dma((3,)),
        ],
        gflop=14.0,
        name="narrow",
    )

    if fast:
        sf = HalvedScatter(hyper, shrink_parts, expand_parts, "ffn")
        sf.core(0)
        sf.core(1)

    grad_mixed, *writer_parts = launch(
        functools.partial(writer_back_kernel, held["writer"]),
        [(me, SM), (grad_cross, VM), (cross_mixed, VM)] + weights("writer"),
        [(shape((rows, width), BF), VM)] + grad_outs("writer", 1),
        [weight_scratch("writer", width), weight_scratch("writer", width), dma((2,))],
        gflop=2.0,
        name="writer_back",
    )

    if fast:
        sf.p1([grad_mixed])

    grad_asks, grad_mem_keys, grad_mem_values = launch(
        cross_backward_kernel,
        [
            (memory_lengths, SM),
            (asks, pair_spec(length)),
            (pairs, pair_spec(memory_size)),
            (pairs, pair_spec(memory_size, blocks)),
            (grad_mixed, pair_spec(length)),
            (cross_mixed, pair_spec(length)),
            (cross_log, log_spec),
        ],
        [
            (shape((rows, width), BF), pair_spec(length)),
            (shape((mem_rows, width), BF), pair_spec(memory_size)),
            (shape((mem_rows, width), BF), pair_spec(memory_size)),
        ],
        attend_scratch(2, memory_size, length, True),
        grid=(seqs, blocks),
        gflop=20.0,
        name="cross_backward",
        after=sf.sent if fast else none,
    )

    whole_spec = pl.BlockSpec((memory_size, width), lambda i: (i, 0))
    reader_parts = launch(
        reader_grad_kernel,
        [
            (me, SM),
            (memory_lengths, SM),
            (mem_flat, whole_spec),
            (grad_mem_keys, whole_spec),
            (grad_mem_values, whole_spec),
        ],
        grad_outs("reader", 2),
        [weight_scratch("reader", width), pltpu.VMEM((width, 2 * width), F32), dma],
        grid=(seqs,),
        gflop=5.0,
        name="reader_grad",
    )

    if fast:
        sf.p2([reader_parts[0]])
        sm = Scatter(hyper, "middle", ("writer", "reader", "query", "outward"))
        sm.core(*writer_parts)
        sm.core(*reader_parts)

    grad_self, grad_mixed, gain_second, *rest_parts = launch(
        functools.partial(query_back_kernel, fast, held["query"], held["outward"]),
        [
            (me, SM),
            (grad_asks, VM),
            (n2, VM),
            (after_self, VM),
            (grad_cross, VM),
            (self_mixed, VM),
            (norm_gains, VM),
        ]
        + weights("query", "outward"),
        [
            (shape((rows, width), F32), VM),
            (shape((rows, width), BF), VM),
            (shape((1, width), F32), VM),
        ]
        + (grad_outs("query", 2) if fast else grad_outs("query", 1) + grad_outs("outward", 1)),
        [
            weight_scratch("query", width),
            weight_scratch("outward", width),
            weight_scratch("query", width),
            weight_scratch("outward", width),
            dma((4,)),
        ],
        gflop=4.0,
        name="query_back",
        after=sf.sent if fast else none,
    )

    if fast:
        sm.core(*rest_parts)
        sf.z2([grad_mixed])
        sm.plane(sf.sent)

    grad_query, grad_keys, grad_values, grad_bias = launch(
        self_backward_kernel,
        [
            (packed, both_spec(rows)),
            (packed, both_spec(rows, blocks)),
            (packed, both_spec(rows, 2 * blocks)),
            (grad_mixed, both_spec(rows)),
            (self_mixed, both_spec(rows)),
            (bias, bias_spec),
            (self_log, log_both),
        ],
        [(shape((rows, width), BF), both_spec(rows))] * 3
        + [(shape((pairs_count, length, 2 * length), F32), bias_spec)],
        attend_scratch(4, length, length, True),
        grid=(blocks,),
        gflop=6.0,
        name="self_backward",
        after=sm.sent if fast else none,
    )

    inward_parts = launch(
        inward_grad_kernel,
        [(me, SM), (n1, VM), (grad_query, VM), (grad_keys, VM), (grad_values, VM)],
        grad_outs("inward", 3),
        [weight_scratch("inward", width), dma],
        gflop=2.0,
        name="inward_grad",
    )

    if fast:
        si = Scatter(hyper, "inward", ("inward",))
        si.core(*inward_parts)
        sf.z1([inward_parts[0]])

    inputs_grad, gain_first = launch(
        functools.partial(inputs_grad_kernel, held["inward"]),
        [
            (me, SM),
            (x_rows, VM),
            (grad_query, VM),
            (grad_keys, VM),
            (grad_values, VM),
            (grad_self, VM),
            (norm_gains, VM),
        ]
        + weights("inward"),
        [(shape((rows, width), F32), VM), (shape((1, width), F32), VM)],
        [weight_scratch("inward", width), dma],
        gflop=2.0,
        name="inputs_grad",
        after=sf.sent if fast else none,
    )

    if fast:
        si.plane([inputs_grad])
        sm.line(si.sent)
        sums = dict(zip(("shrink", "expand"), sf.last((("shrink", 0), ("expand", 4)), sm.sent)))

    double_spec = pl.BlockSpec((2 * KEY_TILE, width), lambda i: (i, 0))
    (encoded_grad,) = launch(
        functools.partial(encoded_grad_kernel, held["reader"]),
        [(me, SM), (memory_lengths, SM), (grad_mem_keys, double_spec), (grad_mem_values, double_spec)]
        + weights("reader"),
        [(shape((mem_rows, width), F32), double_spec)],
        [weight_scratch("reader", width), dma],
        grid=(mem_rows // (2 * KEY_TILE),),
        gflop=5.0,
        name="encoded_grad",
        after=sf.sent if fast else none,
    )

    if fast:
        si.line([encoded_grad])

    (table_part,) = launch(
        functools.partial(table_kernel, bias_table.shape[0]),
        [(turned, VM), (grad_bias, VM)],
        [(shape((heads, 128), F32), VM)],
        [pltpu.VMEM((4, length, length), F32)],
        gflop=6.0,
        name="table",
        after=si.sent if fast else none,
    )

    if fast:
        sums.update(sm.last([table_part]))
        sums.update(si.last(sm.sent))
    else:
        sums = {}
        parts = {
            "shrink": shrink_parts[0],
            "expand": expand_parts[0],
            "writer": writer_parts[0],
            "reader": reader_parts[0],
            "query": rest_parts[0],
            "outward": rest_parts[1],
            "inward": inward_parts[0],
        }
        for name in NAMES:
            full = parts[name].reshape(-1, parts[name].shape[-1]).astype(F32)
            full = lax.psum_scatter(full, "wide", scatter_dimension=0, tiled=True)
            sums[name] = lax.psum_scatter(full, "narrow", scatter_dimension=1, tiled=True)

    grads = [sums[name] for name in NAMES]
    tallest = max(g.shape[0] for g in grads)
    piece = width // narrow_count
    _, totals_at, gains_at, table_at = shared_places([g.shape[1] for g in grads], piece, width)
    row_sums, shared = launch(
        functools.partial(statistics_kernel, piece),
        [(g, VM) for g in grads]
        + [(gain_first, VM), (gain_second, VM), (gain_third, VM), (table_part, VM)],
        [(shape((tallest, 128), F32), VM), (shape((-(-(table_at + heads) // 8) * 8, piece), F32), VM)],
        name="statistics",
    )
    add_y = lax.broadcasted_iota(jnp.int32, shared.shape, 0) >= totals_at
    if fast:
        other = hyper.swap(row_sums, "y")
        shared = shared + jnp.where(add_y, hyper.swap(shared, "y"), 0.0)
        row_sums = row_sums + other
        shared = tie(shared, [other])
        for bit in ("c", "x", "z1", "z2"):
            shared = shared + hyper.swap(shared, bit)
    else:
        row_sums = lax.psum(row_sums, "narrow")
        shared = lax.psum(jnp.where(add_y, lax.psum(shared, "narrow"), shared), "wide")

    step_outs = []
    for g in grads:
        step_outs.append((shape(g.shape, F32), VM))
        step_outs.append((shape((g.shape[0],), F32), VM))
        step_outs.append((shape((g.shape[1],), F32), VM))
    made = launch(
        functools.partial(steps_kernel, wide_count, narrow_count),
        [(g, VM) for g in grads] + [(row_sums, VM), (shared, VM)],
        step_outs,
        name="steps",
    )
    results = []
    for j, grad in enumerate(grads):
        step, row_stat, col_stat = made[3 * j : 3 * j + 3]
        results.extend([grad, step, row_stat, col_stat])
    gains_grad = shared[gains_at:table_at].reshape(3, width)
    table_grad = shared[table_at : table_at + heads, : bias_table.shape[0]].T
    return (
        (
            layer_out,
            inputs_grad.reshape(inputs.shape),
            encoded_grad.reshape(encoded.shape),
        )
        + tuple(results)
        + (gains_grad, table_grad)
    )


def solution(mesh):
    tokens = P(BOTH, None, None)
    weight = P("wide", "narrow")
    per_weight = (weight, weight, P("wide"), P("narrow"))
    return jax.shard_map(
        local,
        mesh=mesh,
        in_specs=(tokens, tokens, P(BOTH), P(BOTH), P(), tokens) + (weight,) * 7 + (P(), P()),
        out_specs=(tokens, tokens, tokens) + per_weight * 7 + (P(), P()),
        check_vma=False,
    )
```

```python
import functools

import jax
import jax.numpy as jnp
from jax import lax
from jax.experimental import pallas as pl
from jax.experimental.pallas import tpu as pltpu
from jax.sharding import PartitionSpec as P

HEADS = 12
DH = 64
EPS = 1e-06
TINY = 1e-30
NEGATIVE = -1e30
SCALE = DH ** (-0.5)

BF = jnp.bfloat16
F32 = jnp.float32
BOTH = ("wide", "narrow")
VMEM_LIMIT = 63 * 1024 * 1024
KEY_TILE = 256

COUNTS = {
    "inward": 3,
    "outward": 1,
    "query": 1,
    "reader": 2,
    "writer": 1,
    "expand": 4,
    "shrink": 4,
}
NAMES = ("inward", "outward", "query", "reader", "writer", "expand", "shrink")
GATHERS = (
    (("inward", 0), ("inward", 1), ("inward", 2), ("outward", 0)),
    (("query", 0), ("writer", 0), ("reader", 0), ("reader", 1)),
    (("expand", 0), ("expand", 1), ("expand", 2), ("expand", 3)),
    (("shrink", 0), ("shrink", 1), ("shrink", 2), ("shrink", 3)),
)


def nn(left, right):
    return lax.dot_general(left, right, (((1,), (0,)), ((), ())), preferred_element_type=F32)


def nt(left, right):
    return lax.dot_general(left, right, (((1,), (1,)), ((), ())), preferred_element_type=F32)


def tn(left, right):
    return lax.dot_general(left, right, (((0,), (0,)), ((), ())), preferred_element_type=F32)


VM = pl.BlockSpec(memory_space=pltpu.VMEM)
SM = pl.BlockSpec(memory_space=pltpu.SMEM)
HB = pl.BlockSpec(memory_space=pl.ANY)


def launch(
    body, ins, outs, scratch=(), grid=None, alias=None, gflop=1.0, name=None, after=(), prefetch=()
):
    ahead, count, extra = len(prefetch), len(ins), len(after)

    def trimmed(*refs):
        body(*refs[: ahead + count], *refs[ahead + count + extra :])

    params = dict(
        out_shape=[o for o, _ in outs],
        input_output_aliases={ahead + k: v for k, v in (alias or {}).items()},
        compiler_params=pltpu.CompilerParams(vmem_limit_bytes=VMEM_LIMIT),
        cost_estimate=pl.CostEstimate(
            flops=int(gflop * 1e10), bytes_accessed=1 << 22, transcendentals=0
        ),
        name=name,
    )
    specs = dict(
        grid=grid if grid is not None else (),
        in_specs=[s for _, s in ins] + [HB] * extra,
        out_specs=[s for _, s in outs],
        scratch_shapes=list(scratch),
    )
    if ahead:
        specs = dict(grid_spec=pltpu.PrefetchScalarGridSpec(num_scalar_prefetch=ahead, **specs))
    return pl.pallas_call(trimmed, **params, **specs)(*prefetch, *[a for a, _ in ins], *after)


def shape(dims, dtype):
    return jax.ShapeDtypeStruct(tuple(dims), dtype)


def weight_scratch(name, width):
    if name == "shrink":
        return pltpu.VMEM((4, 2, 2, 4, width // 16, width), BF)
    return pltpu.VMEM((4, 2, 2, width // 16, width * COUNTS[name]), BF)


class Held:
    def __init__(self, arrays, start=0):
        self.arrays, self.start = list(arrays), start

    def ins(self):
        return [(a, HB) for a in self.arrays]


def load(name, held, refs, scratch, me, sem):
    if len(refs) == 1 and refs[0].shape == scratch.shape:
        pltpu.make_async_copy(refs[0], scratch, sem).start()
        return
    count = COUNTS[name]
    piece = refs[0].shape[-1]

    def columns(y, p):
        if name == "shrink":
            return pl.ds(pl.multiple_of(y * piece, 128), piece)
        return pl.ds(pl.multiple_of((y * count + p) * piece, 128), piece)

    for p in range(count):
        if len(refs) == 1:
            for y in range(2):
                src = refs[0].at[:, :, :, y, held.start + p]
                cols = columns(y, p)
                dst = scratch.at[:, :, :, p, :, cols] if name == "shrink" else scratch.at[:, :, :, :, cols]
                pltpu.make_async_copy(src, dst, sem).start()
            continue
        for k in range(4):
            for b in range(2):
                x, y, c = me[1] ^ (k & 1), me[3] ^ (k >> 1), me[2] ^ b
                src = refs[k * 2 + b].at[:, held.start + p]
                cols = columns(y, p)
                dst = scratch.at[:, x, c, p, :, cols] if name == "shrink" else scratch.at[:, x, c, :, cols]
                pltpu.make_async_copy(src, dst, sem).start()


def arrived(scratch, sem):
    pltpu.make_async_copy(scratch, scratch, sem).wait()


def store(name, scratch, outs, start, me, sem):
    if len(outs) == 1 and outs[0].shape == scratch.shape:
        pltpu.make_async_copy(scratch, outs[0], sem).start()
        return
    count = COUNTS[name]
    piece = outs[0].shape[-1]
    if len(outs) == 1:
        for y in range(2):
            for p in range(count):
                src = scratch.at[:, :, :, p, :, pl.ds(y * piece, piece)]
                pltpu.make_async_copy(src, outs[0].at[:, :, :, y, p], sem).start()
        return
    for b in range(2):
        c = me[2] ^ b
        for y in range(2):
            for p in range(count):
                if name == "shrink":
                    src = scratch.at[:, :, c, p, :, pl.ds(y * piece, piece)]
                else:
                    src = scratch.at[:, :, c, :, pl.ds((y * count + p) * piece, piece)]
                pltpu.make_async_copy(src, outs[b].at[:, :, y, start + p], sem).start()


def flat(block):
    return block.reshape(-1, block.shape[-1])


def put_rows(scratch, value, cols):
    scratch[:, :, :, :, cols] = value.reshape(scratch.shape[:4] + (value.shape[-1],))


def normed(values, gain):
    r = lax.rsqrt(jnp.mean(values * values, axis=-1, keepdims=True) + EPS)
    return values * r * gain


def norm_back(values, gain, grad):
    r = lax.rsqrt(jnp.mean(values * values, axis=-1, keepdims=True) + EPS)
    inner = jnp.mean(values * gain * grad, axis=-1, keepdims=True)
    back = r * gain * grad - values * (r * r * r * inner)
    return back, jnp.sum(grad * values * r, axis=0, keepdims=True)


def prepare_kernel(lens, x, cot, gains, buckets, table, n1, kept, bias):
    rows = cot.shape[1]
    for s in range(x.shape[0]):
        values = x[s].astype(F32)
        n1[s * rows : (s + 1) * rows, :] = normed(values, gains[0:1, :]).astype(BF)
        keep = lax.broadcasted_iota(jnp.int32, (rows, 1), 0) < lens[s]
        kept[s * rows : (s + 1) * rows, :] = jnp.where(keep, cot[s].astype(F32), 0.0).astype(BF)
    half = 128
    heads = 2 * bias.shape[0]

    @pl.loop(0, rows // 8)
    def _(step):
        start = pl.multiple_of(step * 8, 8)
        for side in range(rows // half):
            which = buckets[pl.ds(start, 8), side * half : (side + 1) * half]
            key = start + lax.broadcasted_iota(jnp.int32, (8, half), 0)
            query = side * half + lax.broadcasted_iota(jnp.int32, (8, half), 1)
            for h in range(heads):
                row = jnp.broadcast_to(table[h : h + 1, :], (8, half))
                found = jnp.take_along_axis(row, which, axis=1)
                at = (h % 2) * rows + side * half
                bias[h // 2, pl.ds(start, 8), at : at + half] = jnp.where(
                    key <= query, found, NEGATIVE
                )


CHUNK = 32


def stacked(block):
    lane = lax.broadcasted_iota(jnp.int32, block.shape, 1)
    zero = jnp.zeros_like(block)
    return jnp.concatenate((jnp.where(lane < DH, block, zero), jnp.where(lane < DH, zero, block)))


def unstacked(block):
    queries = block.shape[1] // 2
    return jnp.concatenate((block[:DH, :queries], block[DH:, queries:]), axis=0).T


def folded(block, by):
    return by(block.reshape(block.shape[0] // 8, 8, block.shape[1]), axis=0)


def chunks(size):
    return [slice(at, at + CHUNK) for at in range(0, size, CHUNK)]


def forward_units(units, size, fix):
    for query, keys, values, scores, probs, mixed, logsum, which in units:
        scores[:size] = nt(keys, stacked(query * jnp.asarray(SCALE, BF)))
    for query, keys, values, scores, probs, mixed, logsum, which in units:
        top = None
        for part in chunks(size):
            block, changed = fix(scores[part], part, which)
            if changed:
                scores[part] = block
            block = folded(block, jnp.max)
            top = block if top is None else jnp.maximum(top, block)
        highest = jnp.max(top, axis=0, keepdims=True)
        total = jnp.zeros((8, highest.shape[1]), F32)
        for part in chunks(size):
            weights = jnp.exp(scores[part] - highest)
            total = total + folded(weights, jnp.sum)
            probs[part] = weights.astype(BF)
        total = jnp.sum(total, axis=0, keepdims=True)
        logsum[...] = highest + jnp.log(total)
        mixed[...] = unstacked(tn(values, probs[:size]) * (1.0 / total)).astype(BF)


def backward_units(units, size, fix):
    for query, keys, values, grad, mixed, logsum, scores, slopes, probs, grads, outs, which in units:
        scores[:size] = nt(keys, stacked(query * jnp.asarray(SCALE, BF)))
        slopes[:size] = nt(values, stacked(grad))
    for query, keys, values, grad, mixed, logsum, scores, slopes, probs, grads, outs, which in units:
        product = stacked(grad.astype(F32) * mixed.astype(F32))
        high = product.astype(BF)
        low = (product - high.astype(F32)).astype(BF)
        ones = jnp.ones((8, product.shape[1]), BF)
        inner = (nt(ones, high) + nt(ones, low))[0:1]
        for part in chunks(size):
            block, keep = fix(scores[part], part, which)
            weights = jnp.exp(block - logsum[...])
            if keep is not None:
                weights = jnp.where(keep, weights, 0.0)
            probs[part] = weights.astype(BF)
            grads[part] = (weights * (slopes[part] - inner)).astype(BF)
        left = grads[:size]
        outs[0][...] = (unstacked(tn(keys, left)) * SCALE).astype(BF)
        outs[1][...] = nn(left, stacked(query * jnp.asarray(SCALE, BF))).astype(BF)
        outs[2][...] = nn(probs[:size], stacked(grad)).astype(BF)


def self_units(length):
    return [(slice(s * length, (s + 1) * length), slice(j * 128, (j + 1) * 128), s, j) for s in range(2) for j in range(2)]


def self_forward_kernel(query, keys, values, bias, mixed, logsum, scores, probs):
    length = bias.shape[1]
    units = []
    for rows, cols, s, j in self_units(length):
        u = s * 2 + j
        units.append(
            (
                query[rows, cols],
                keys[rows, cols],
                values[rows, cols],
                scores.at[u],
                probs.at[u],
                mixed.at[rows, cols],
                logsum.at[j, s],
                j,
            )
        )
    forward_units(units, length, lambda block, part, j: (block + bias[j, part, :], True))


def self_backward_kernel(
    query, keys, values, grad, mixed, bias, logsum, gq, gk, gv, grad_bias, scores, slopes, probs, grads
):
    length = bias.shape[1]
    units = []
    for rows, cols, s, j in self_units(length):
        u = s * 2 + j
        units.append(
            (
                query[rows, cols],
                keys[rows, cols],
                values[rows, cols],
                grad[rows, cols],
                mixed[rows, cols],
                logsum.at[j, s],
                scores.at[u],
                slopes.at[u],
                probs.at[u],
                grads.at[u],
                (gq.at[rows, cols], gk.at[rows, cols], gv.at[rows, cols]),
                j,
            )
        )
    backward_units(units, length, lambda block, part, j: (block + bias[j, part, :], None))
    for j in range(2):
        for part in chunks(length):
            grad_bias[j, part, :] = grads[j, part, :].astype(F32) + grads[2 + j, part, :].astype(F32)


def last_tile(valid, size, part, block):
    if part.start < size - KEY_TILE:
        return None
    return part.start + lax.broadcasted_iota(jnp.int32, block.shape, 0) < valid


def cross_forward_kernel(lens, query, keys, values, mixed, logsum, scores, probs):
    valid = lens[pl.program_id(0)]
    for tiles in range(1, keys.shape[0] // KEY_TILE + 1):

        @pl.when((valid + KEY_TILE - 1) // KEY_TILE == tiles)
        def _():
            size = tiles * KEY_TILE

            def fix(block, part, which):
                keep = last_tile(valid, size, part, block)
                if keep is None:
                    return block, False
                return jnp.where(keep, block, NEGATIVE), True

            units = []
            for j in range(2):
                cols = slice(j * 128, (j + 1) * 128)
                units.append(
                    (
                        query[:, cols],
                        keys[:size, cols],
                        values[:size, cols],
                        scores.at[j],
                        probs.at[j],
                        mixed.at[:, cols],
                        logsum.at[j, 0],
                        None,
                    )
                )
            forward_units(units, size, fix)


def cross_backward_kernel(
    lens, query, keys, values, grad, mixed, logsum, gq, gk, gv, scores, slopes, probs, grads
):
    valid = lens[pl.program_id(0)]
    for tiles in range(1, keys.shape[0] // KEY_TILE + 1):

        @pl.when((valid + KEY_TILE - 1) // KEY_TILE == tiles)
        def _():
            size = tiles * KEY_TILE
            units = []
            for j in range(2):
                cols = slice(j * 128, (j + 1) * 128)
                units.append(
                    (
                        query[:, cols],
                        keys[:size, cols],
                        values[:size, cols],
                        grad[:, cols],
                        mixed[:, cols],
                        logsum.at[j, 0],
                        scores.at[j],
                        slopes.at[j],
                        probs.at[j],
                        grads.at[j],
                        (gq.at[:, cols], gk.at[:size, cols], gv.at[:size, cols]),
                        None,
                    )
                )
            backward_units(
                units,
                size,
                lambda block, part, which: (block, last_tile(valid, size, part, block)),
            )


def attend_scratch(units, keys, queries, backward):
    wide = pltpu.VMEM((units, keys, 2 * queries), F32)
    thin = pltpu.VMEM((units, keys, 2 * queries), BF)
    return [wide, wide, thin, thin] if backward else [wide, thin]


def pair_spec(rows, base=0):
    return pl.BlockSpec((rows, 256), lambda s, p: (s, base + p))


def both_spec(rows, base=0):
    return pl.BlockSpec((rows, 256), lambda p: (0, base + p))


def inward_kernel(held, me, n1, *rest):
    refs, (packed, weight, sem) = rest[: len(held.arrays)], rest[len(held.arrays) :]
    load("inward", held, refs, weight, me, sem)
    arrived(weight, sem)
    size = n1.shape[1]
    left = n1[...]
    for block in range(3):
        cols = slice(block * size, (block + 1) * size)
        packed[:, cols] = nn(left, flat(weight[..., cols])).astype(BF)


def outward_kernel(held, me, x, mixed, gains, *rest):
    refs, (after, n2, weight, sem) = rest[: len(held.arrays)], rest[len(held.arrays) :]
    load("outward", held, refs, weight, me, sem)
    arrived(weight, sem)
    values = x[...].astype(F32) + nn(mixed[...], flat(weight[...]))
    after[...] = values
    n2[...] = normed(values, gains[1:2, :]).astype(BF)


def memory_kernel(held_query, held_reader, me, lens, n2, encoded, *rest):
    k, both = len(held_query.arrays), len(held_query.arrays) + len(held_reader.arrays)
    refs_query, refs_reader = rest[:k], rest[k:both]
    asks, pairs, weight_query, weight_reader, sems = rest[both:]
    step = pl.program_id(0)
    tiles = pl.num_programs(0) // lens.shape[0]

    @pl.when(step == 0)
    def _():
        load("query", held_query, refs_query, weight_query, me, sems.at[0])
        load("reader", held_reader, refs_reader, weight_reader, me, sems.at[1])
        arrived(weight_query, sems.at[0])
        asks[...] = nn(n2[...], flat(weight_query[...])).astype(BF)
        arrived(weight_reader, sems.at[1])

    @pl.when(lax.rem(step, tiles) * encoded.shape[0] < lens[step // tiles])
    def _():
        size = encoded.shape[1]
        left = encoded[...]
        for block in range(2):
            cols = slice(block * size, (block + 1) * size)
            pairs[:, cols] = nn(left, flat(weight_reader[..., cols])).astype(BF)


def gelu_parts(v):
    phi = 0.5 * (1.0 + lax.erf(v * (0.5**0.5)))
    density = jnp.exp(-0.5 * v * v) * 0.3989422804014327
    return v * phi, phi + v * density


def widen_kernel(held_writer, held_expand, me, after_self, mixed, gains, kept, *rest):
    k, both = len(held_writer.arrays), len(held_writer.arrays) + len(held_expand.arrays)
    refs_writer, refs_expand = rest[:k], rest[k:both]
    outs = rest[both:]
    after_cross, n3, hidden, slope = outs[:4]
    grads, (weight_writer, weight_expand, shrink_grad, sems) = outs[4:-4], outs[-4:]
    load("writer", held_writer, refs_writer, weight_writer, me, sems.at[0])
    load("expand", held_expand, refs_expand, weight_expand, me, sems.at[1])
    arrived(weight_writer, sems.at[0])
    values = after_self[...] + nn(mixed[...], flat(weight_writer[...]))
    after_cross[...] = values
    n3[...] = normed(values, gains[2:3, :]).astype(BF)
    arrived(weight_expand, sems.at[1])
    size = n3.shape[1]

    for z in range(4):
        cols = slice(z * size, (z + 1) * size)
        before = nn(n3[...], flat(weight_expand[:, :, :, :, cols]))
        active, gate = gelu_parts(before)
        active = active.astype(BF)
        hidden[:, cols] = active
        slope[:, cols] = gate.astype(BF)
        grad = tn(active, kept[...]).astype(BF)
        shrink_grad[z] = grad.reshape(shrink_grad.shape[1:])

    store("shrink", shrink_grad, grads, 0, me, sems.at[2])
    arrived(shrink_grad, sems.at[2])


def narrow_kernel(
    held_shrink, held_expand, me, lens, n3, kept, gains, after_hbm, hidden_hbm, slope_hbm, *rest
):
    k, both = len(held_shrink.arrays), len(held_shrink.arrays) + len(held_expand.arrays)
    refs_shrink, refs_expand = rest[:k], rest[k:both]
    outs = rest[both:]
    layer_out, grad_cross, gain_part = outs[:3]
    grads, scratch = outs[3:-8], outs[-8:]
    weight_shrink, weight_expand, expand_grad, grad_wide, after_cross, hidden, slope, sems = scratch
    load("shrink", held_shrink, refs_shrink, weight_shrink, me, sems.at[0])
    pltpu.make_async_copy(slope_hbm, slope, sems.at[3]).start()
    load("expand", held_expand, refs_expand, weight_expand, me, sems.at[1])
    pltpu.make_async_copy(hidden_hbm, hidden, sems.at[4]).start()
    pltpu.make_async_copy(after_hbm, after_cross, sems.at[5]).start()
    size = n3.shape[1]
    arrived(weight_shrink, sems.at[0])
    arrived(slope, sems.at[3])
    for z in range(4):
        cols = slice(z * size, (z + 1) * size)
        grad_wide[:, cols] = (
            slope[:, cols].astype(F32) * nt(kept[...], flat(weight_shrink[z]))
        ).astype(BF)
    turned = n3[...].T
    for z in range(4):
        cols = slice(z * size, (z + 1) * size)
        put_rows(expand_grad, nn(turned, grad_wide[:, cols]).astype(BF), cols)
    store("expand", expand_grad, grads, 0, me, sems.at[2])
    arrived(hidden, sems.at[4])
    arrived(after_cross, sems.at[5])
    total = after_cross[...] + nn(hidden[...], flat(weight_shrink[...]))
    rows = total.shape[0] // lens.shape[0]
    for s in range(lens.shape[0]):
        part = slice(s * rows, (s + 1) * rows)
        keep = lax.broadcasted_iota(jnp.int32, (rows, 1), 0) < lens[s]
        layer_out[s] = jnp.where(keep, total[part, :], 0.0).astype(BF)
    arrived(weight_expand, sems.at[1])
    grad_norm = nt(grad_wide[...], flat(weight_expand[...]))
    back, gain = norm_back(after_cross[...], gains[2:3, :], grad_norm)
    grad_cross[...] = kept[...].astype(F32) + back
    gain_part[...] = gain
    arrived(expand_grad, sems.at[2])


def writer_back_kernel(held, me, grad_cross, mixed, *rest):
    k = len(held.arrays)
    refs, outs = rest[:k], rest[k:]
    grad_mixed, grads, (weight, grad_scratch, sems) = outs[0], outs[1:-3], outs[-3:]
    load("writer", held, refs, weight, me, sems.at[0])
    branch = grad_cross[...].astype(BF)
    put_rows(grad_scratch, tn(mixed[...], branch).astype(BF), slice(None))
    store("writer", grad_scratch, grads, 0, me, sems.at[1])
    arrived(weight, sems.at[0])
    grad_mixed[...] = nt(branch, flat(weight[...])).astype(BF)
    arrived(grad_scratch, sems.at[1])


def query_back_kernel(
    packed_mode,
    held_query,
    held_out,
    me,
    grad_asks,
    n2,
    after_self,
    grad_cross,
    mixed,
    gains,
    *rest,
):
    k, both = len(held_query.arrays), len(held_query.arrays) + len(held_out.arrays)
    refs_query, refs_out = rest[:k], rest[k:both]
    rest = rest[both:]
    grad_self, grad_mixed, gain_part = rest[:3]
    weight_query, weight_out, query_grad, out_grad, sems = rest[-5:]
    grads = rest[3:-5]
    load("query", held_query, refs_query, weight_query, me, sems.at[0])
    load("outward", held_out, refs_out, weight_out, me, sems.at[1])
    put_rows(query_grad, tn(n2[...], grad_asks[...]).astype(BF), slice(None))
    store("query", query_grad, grads if packed_mode else grads[:1], 0, me, sems.at[2])
    arrived(weight_query, sems.at[0])
    back, gain = norm_back(
        after_self[...], gains[1:2, :], nt(grad_asks[...], flat(weight_query[...]))
    )
    total = grad_cross[...] + back
    grad_self[...] = total
    gain_part[...] = gain
    branch = total.astype(BF)
    arrived(weight_out, sems.at[1])
    grad_mixed[...] = nt(branch, flat(weight_out[...])).astype(BF)
    put_rows(out_grad, tn(mixed[...], branch).astype(BF), slice(None))
    store("outward", out_grad, grads if packed_mode else grads[1:], 1, me, sems.at[3])
    arrived(query_grad, sems.at[2])
    arrived(out_grad, sems.at[3])


def inward_grad_kernel(me, n1, gq, gk, gv, *rest):
    grads, (scratch, sem) = rest[:-2], rest[-2:]
    size = n1.shape[1]
    turned = n1[...].T
    for block, grad in enumerate((gq, gk, gv)):
        cols = slice(block * size, (block + 1) * size)
        put_rows(scratch, nn(turned, grad[...]).astype(BF), cols)
    store("inward", scratch, grads, 0, me, sem)
    arrived(scratch, sem)


def inputs_grad_kernel(held, me, gq, gk, gv, gains, x_hbm, self_hbm, *rest):
    k = len(held.arrays)
    refs, (out, gain_part, weight, x, grad_self, sems) = rest[:k], rest[k:]
    load("inward", held, refs, weight, me, sems.at[0])
    pltpu.make_async_copy(x_hbm, x, sems.at[1]).start()
    pltpu.make_async_copy(self_hbm, grad_self, sems.at[2]).start()
    arrived(weight, sems.at[0])
    size = gq.shape[1]
    total = 0.0
    for block, grad in enumerate((gq, gk, gv)):
        cols = slice(block * size, (block + 1) * size)
        total = total + nt(grad[...], flat(weight[..., cols]))
    arrived(x, sems.at[1])
    arrived(grad_self, sems.at[2])
    back, gain = norm_back(x[...].astype(F32), gains[0:1, :], total)
    out[...] = grad_self[...] + back
    gain_part[...] = gain


def reader_grad_kernel(me, lens, encoded, gk, gv, *rest):
    grads, (scratch, total, sem) = rest[:-3], rest[-3:]
    step = pl.program_id(0)
    size = encoded.shape[1]
    valid = lens[step]
    for tiles in range(1, encoded.shape[0] // KEY_TILE + 1):

        @pl.when((valid + KEY_TILE - 1) // KEY_TILE == tiles)
        def _():
            rows = tiles * KEY_TILE
            turned = encoded[:rows].T
            for block, grad in enumerate((gk, gv)):
                cols = slice(block * size, (block + 1) * size)
                before = jnp.where(step == 0, 0.0, total[:, cols])
                total[:, cols] = before + nn(turned, grad[:rows])

    @pl.when(step == pl.num_programs(0) - 1)
    def _():
        put_rows(scratch, total[...].astype(BF), slice(None))
        store("reader", scratch, grads, 0, me, sem)
        arrived(scratch, sem)


def encoded_grad_kernel(held, me, lens, gk, gv, *rest):
    refs, (out, weight, sem) = rest[: len(held.arrays)], rest[len(held.arrays) :]
    step = pl.program_id(0)
    steps = pl.num_programs(0) // lens.shape[0]
    height, size = gk.shape
    left = lens[step // steps] - lax.rem(step, steps) * height

    @pl.when(step == 0)
    def _():
        load("reader", held, refs, weight, me, sem)
        arrived(weight, sem)

    for tiles in range(1, height // KEY_TILE + 1):
        rows = tiles * KEY_TILE
        last = tiles == height // KEY_TILE
        fits = left > rows - KEY_TILE

        @pl.when(fits if last else jnp.logical_and(fits, left <= rows))
        def _():
            out[:rows] = nt(gk[:rows], flat(weight[..., :size])) + nt(
                gv[:rows], flat(weight[..., size:])
            )
            if rows < height:
                out[rows:] = jnp.zeros((height - rows, size), F32)

    @pl.when(left <= 0)
    def _():
        out[...] = jnp.zeros_like(out)


def table_kernel(count, buckets, grad_bias, out, hot):
    pairs, length = grad_bias.shape[:2]
    group = hot.shape[0]
    lane = lax.broadcasted_iota(jnp.int32, out.shape, 1)

    def one(step, total):
        for k in range(group):
            hot[k] = jnp.where(buckets[...] == step * group + k, 1.0, 0.0)
        rows = [[] for _ in range(group)]
        for h in range(2 * pairs):
            cols = slice((h % 2) * length, (h % 2 + 1) * length)
            sums = [jnp.zeros((8, length), F32) for _ in range(group)]
            for part in chunks(length):
                value = grad_bias[h // 2, part, cols]
                for k in range(group):
                    sums[k] = sums[k] + folded(hot[k, part] * value, jnp.sum)
            for k in range(group):
                rows[k].append(jnp.sum(sums[k], axis=0, keepdims=True))
        for k in range(group):
            value = jnp.sum(jnp.concatenate(rows[k], axis=0), axis=1, keepdims=True)
            total = total + jnp.where(lane == step * group + k, value, 0.0)
        return total

    out[...] = lax.fori_loop(0, count // group, one, jnp.zeros(out.shape, F32))


def shared_places(widths, piece, width):
    starts = [0]
    for w in widths:
        starts.append(starts[-1] + w // piece)
    return starts[:-1], starts[-1], starts[-1] + 1, starts[-1] + 1 + 3 * (width // piece)


def statistics_kernel(piece, *refs):
    grads, gains, table, rows, shared = refs[:7], refs[7:10], refs[10], refs[11], refs[12]
    width = gains[0].shape[1]
    starts, totals_at, gains_at, table_at = shared_places([g.shape[1] for g in grads], piece, width)
    rows[...] = jnp.zeros_like(rows)
    shared[...] = jnp.zeros_like(shared)
    lane = lax.broadcasted_iota(jnp.int32, (1, 128), 1)
    lane_piece = lax.broadcasted_iota(jnp.int32, (1, piece), 1)
    totals = jnp.zeros((1, piece), F32)
    for j, grad in enumerate(grads):
        square = grad[...] * grad[...]
        count, wide = square.shape
        sums = jnp.sum(square, axis=1, keepdims=True)
        rows[:count, :] += jnp.where(lane == j, sums, 0.0)
        columns = jnp.sum(square, axis=0, keepdims=True)
        for p in range(wide // piece):
            at = starts[j] + p
            shared[at : at + 1, :] = columns[:, p * piece : (p + 1) * piece]
        totals = totals + jnp.where(lane_piece == j, jnp.sum(sums, axis=0, keepdims=True), 0.0)
    shared[totals_at : totals_at + 1, :] = totals
    for k in range(3):
        for p in range(width // piece):
            at = gains_at + k * (width // piece) + p
            shared[at : at + 1, :] = gains[k][:, p * piece : (p + 1) * piece]
    keep = min(piece, table.shape[1])
    shared[table_at : table_at + table.shape[0], :keep] = table[:, :keep]


def steps_kernel(wide, narrow, *refs):
    grads, rows, shared = refs[:7], refs[7], refs[8]
    outs = refs[9:]
    piece = shared.shape[1]
    starts, totals_at, _, _ = shared_places([g.shape[1] for g in grads], piece, piece)
    turned = rows[...].T
    for j, grad in enumerate(grads):
        step, row_out, col_out = outs[3 * j : 3 * j + 3]
        count, width = grad.shape
        full_rows, full_cols = count * wide, width * narrow
        row = rows[:count, j : j + 1] / full_cols + TINY
        mean = shared[totals_at : totals_at + 1, j : j + 1] / (full_rows * full_cols) + TINY
        cols = []
        for p in range(width // piece):
            at = starts[j] + p
            part = slice(p * piece, (p + 1) * piece)
            col = shared[at : at + 1, :] / full_rows + TINY
            step[:, part] = grad[:, part] * lax.rsqrt(row * col / mean)
            cols.append(col)
        row_out[...] = (turned[j : j + 1, :count] / full_cols + TINY).reshape(count)
        col = cols[0] if len(cols) == 1 else jnp.concatenate(cols, axis=1)
        col_out[...] = col.reshape(width)


def tie(value, after):
    after = tuple(after)
    return lax.optimization_barrier((value,) + after)[0] if after else value


def join(gathers, arrays=()):
    keys = [(g, key) for g in gathers for key in g.live]
    flat_values, tree = jax.tree.flatten(([g.live[key] for g, key in keys], list(arrays)))
    values, arrays = jax.tree.unflatten(tree, lax.optimization_barrier(tuple(flat_values)))
    for (g, key), value in zip(keys, values):
        g.live[key] = value
    return arrays


class Hyper:
    MASKS = {"y": 1, "c": 2, "x": 4, "xy": 5, "z1": 8, "z2": 16, "z3": 24}

    def __init__(self):
        wide = lax.axis_index("wide")
        self.z, self.x, self.c = wide // 4, (wide // 2) % 2, wide % 2
        self.y = lax.axis_index("narrow")
        self.me = jnp.stack((self.z, self.x, self.c, self.y)).astype(jnp.int32)

    def swap(self, value, bit, after=()):
        mask = self.MASKS[bit]
        return lax.ppermute(tie(value, after), BOTH, [(i, i ^ mask) for i in range(32)])


class Gather:
    def __init__(self, hyper, shards, plan, width):
        self.hyper, self.plan = hyper, plan
        self.live = {"own": jnp.stack([cut(name, shards[name], width)[p] for name, p in plan])}

    def z(self):
        own = self.live["own"]
        self.live["others"] = [self.hyper.swap(own, bit) for bit in ("z1", "z2", "z3")]

    def z1(self):
        self.live["other"] = self.hyper.swap(self.live["own"], "z1")

    def z2(self):
        h = self.hyper
        own, other = self.live.pop("own"), self.live.pop("other")
        pair = jnp.where(h.z % 2 == 0, jnp.stack((own, other)), jnp.stack((other, own)))
        self.live["own"], self.live["other"] = pair, h.swap(pair, "z2")

    def plane(self):
        h = self.hyper
        own = self.live.pop("own")
        if "others" in self.live:
            one, two, three = self.live.pop("others")
            even = h.z % 2 == 0
            own = jnp.where(even, jnp.stack((own, one)), jnp.stack((one, own)))
            other = jnp.where(even, jnp.stack((two, three)), jnp.stack((three, two)))
        else:
            other = self.live.pop("other")
        quad = jnp.where(
            h.z // 2 == 0, jnp.concatenate((own, other)), jnp.concatenate((other, own))
        )
        self.live["quads"] = [quad] + [h.swap(quad, bit) for bit in ("x", "y", "xy")]

    def core_own(self):
        self.live["first"] = self.hyper.swap(self.live["quads"][0], "c")

    def core(self):
        self.live["cores"] = [self.live.pop("first")] + [
            self.hyper.swap(quad, "c") for quad in self.live["quads"][1:]
        ]

    def held(self, name):
        arrays = [a for two in zip(self.live["quads"], self.live["cores"]) for a in two]
        return Held(arrays, self.plan.index((name, 0)))


def fold_kernel(counts, joint, names, me, *refs):
    na, nb, nj = counts
    first, second, both, outs = refs[:na], refs[na : na + nb], refs[na + nb : na + nb + nj], refs[na + nb + nj :]
    pa = first[0].shape[3]

    def add(parts, part):
        return sum([r[...].astype(F32) for r in parts] + [r[:, :, :, part].astype(F32) for r in both])

    one = add(first, slice(0, pa))
    two = add(second, slice(pa, None))
    if names:
        pieces = [one[0, 0, 0, p] for p in range(one.shape[3])]
        pieces += [two[0, 0, 0, p] for p in range(two.shape[3])]
        for out, (name, start) in zip(outs, names):
            for p in range(COUNTS[name]):
                piece = pieces[start + p]
                if name == "shrink":
                    out[p * piece.shape[0] : (p + 1) * piece.shape[0], :] = piece
                else:
                    out[:, p * piece.shape[1] : (p + 1) * piece.shape[1]] = piece
    elif joint:
        outs[0][:, :, :, :pa] = one.astype(outs[0].dtype)
        outs[0][:, :, :, pa:] = two.astype(outs[0].dtype)
    else:
        outs[0][...] = one.astype(outs[0].dtype)
        outs[1][...] = two.astype(outs[1].dtype)


class HalvedScatter:
    def __init__(self, hyper, first, second, name):
        self.hyper, self.halves, self.name = hyper, (first, second), name
        self.parts = [[], []]
        self.joint = []
        self.sizes = [half[0].shape[3] for half in (first, second)]
        self.block = first[0].shape[4:]

    def core(self, half, after=()):
        keep, send = self.halves[half]
        recv = self.hyper.swap(send, "c", after)
        self.parts[half] = [keep, recv]
        return [recv]

    def fold(self, picks, out_dims, joint, after, step):
        ins = []
        for half in range(2):
            p = self.sizes[half]
            for array, (dims, index) in zip(self.parts[half], picks[half]):
                spec = pl.BlockSpec(
                    tuple(dims) + (p,) + self.block,
                    lambda i, me, index=index: tuple(index(me)) + (0, 0, 0),
                )
                ins.append((array, spec))
        whole = sum(self.sizes)
        for array, index in zip(self.joint, picks[2]):
            spec = pl.BlockSpec(
                (1, 1, 1, whole) + self.block,
                lambda i, me, index=index: (index(me), 0, 0, 0, 0, 0),
            )
            ins.append((array, spec))
        outs = []
        rows, cols = self.block
        for dims, kind in out_dims:
            if isinstance(dims, str):
                count = COUNTS[dims]
                full = (count * rows, cols) if dims == "shrink" else (rows, count * cols)
                outs.append((shape(full, F32), pl.BlockSpec(full, lambda i, me: (0, 0))))
                continue
            p = whole if joint else self.sizes[len(outs)]
            full = tuple(dims) + (p,) + self.block
            outs.append((shape(full, kind), pl.BlockSpec(full, lambda i, me: (0,) * 6)))
        counts = (len(self.parts[0]), len(self.parts[1]), len(self.joint))
        names = out_dims if step == "last" else None
        self.sent = launch(
            functools.partial(fold_kernel, counts, joint, names),
            ins,
            outs,
            grid=(1,),
            gflop=1.0,
            name=f"{self.name}_{step}",
            after=after,
            prefetch=(self.hyper.me,),
        )
        return self.sent

    def p1(self, after=()):
        a = [((4, 2, 1), lambda me: (0, 0, 1 - me[3]))] * 2
        b = [((4, 1, 2), lambda me: (0, 1 - me[1], 0))] * 2
        sent = self.fold((a, b, ()), (((4, 2, 1), BF), ((4, 1, 2), BF)), False, after, "p1")
        recv = [self.hyper.swap(value, bit) for value, bit in zip(sent, "yx")]
        for half in range(2):
            self.parts[half].append(recv[half])
        return recv

    def p2(self, after=()):
        four = (4, 1, 1)
        a = [(four, lambda me: (0, 1 - me[1], me[3]))] * 2
        a += [(four, lambda me: (0, 1 - me[1], 0))]
        b = [(four, lambda me: (0, me[1], 1 - me[3]))] * 2
        b += [(four, lambda me: (0, 0, 1 - me[3]))]
        sent = self.fold((a, b, ()), ((four, BF), (four, BF)), False, after, "p2")
        recv = [self.hyper.swap(value, bit) for value, bit in zip(sent, "xy")]
        for half in range(2):
            self.parts[half].append(recv[half])
        return recv

    def own(self, count, place):
        dims = (count, 1, 1)
        a = [(dims, lambda me: (place(me), me[1], me[3]))] * 2
        a += [(dims, lambda me: (place(me), me[1], 0)), (dims, lambda me: (place(me), 0, 0))]
        b = [(dims, lambda me: (place(me), me[1], me[3]))] * 2
        b += [(dims, lambda me: (place(me), 0, me[3])), (dims, lambda me: (place(me), 0, 0))]
        return a, b

    def z2(self, after=()):
        a, b = self.own(2, lambda me: 1 - me[0] // 2)
        (sent,) = self.fold((a, b, ()), (((2, 1, 1), BF),), True, after, "z2")
        recv = self.hyper.swap(sent, "z2")
        self.joint.append(recv)
        return [recv]

    def z1(self, after=()):
        a, b = self.own(1, lambda me: (me[0] // 2) * 2 + 1 - lax.rem(me[0], 2))
        j = [lambda me: 1 - lax.rem(me[0], 2)]
        (sent,) = self.fold((a, b, j), (((1, 1, 1), BF),), True, after, "z1")
        recv = self.hyper.swap(sent, "z1")
        self.joint.append(recv)
        return [recv]

    def last(self, weights, after=()):
        a, b = self.own(1, lambda me: me[0])
        j = [lambda me: lax.rem(me[0], 2), lambda me: 0]
        return self.fold((a, b, j), weights, True, after, "last")


def plane_kernel(me, *refs):
    groups, outs = refs[:-4], refs[-4:]
    for k, out in enumerate(outs):
        x, y = me[1] ^ (k & 1), me[3] ^ (k >> 1)
        at = 0
        for keep, recv in zip(groups[::2], groups[1::2]):
            total = keep[:, x, y].astype(F32) + recv[:, x, y].astype(F32)
            out[:, at : at + total.shape[1]] = total.astype(out.dtype)
            at += total.shape[1]


def line_kernel(me, own, one, two, three, *outs):
    for k, out in enumerate(outs):
        z = me[0] ^ k
        total = own[z] + one[z].astype(F32) + two[z].astype(F32) + three[z].astype(F32)
        out[...] = total.astype(out.dtype)


def last_kernel(names, own, one, two, three, *outs):
    total = own[...] + one[...].astype(F32) + two[...].astype(F32) + three[...].astype(F32)
    at = 0
    for out, name in zip(outs, names):
        for p in range(COUNTS[name]):
            piece = total[at + p]
            if name == "shrink":
                out[p * piece.shape[0] : (p + 1) * piece.shape[0], :] = piece
            else:
                out[:, p * piece.shape[1] : (p + 1) * piece.shape[1]] = piece
        at += COUNTS[name]


class Scatter:
    def __init__(self, hyper, name, weights):
        self.hyper, self.name, self.weights = hyper, name, weights
        self.groups = []

    def core(self, keep, send):
        self.groups.append((keep, self.hyper.swap(send, "c")))

    def plane(self, after=()):
        count = sum(keep.shape[3] for keep, _ in self.groups)
        block = self.groups[0][0].shape[4:]
        dims = (4, count) + block
        self.own, *sent = launch(
            plane_kernel,
            [(self.hyper.me, SM)] + [(a, VM) for group in self.groups for a in group],
            [(shape(dims, F32), VM)] + [(shape(dims, BF), VM)] * 3,
            name=self.name + "_plane",
            after=after,
        )
        self.sent = sent
        self.got = [self.hyper.swap(a, bit) for a, bit in zip(sent, ("x", "y", "xy"))]

    def line(self, after=()):
        dims = self.own.shape[1:]
        self.own, *sent = launch(
            line_kernel,
            [(self.hyper.me, SM), (self.own, VM)] + [(a, VM) for a in self.got],
            [(shape(dims, F32), VM)] + [(shape(dims, BF), VM)] * 3,
            name=self.name + "_line",
            after=after,
        )
        self.sent = sent
        self.got = [self.hyper.swap(a, bit) for a, bit in zip(sent, ("z1", "z2", "z3"))]

    def last(self, after=()):
        rows, cols = self.own.shape[1:]
        outs = []
        for name in self.weights:
            count = COUNTS[name]
            full = (count * rows, cols) if name == "shrink" else (rows, count * cols)
            outs.append((shape(full, F32), VM))
        totals = launch(
            functools.partial(last_kernel, self.weights),
            [(self.own, VM)] + [(a, VM) for a in self.got],
            outs,
            name=self.name + "_last",
            after=after,
        )
        self.sent = totals
        return dict(zip(self.weights, totals))


def cut(name, shard, width):
    count = COUNTS[name]
    if name == "shrink":
        return shard.reshape(count, shard.shape[0] // count, shard.shape[1])
    rows, cols = shard.shape
    return jnp.transpose(shard.reshape(rows, count, cols // count), (1, 0, 2))


def whole_shape(name, width):
    if name == "shrink":
        return (4, 2, 2, 4, width // 16, width)
    return (4, 2, 2, width // 16, width * COUNTS[name])


def local(
    inputs,
    encoded,
    target_lengths,
    memory_lengths,
    buckets,
    cotangent,
    self_inward,
    self_outward,
    cross_query,
    cross_reader,
    cross_writer,
    expand_weight,
    shrink_weight,
    norm_gains,
    bias_table,
):
    wide_count = lax.axis_size("wide")
    narrow_count = lax.axis_size("narrow")
    fast = (wide_count, narrow_count) == (16, 2)
    seqs, length, width = inputs.shape
    memory_size = encoded.shape[1]
    rows, mem_rows = seqs * length, seqs * memory_size
    wide_hidden = expand_weight.shape[1] * narrow_count
    shards = dict(
        zip(
            NAMES,
            (
                self_inward,
                self_outward,
                cross_query,
                cross_reader,
                cross_writer,
                expand_weight,
                shrink_weight,
            ),
        )
    )
    hyper = Hyper() if fast else None
    me = hyper.me if fast else jnp.zeros((4,), jnp.int32)
    none = []

    def grad_outs(name, count):
        if fast:
            block = shape((4, 2, 2, count, width // 16, width // 2), BF)
            return [(block, HB), (block, HB)]
        return [(shape(whole_shape(name, width), BF), HB)]

    dma = pltpu.SemaphoreType.DMA
    x_rows = inputs.reshape(rows, width)
    mem_flat = encoded.reshape(mem_rows, width)
    heads = HEADS
    pairs_count = heads // 2
    turned = buckets.T
    table = jnp.pad(bias_table.T, ((0, 0), (0, 128 - bias_table.shape[0])))

    def weights(*names):
        return [entry for name in names for entry in held[name].ins()]

    held = {}
    if fast:
        ga, gb, gc, gd = [Gather(hyper, shards, plan, width) for plan in GATHERS]
        ga.z()
    else:
        for name in NAMES:
            full = lax.all_gather(shards[name], "narrow", axis=1, tiled=True)
            full = lax.all_gather(full, "wide", axis=0, tiled=True)
            full = full.reshape(whole_shape(name, width))
            held[name] = Held((full,))

    n1, kept, bias = launch(
        prepare_kernel,
        [
            (target_lengths, SM),
            (inputs, VM),
            (cotangent, VM),
            (norm_gains, VM),
            (turned, VM),
            (table, VM),
        ],
        [
            (shape((rows, width), BF), VM),
            (shape((rows, width), BF), VM),
            (shape((pairs_count, length, 2 * length), F32), VM),
        ],
        name="prepare",
    )

    if fast:
        n1, kept, bias = join((ga,), (n1, kept, bias))
        ga.plane()
        ga.core_own()
        gb.z1()
        gb.z2()
        join((ga, gb))
        ga.core()
        gb.plane()
        gc.z1()
        for name in ("inward", "outward"):
            held[name] = ga.held(name)

    (packed,) = launch(
        functools.partial(inward_kernel, held["inward"]),
        [(me, SM), (n1, VM)] + weights("inward"),
        [(shape((rows, 3 * width), BF), VM)],
        [weight_scratch("inward", width), dma],
        gflop=2.0,
        name="inward",
    )

    bias_spec = pl.BlockSpec((2, length, 2 * length), lambda p: (p, 0, 0))
    log_both = pl.BlockSpec((2, seqs, 1, 2 * length), lambda p: (p, 0, 0, 0))
    log_spec = pl.BlockSpec((2, 1, 1, 2 * length), lambda s, p: (p, s, 0, 0))
    log_shape = shape((pairs_count, seqs, 1, 2 * length), F32)
    blocks = pairs_count // 2
    self_mixed, self_log = launch(
        self_forward_kernel,
        [
            (packed, both_spec(rows)),
            (packed, both_spec(rows, blocks)),
            (packed, both_spec(rows, 2 * blocks)),
            (bias, bias_spec),
        ],
        [(shape((rows, width), BF), both_spec(rows)), (log_shape, log_both)],
        attend_scratch(4, length, length, False),
        grid=(blocks,),
        gflop=5.0,
        name="self_forward",
    )

    if fast:
        self_mixed, self_log = join((gc,), (self_mixed, self_log))
        gc.z2()

    after_self, n2 = launch(
        functools.partial(outward_kernel, held["outward"]),
        [(me, SM), (x_rows, VM), (self_mixed, VM), (norm_gains, VM)] + weights("outward"),
        [(shape((rows, width), F32), VM), (shape((rows, width), BF), VM)],
        [weight_scratch("outward", width), dma],
        gflop=2.0,
        name="outward",
    )

    if fast:
        after_self, n2 = join((gb, gc), (after_self, n2))
        gb.core_own()
        gb.core()
        gc.plane()
        gd.z1()
        for name in ("query", "writer", "reader"):
            held[name] = gb.held(name)

    tile_spec = pl.BlockSpec((KEY_TILE, width), lambda i: (i, 0))
    asks, pairs = launch(
        functools.partial(memory_kernel, held["query"], held["reader"]),
        [(me, SM), (memory_lengths, SM), (n2, VM), (mem_flat, pl.BlockSpec((2 * KEY_TILE, width), lambda i: (i, 0)))]
        + weights("query", "reader"),
        [
            (shape((rows, width), BF), pl.BlockSpec((rows, width), lambda i: (0, 0))),
            (
                shape((mem_rows, 2 * width), BF),
                pl.BlockSpec((2 * KEY_TILE, 2 * width), lambda i: (i, 0)),
            ),
        ],
        [weight_scratch("query", width), weight_scratch("reader", width), dma((2,))],
        grid=(mem_rows // (2 * KEY_TILE),),
        gflop=6.0,
        name="memory",
    )

    if fast:
        asks, pairs = join((gd,), (asks, pairs))
        gc.core_own()
        gd.z2()

    cross_mixed, cross_log = launch(
        cross_forward_kernel,
        [
            (memory_lengths, SM),
            (asks, pair_spec(length)),
            (pairs, pair_spec(memory_size)),
            (pairs, pair_spec(memory_size, blocks)),
        ],
        [(shape((rows, width), BF), pair_spec(length)), (log_shape, log_spec)],
        attend_scratch(2, memory_size, length, False),
        grid=(seqs, blocks),
        gflop=10.0,
        name="cross_forward",
    )

    if fast:
        cross_mixed, cross_log = join((gc, gd), (cross_mixed, cross_log))
        gc.core()
        held["expand"] = gc.held("expand")
        gd.plane()
        gd.core_own()

    after_cross, n3, hidden, slope, *shrink_parts = launch(
        functools.partial(widen_kernel, held["writer"], held["expand"]),
        [(me, SM), (after_self, VM), (cross_mixed, VM), (norm_gains, VM), (kept, VM)]
        + weights("writer", "expand"),
        [
            (shape((rows, width), F32), VM),
            (shape((rows, width), BF), VM),
            (shape((rows, wide_hidden), BF), VM),
            (shape((rows, wide_hidden), BF), VM),
        ]
        + grad_outs("shrink", 4),
        [
            weight_scratch("writer", width),
            weight_scratch("expand", width),
            weight_scratch("shrink", width),
            dma((3,)),
        ],
        gflop=10.0,
        name="widen",
    )

    if fast:
        after_cross, n3, hidden, slope = join((gd,), (after_cross, n3, hidden, slope))
        gd.core()
        held["shrink"] = gd.held("shrink")

    layer_out, grad_cross, gain_third, *expand_parts = launch(
        functools.partial(narrow_kernel, held["shrink"], held["expand"]),
        [
            (me, SM),
            (target_lengths, SM),
            (n3, VM),
            (kept, VM),
            (norm_gains, VM),
            (after_cross, HB),
            (hidden, HB),
            (slope, HB),
        ]
        + weights("shrink", "expand"),
        [
            (shape((seqs, length, width), BF), VM),
            (shape((rows, width), F32), VM),
            (shape((1, width), F32), VM),
        ]
        + grad_outs("expand", 4),
        [
            weight_scratch("shrink", width),
            weight_scratch("expand", width),
            weight_scratch("expand", width),
            pltpu.VMEM((rows, wide_hidden), BF),
            pltpu.VMEM((rows, width), F32),
            pltpu.VMEM((rows, wide_hidden), BF),
            pltpu.VMEM((rows, wide_hidden), BF),
            dma((6,)),
        ],
        gflop=14.0,
        name="narrow",
    )

    if fast:
        sf = HalvedScatter(hyper, shrink_parts, expand_parts, "ffn")
        sf.core(0)
        sf.core(1)

    grad_mixed, *writer_parts = launch(
        functools.partial(writer_back_kernel, held["writer"]),
        [(me, SM), (grad_cross, VM), (cross_mixed, VM)] + weights("writer"),
        [(shape((rows, width), BF), VM)] + grad_outs("writer", 1),
        [weight_scratch("writer", width), weight_scratch("writer", width), dma((2,))],
        gflop=2.0,
        name="writer_back",
    )

    if fast:
        sf.p1([grad_mixed])

    grad_asks, grad_mem_keys, grad_mem_values = launch(
        cross_backward_kernel,
        [
            (memory_lengths, SM),
            (asks, pair_spec(length)),
            (pairs, pair_spec(memory_size)),
            (pairs, pair_spec(memory_size, blocks)),
            (grad_mixed, pair_spec(length)),
            (cross_mixed, pair_spec(length)),
            (cross_log, log_spec),
        ],
        [
            (shape((rows, width), BF), pair_spec(length)),
            (shape((mem_rows, width), BF), pair_spec(memory_size)),
            (shape((mem_rows, width), BF), pair_spec(memory_size)),
        ],
        attend_scratch(2, memory_size, length, True),
        grid=(seqs, blocks),
        gflop=20.0,
        name="cross_backward",
        after=sf.sent if fast else none,
    )

    whole_spec = pl.BlockSpec((memory_size, width), lambda i: (i, 0))
    reader_parts = launch(
        reader_grad_kernel,
        [
            (me, SM),
            (memory_lengths, SM),
            (mem_flat, whole_spec),
            (grad_mem_keys, whole_spec),
            (grad_mem_values, whole_spec),
        ],
        grad_outs("reader", 2),
        [weight_scratch("reader", width), pltpu.VMEM((width, 2 * width), F32), dma],
        grid=(seqs,),
        gflop=5.0,
        name="reader_grad",
    )

    if fast:
        sf.p2([reader_parts[0]])
        sm = Scatter(hyper, "middle", ("writer", "reader", "query", "outward"))
        sm.core(*writer_parts)
        sm.core(*reader_parts)

    grad_self, grad_mixed, gain_second, *rest_parts = launch(
        functools.partial(query_back_kernel, fast, held["query"], held["outward"]),
        [
            (me, SM),
            (grad_asks, VM),
            (n2, VM),
            (after_self, VM),
            (grad_cross, VM),
            (self_mixed, VM),
            (norm_gains, VM),
        ]
        + weights("query", "outward"),
        [
            (shape((rows, width), F32), VM),
            (shape((rows, width), BF), VM),
            (shape((1, width), F32), VM),
        ]
        + (grad_outs("query", 2) if fast else grad_outs("query", 1) + grad_outs("outward", 1)),
        [
            weight_scratch("query", width),
            weight_scratch("outward", width),
            weight_scratch("query", width),
            weight_scratch("outward", width),
            dma((4,)),
        ],
        gflop=4.0,
        name="query_back",
        after=sf.sent if fast else none,
    )

    if fast:
        sm.core(*rest_parts)
        sf.z2([grad_mixed])
        sm.plane(sf.sent)

    grad_query, grad_keys, grad_values, grad_bias = launch(
        self_backward_kernel,
        [
            (packed, both_spec(rows)),
            (packed, both_spec(rows, blocks)),
            (packed, both_spec(rows, 2 * blocks)),
            (grad_mixed, both_spec(rows)),
            (self_mixed, both_spec(rows)),
            (bias, bias_spec),
            (self_log, log_both),
        ],
        [(shape((rows, width), BF), both_spec(rows))] * 3
        + [(shape((pairs_count, length, 2 * length), F32), bias_spec)],
        attend_scratch(4, length, length, True),
        grid=(blocks,),
        gflop=6.0,
        name="self_backward",
        after=sm.sent if fast else none,
    )

    inward_parts = launch(
        inward_grad_kernel,
        [(me, SM), (n1, VM), (grad_query, VM), (grad_keys, VM), (grad_values, VM)],
        grad_outs("inward", 3),
        [weight_scratch("inward", width), dma],
        gflop=2.0,
        name="inward_grad",
    )

    if fast:
        si = Scatter(hyper, "inward", ("inward",))
        si.core(*inward_parts)
        sf.z1([inward_parts[0]])

    inputs_grad, gain_first = launch(
        functools.partial(inputs_grad_kernel, held["inward"]),
        [
            (me, SM),
            (grad_query, VM),
            (grad_keys, VM),
            (grad_values, VM),
            (norm_gains, VM),
            (x_rows, HB),
            (grad_self, HB),
        ]
        + weights("inward"),
        [(shape((rows, width), F32), VM), (shape((1, width), F32), VM)],
        [
            weight_scratch("inward", width),
            pltpu.VMEM((rows, width), BF),
            pltpu.VMEM((rows, width), F32),
            dma((3,)),
        ],
        gflop=2.0,
        name="inputs_grad",
        after=sf.sent if fast else none,
    )

    if fast:
        si.plane([inputs_grad])
        sm.line(si.sent)
        sums = dict(zip(("shrink", "expand"), sf.last((("shrink", 0), ("expand", 4)), sm.sent)))

    double_spec = pl.BlockSpec((2 * KEY_TILE, width), lambda i: (i, 0))
    (encoded_grad,) = launch(
        functools.partial(encoded_grad_kernel, held["reader"]),
        [(me, SM), (memory_lengths, SM), (grad_mem_keys, double_spec), (grad_mem_values, double_spec)]
        + weights("reader"),
        [(shape((mem_rows, width), F32), double_spec)],
        [weight_scratch("reader", width), dma],
        grid=(mem_rows // (2 * KEY_TILE),),
        gflop=5.0,
        name="encoded_grad",
        after=sf.sent if fast else none,
    )

    if fast:
        si.line([encoded_grad])

    (table_part,) = launch(
        functools.partial(table_kernel, bias_table.shape[0]),
        [(turned, VM), (grad_bias, VM)],
        [(shape((heads, 128), F32), VM)],
        [pltpu.VMEM((4, length, length), F32)],
        gflop=6.0,
        name="table",
        after=si.sent if fast else none,
    )

    if fast:
        sums.update(sm.last([table_part]))
        sums.update(si.last(sm.sent))
    else:
        sums = {}
        parts = {
            "shrink": shrink_parts[0],
            "expand": expand_parts[0],
            "writer": writer_parts[0],
            "reader": reader_parts[0],
            "query": rest_parts[0],
            "outward": rest_parts[1],
            "inward": inward_parts[0],
        }
        for name in NAMES:
            full = parts[name].reshape(-1, parts[name].shape[-1]).astype(F32)
            full = lax.psum_scatter(full, "wide", scatter_dimension=0, tiled=True)
            sums[name] = lax.psum_scatter(full, "narrow", scatter_dimension=1, tiled=True)

    grads = [sums[name] for name in NAMES]
    tallest = max(g.shape[0] for g in grads)
    piece = width // narrow_count
    _, totals_at, gains_at, table_at = shared_places([g.shape[1] for g in grads], piece, width)
    row_sums, shared = launch(
        functools.partial(statistics_kernel, piece),
        [(g, VM) for g in grads]
        + [(gain_first, VM), (gain_second, VM), (gain_third, VM), (table_part, VM)],
        [(shape((tallest, 128), F32), VM), (shape((-(-(table_at + heads) // 8) * 8, piece), F32), VM)],
        name="statistics",
    )
    add_y = lax.broadcasted_iota(jnp.int32, shared.shape, 0) >= totals_at
    if fast:
        other = hyper.swap(row_sums, "y")
        shared = shared + jnp.where(add_y, hyper.swap(shared, "y"), 0.0)
        row_sums = row_sums + other
        shared = tie(shared, [other])
        for bit in ("c", "x", "z1", "z2"):
            shared = shared + hyper.swap(shared, bit)
    else:
        row_sums = lax.psum(row_sums, "narrow")
        shared = lax.psum(jnp.where(add_y, lax.psum(shared, "narrow"), shared), "wide")

    step_outs = []
    for g in grads:
        step_outs.append((shape(g.shape, F32), VM))
        step_outs.append((shape((g.shape[0],), F32), VM))
        step_outs.append((shape((g.shape[1],), F32), VM))
    made = launch(
        functools.partial(steps_kernel, wide_count, narrow_count),
        [(g, VM) for g in grads] + [(row_sums, VM), (shared, VM)],
        step_outs,
        name="steps",
    )
    results = []
    for j, grad in enumerate(grads):
        step, row_stat, col_stat = made[3 * j : 3 * j + 3]
        results.extend([grad, step, row_stat, col_stat])
    gains_grad = shared[gains_at:table_at].reshape(3, width)
    table_grad = shared[table_at : table_at + heads, : bias_table.shape[0]].T
    return (
        (
            layer_out,
            inputs_grad.reshape(inputs.shape),
            encoded_grad.reshape(encoded.shape),
        )
        + tuple(results)
        + (gains_grad, table_grad)
    )


def solution(mesh):
    tokens = P(BOTH, None, None)
    weight = P("wide", "narrow")
    per_weight = (weight, weight, P("wide"), P("narrow"))
    return jax.shard_map(
        local,
        mesh=mesh,
        in_specs=(tokens, tokens, P(BOTH), P(BOTH), P(), tokens) + (weight,) * 7 + (P(), P()),
        out_specs=(tokens, tokens, tokens) + per_weight * 7 + (P(), P()),
        check_vma=False,
    )
```

```python
import functools

import jax
import jax.numpy as jnp
from jax import lax
from jax.experimental import pallas as pl
from jax.experimental.pallas import tpu as pltpu
from jax.sharding import PartitionSpec as P

HEADS = 12
DH = 64
EPS = 1e-06
TINY = 1e-30
NEGATIVE = -1e30
SCALE = DH ** (-0.5)

BF = jnp.bfloat16
F32 = jnp.float32
BOTH = ("wide", "narrow")
VMEM_LIMIT = 63 * 1024 * 1024
KEY_TILE = 256

COUNTS = {
    "inward": 3,
    "outward": 1,
    "query": 1,
    "reader": 2,
    "writer": 1,
    "expand": 4,
    "shrink": 4,
}
NAMES = ("inward", "outward", "query", "reader", "writer", "expand", "shrink")
GATHERS = (
    (("inward", 0), ("inward", 1), ("inward", 2), ("outward", 0)),
    (("query", 0), ("writer", 0), ("reader", 0), ("reader", 1)),
    (("expand", 0), ("expand", 1), ("expand", 2), ("expand", 3)),
    (("shrink", 0), ("shrink", 1), ("shrink", 2), ("shrink", 3)),
)


def nn(left, right):
    return lax.dot_general(left, right, (((1,), (0,)), ((), ())), preferred_element_type=F32)


def nt(left, right):
    return lax.dot_general(left, right, (((1,), (1,)), ((), ())), preferred_element_type=F32)


def tn(left, right):
    return lax.dot_general(left, right, (((0,), (0,)), ((), ())), preferred_element_type=F32)


VM = pl.BlockSpec(memory_space=pltpu.VMEM)
SM = pl.BlockSpec(memory_space=pltpu.SMEM)
HB = pl.BlockSpec(memory_space=pl.ANY)


def launch(
    body, ins, outs, scratch=(), grid=None, alias=None, gflop=1.0, name=None, after=(), prefetch=()
):
    ahead, count, extra = len(prefetch), len(ins), len(after)

    def trimmed(*refs):
        body(*refs[: ahead + count], *refs[ahead + count + extra :])

    params = dict(
        out_shape=[o for o, _ in outs],
        input_output_aliases={ahead + k: v for k, v in (alias or {}).items()},
        compiler_params=pltpu.CompilerParams(vmem_limit_bytes=VMEM_LIMIT),
        cost_estimate=pl.CostEstimate(
            flops=int(gflop * 1e10), bytes_accessed=1 << 22, transcendentals=0
        ),
        name=name,
    )
    specs = dict(
        grid=grid if grid is not None else (),
        in_specs=[s for _, s in ins] + [HB] * extra,
        out_specs=[s for _, s in outs],
        scratch_shapes=list(scratch),
    )
    if ahead:
        specs = dict(grid_spec=pltpu.PrefetchScalarGridSpec(num_scalar_prefetch=ahead, **specs))
    return pl.pallas_call(trimmed, **params, **specs)(*prefetch, *[a for a, _ in ins], *after)


def shape(dims, dtype):
    return jax.ShapeDtypeStruct(tuple(dims), dtype)


def weight_scratch(name, width):
    if name == "shrink":
        return pltpu.VMEM((4, 2, 2, 4, width // 16, width), BF)
    return pltpu.VMEM((4, 2, 2, width // 16, width * COUNTS[name]), BF)


class Held:
    def __init__(self, arrays, start=0):
        self.arrays, self.start = list(arrays), start

    def ins(self):
        return [(a, HB) for a in self.arrays]


def load(name, held, refs, scratch, me, sem):
    if len(refs) == 1 and refs[0].shape == scratch.shape:
        pltpu.make_async_copy(refs[0], scratch, sem).start()
        return
    count = COUNTS[name]
    piece = refs[0].shape[-1]

    def columns(y, p):
        if name == "shrink":
            return pl.ds(pl.multiple_of(y * piece, 128), piece)
        return pl.ds(pl.multiple_of((y * count + p) * piece, 128), piece)

    for p in range(count):
        if len(refs) == 1:
            for y in range(2):
                src = refs[0].at[:, :, :, y, held.start + p]
                cols = columns(y, p)
                dst = scratch.at[:, :, :, p, :, cols] if name == "shrink" else scratch.at[:, :, :, :, cols]
                pltpu.make_async_copy(src, dst, sem).start()
            continue
        for k in range(4):
            for b in range(2):
                x, y, c = me[1] ^ (k & 1), me[3] ^ (k >> 1), me[2] ^ b
                src = refs[k * 2 + b].at[:, held.start + p]
                cols = columns(y, p)
                dst = scratch.at[:, x, c, p, :, cols] if name == "shrink" else scratch.at[:, x, c, :, cols]
                pltpu.make_async_copy(src, dst, sem).start()


def arrived(scratch, sem):
    pltpu.make_async_copy(scratch, scratch, sem).wait()


def store(name, scratch, outs, start, me, sem):
    if len(outs) == 1 and outs[0].shape == scratch.shape:
        pltpu.make_async_copy(scratch, outs[0], sem).start()
        return
    count = COUNTS[name]
    piece = outs[0].shape[-1]
    if len(outs) == 1:
        for y in range(2):
            for p in range(count):
                src = scratch.at[:, :, :, p, :, pl.ds(y * piece, piece)]
                pltpu.make_async_copy(src, outs[0].at[:, :, :, y, p], sem).start()
        return
    for b in range(2):
        c = me[2] ^ b
        for y in range(2):
            for p in range(count):
                if name == "shrink":
                    src = scratch.at[:, :, c, p, :, pl.ds(y * piece, piece)]
                else:
                    src = scratch.at[:, :, c, :, pl.ds((y * count + p) * piece, piece)]
                pltpu.make_async_copy(src, outs[b].at[:, :, y, start + p], sem).start()


def flat(block):
    return block.reshape(-1, block.shape[-1])


def put_rows(scratch, value, cols):
    scratch[:, :, :, :, cols] = value.reshape(scratch.shape[:4] + (value.shape[-1],))


def normed(values, gain):
    r = lax.rsqrt(jnp.mean(values * values, axis=-1, keepdims=True) + EPS)
    return values * r * gain


def norm_back(values, gain, grad):
    r = lax.rsqrt(jnp.mean(values * values, axis=-1, keepdims=True) + EPS)
    inner = jnp.mean(values * gain * grad, axis=-1, keepdims=True)
    back = r * gain * grad - values * (r * r * r * inner)
    return back, jnp.sum(grad * values * r, axis=0, keepdims=True)


def prepare_kernel(lens, x, cot, gains, buckets, table, n1, kept, bias):
    rows = cot.shape[1]
    for s in range(x.shape[0]):
        values = x[s].astype(F32)
        n1[s * rows : (s + 1) * rows, :] = normed(values, gains[0:1, :]).astype(BF)
        keep = lax.broadcasted_iota(jnp.int32, (rows, 1), 0) < lens[s]
        kept[s * rows : (s + 1) * rows, :] = jnp.where(keep, cot[s].astype(F32), 0.0).astype(BF)
    half = 128
    heads = 2 * bias.shape[0]

    @pl.loop(0, rows // 8)
    def _(step):
        start = pl.multiple_of(step * 8, 8)
        for side in range(rows // half):
            which = buckets[pl.ds(start, 8), side * half : (side + 1) * half]
            key = start + lax.broadcasted_iota(jnp.int32, (8, half), 0)
            query = side * half + lax.broadcasted_iota(jnp.int32, (8, half), 1)
            for h in range(heads):
                row = jnp.broadcast_to(table[h : h + 1, :], (8, half))
                found = jnp.take_along_axis(row, which, axis=1)
                at = (h % 2) * rows + side * half
                bias[h // 2, pl.ds(start, 8), at : at + half] = jnp.where(
                    key <= query, found, NEGATIVE
                )


CHUNK = 32


def stacked(block):
    lane = lax.broadcasted_iota(jnp.int32, block.shape, 1)
    zero = jnp.zeros_like(block)
    return jnp.concatenate((jnp.where(lane < DH, block, zero), jnp.where(lane < DH, zero, block)))


def unstacked(block):
    queries = block.shape[1] // 2
    return jnp.concatenate((block[:DH, :queries], block[DH:, queries:]), axis=0).T


def folded(block, by):
    return by(block.reshape(block.shape[0] // 8, 8, block.shape[1]), axis=0)


def chunks(size):
    return [slice(at, at + CHUNK) for at in range(0, size, CHUNK)]


def forward_units(units, size, fix):
    for query, keys, values, scores, probs, mixed, logsum, which in units:
        scores[:size] = nt(keys, stacked(query * jnp.asarray(SCALE, BF)))
    for query, keys, values, scores, probs, mixed, logsum, which in units:
        top = None
        for part in chunks(size):
            block, changed = fix(scores[part], part, which)
            if changed:
                scores[part] = block
            block = folded(block, jnp.max)
            top = block if top is None else jnp.maximum(top, block)
        highest = jnp.max(top, axis=0, keepdims=True)
        total = jnp.zeros((8, highest.shape[1]), F32)
        for part in chunks(size):
            weights = jnp.exp(scores[part] - highest)
            total = total + folded(weights, jnp.sum)
            probs[part] = weights.astype(BF)
        total = jnp.sum(total, axis=0, keepdims=True)
        logsum[...] = highest + jnp.log(total)
        mixed[...] = unstacked(tn(values, probs[:size]) * (1.0 / total)).astype(BF)


def backward_units(units, size, fix):
    for query, keys, values, grad, mixed, logsum, scores, slopes, probs, grads, outs, which in units:
        scores[:size] = nt(keys, stacked(query * jnp.asarray(SCALE, BF)))
        slopes[:size] = nt(values, stacked(grad))
    for query, keys, values, grad, mixed, logsum, scores, slopes, probs, grads, outs, which in units:
        product = stacked(grad.astype(F32) * mixed.astype(F32))
        high = product.astype(BF)
        low = (product - high.astype(F32)).astype(BF)
        ones = jnp.ones((8, product.shape[1]), BF)
        inner = (nt(ones, high) + nt(ones, low))[0:1]
        for part in chunks(size):
            block, keep = fix(scores[part], part, which)
            weights = jnp.exp(block - logsum[...])
            if keep is not None:
                weights = jnp.where(keep, weights, 0.0)
            probs[part] = weights.astype(BF)
            grads[part] = (weights * (slopes[part] - inner)).astype(BF)
        left = grads[:size]
        outs[0][...] = (unstacked(tn(keys, left)) * SCALE).astype(BF)
        outs[1][...] = nn(left, stacked(query * jnp.asarray(SCALE, BF))).astype(BF)
        outs[2][...] = nn(probs[:size], stacked(grad)).astype(BF)


def self_units(length):
    return [(slice(s * length, (s + 1) * length), slice(j * 128, (j + 1) * 128), s, j) for s in range(2) for j in range(2)]


def self_forward_kernel(query, keys, values, bias, mixed, logsum, scores, probs):
    length = bias.shape[1]
    units = []
    for rows, cols, s, j in self_units(length):
        u = s * 2 + j
        units.append(
            (
                query[rows, cols],
                keys[rows, cols],
                values[rows, cols],
                scores.at[u],
                probs.at[u],
                mixed.at[rows, cols],
                logsum.at[j, s],
                j,
            )
        )
    forward_units(units, length, lambda block, part, j: (block + bias[j, part, :], True))


def self_backward_kernel(
    query, keys, values, grad, mixed, bias, logsum, gq, gk, gv, grad_bias, scores, slopes, probs, grads
):
    length = bias.shape[1]
    units = []
    for rows, cols, s, j in self_units(length):
        u = s * 2 + j
        units.append(
            (
                query[rows, cols],
                keys[rows, cols],
                values[rows, cols],
                grad[rows, cols],
                mixed[rows, cols],
                logsum.at[j, s],
                scores.at[u],
                slopes.at[u],
                probs.at[u],
                grads.at[u],
                (gq.at[rows, cols], gk.at[rows, cols], gv.at[rows, cols]),
                j,
            )
        )
    backward_units(units, length, lambda block, part, j: (block + bias[j, part, :], None))
    for j in range(2):
        for part in chunks(length):
            grad_bias[j, part, :] = grads[j, part, :].astype(F32) + grads[2 + j, part, :].astype(F32)


def last_tile(valid, size, part, block):
    if part.start < size - KEY_TILE:
        return None
    return part.start + lax.broadcasted_iota(jnp.int32, block.shape, 0) < valid


def cross_forward_kernel(lens, query, keys, values, mixed, logsum, scores, probs):
    valid = lens[pl.program_id(0)]
    for tiles in range(1, keys.shape[0] // KEY_TILE + 1):

        @pl.when((valid + KEY_TILE - 1) // KEY_TILE == tiles)
        def _():
            size = tiles * KEY_TILE

            def fix(block, part, which):
                keep = last_tile(valid, size, part, block)
                if keep is None:
                    return block, False
                return jnp.where(keep, block, NEGATIVE), True

            units = []
            for j in range(2):
                cols = slice(j * 128, (j + 1) * 128)
                units.append(
                    (
                        query[:, cols],
                        keys[:size, cols],
                        values[:size, cols],
                        scores.at[j],
                        probs.at[j],
                        mixed.at[:, cols],
                        logsum.at[j, 0],
                        None,
                    )
                )
            forward_units(units, size, fix)


def cross_backward_kernel(
    lens, query, keys, values, grad, mixed, logsum, gq, gk, gv, scores, slopes, probs, grads
):
    valid = lens[pl.program_id(0)]
    for tiles in range(1, keys.shape[0] // KEY_TILE + 1):

        @pl.when((valid + KEY_TILE - 1) // KEY_TILE == tiles)
        def _():
            size = tiles * KEY_TILE
            units = []
            for j in range(2):
                cols = slice(j * 128, (j + 1) * 128)
                units.append(
                    (
                        query[:, cols],
                        keys[:size, cols],
                        values[:size, cols],
                        grad[:, cols],
                        mixed[:, cols],
                        logsum.at[j, 0],
                        scores.at[j],
                        slopes.at[j],
                        probs.at[j],
                        grads.at[j],
                        (gq.at[:, cols], gk.at[:size, cols], gv.at[:size, cols]),
                        None,
                    )
                )
            backward_units(
                units,
                size,
                lambda block, part, which: (block, last_tile(valid, size, part, block)),
            )


def attend_scratch(units, keys, queries, backward):
    wide = pltpu.VMEM((units, keys, 2 * queries), F32)
    thin = pltpu.VMEM((units, keys, 2 * queries), BF)
    return [wide, wide, thin, thin] if backward else [wide, thin]


def pair_spec(rows, base=0):
    return pl.BlockSpec((rows, 256), lambda s, p: (s, base + p))


def both_spec(rows, base=0):
    return pl.BlockSpec((rows, 256), lambda p: (0, base + p))


def inward_kernel(held, me, n1, *rest):
    refs, (packed, weight, sem) = rest[: len(held.arrays)], rest[len(held.arrays) :]
    load("inward", held, refs, weight, me, sem)
    arrived(weight, sem)
    size = n1.shape[1]
    left = n1[...]
    for block in range(3):
        cols = slice(block * size, (block + 1) * size)
        packed[:, cols] = nn(left, flat(weight[..., cols])).astype(BF)


def outward_kernel(held, me, x, mixed, gains, *rest):
    refs, (after, n2, weight, sem) = rest[: len(held.arrays)], rest[len(held.arrays) :]
    load("outward", held, refs, weight, me, sem)
    arrived(weight, sem)
    values = x[...].astype(F32) + nn(mixed[...], flat(weight[...]))
    after[...] = values
    n2[...] = normed(values, gains[1:2, :]).astype(BF)


def memory_kernel(held_query, held_reader, me, lens, n2, encoded, *rest):
    k, both = len(held_query.arrays), len(held_query.arrays) + len(held_reader.arrays)
    refs_query, refs_reader = rest[:k], rest[k:both]
    asks, pairs, weight_query, weight_reader, sems = rest[both:]
    step = pl.program_id(0)
    tiles = pl.num_programs(0) // lens.shape[0]

    @pl.when(step == 0)
    def _():
        load("query", held_query, refs_query, weight_query, me, sems.at[0])
        load("reader", held_reader, refs_reader, weight_reader, me, sems.at[1])
        arrived(weight_query, sems.at[0])
        asks[...] = nn(n2[...], flat(weight_query[...])).astype(BF)
        arrived(weight_reader, sems.at[1])

    @pl.when(lax.rem(step, tiles) * encoded.shape[0] < lens[step // tiles])
    def _():
        size = encoded.shape[1]
        left = encoded[...]
        for block in range(2):
            cols = slice(block * size, (block + 1) * size)
            pairs[:, cols] = nn(left, flat(weight_reader[..., cols])).astype(BF)


def gelu_parts(v):
    phi = 0.5 * (1.0 + lax.erf(v * (0.5**0.5)))
    density = jnp.exp(-0.5 * v * v) * 0.3989422804014327
    return v * phi, phi + v * density


def widen_kernel(held_writer, held_expand, me, after_self, mixed, gains, kept, *rest):
    k, both = len(held_writer.arrays), len(held_writer.arrays) + len(held_expand.arrays)
    refs_writer, refs_expand = rest[:k], rest[k:both]
    outs = rest[both:]
    after_cross, n3, hidden, slope = outs[:4]
    grads, (weight_writer, weight_expand, shrink_grad, sems) = outs[4:-4], outs[-4:]
    load("writer", held_writer, refs_writer, weight_writer, me, sems.at[0])
    load("expand", held_expand, refs_expand, weight_expand, me, sems.at[1])
    arrived(weight_writer, sems.at[0])
    values = after_self[...] + nn(mixed[...], flat(weight_writer[...]))
    after_cross[...] = values
    n3[...] = normed(values, gains[2:3, :]).astype(BF)
    arrived(weight_expand, sems.at[1])
    size = n3.shape[1]

    for z in range(4):
        cols = slice(z * size, (z + 1) * size)
        before = nn(n3[...], flat(weight_expand[:, :, :, :, cols]))
        active, gate = gelu_parts(before)
        active = active.astype(BF)
        hidden[:, cols] = active
        slope[:, cols] = gate.astype(BF)
        grad = tn(active, kept[...]).astype(BF)
        shrink_grad[z] = grad.reshape(shrink_grad.shape[1:])

    store("shrink", shrink_grad, grads, 0, me, sems.at[2])
    arrived(shrink_grad, sems.at[2])


def narrow_kernel(
    held_shrink, held_expand, me, lens, n3, kept, gains, after_hbm, hidden_hbm, slope_hbm, *rest
):
    k, both = len(held_shrink.arrays), len(held_shrink.arrays) + len(held_expand.arrays)
    refs_shrink, refs_expand = rest[:k], rest[k:both]
    outs = rest[both:]
    layer_out, grad_cross, gain_part = outs[:3]
    grads, scratch = outs[3:-8], outs[-8:]
    weight_shrink, weight_expand, expand_grad, grad_wide, after_cross, hidden, slope, sems = scratch
    load("shrink", held_shrink, refs_shrink, weight_shrink, me, sems.at[0])
    pltpu.make_async_copy(slope_hbm, slope, sems.at[3]).start()
    load("expand", held_expand, refs_expand, weight_expand, me, sems.at[1])
    pltpu.make_async_copy(hidden_hbm, hidden, sems.at[4]).start()
    pltpu.make_async_copy(after_hbm, after_cross, sems.at[5]).start()
    size = n3.shape[1]
    arrived(weight_shrink, sems.at[0])
    arrived(slope, sems.at[3])
    for z in range(4):
        cols = slice(z * size, (z + 1) * size)
        grad_wide[:, cols] = (
            slope[:, cols].astype(F32) * nt(kept[...], flat(weight_shrink[z]))
        ).astype(BF)
    turned = n3[...].T
    for z in range(4):
        cols = slice(z * size, (z + 1) * size)
        put_rows(expand_grad, nn(turned, grad_wide[:, cols]).astype(BF), cols)
    store("expand", expand_grad, grads, 0, me, sems.at[2])
    arrived(hidden, sems.at[4])
    arrived(after_cross, sems.at[5])
    total = after_cross[...] + nn(hidden[...], flat(weight_shrink[...]))
    rows = total.shape[0] // lens.shape[0]
    for s in range(lens.shape[0]):
        part = slice(s * rows, (s + 1) * rows)
        keep = lax.broadcasted_iota(jnp.int32, (rows, 1), 0) < lens[s]
        layer_out[s] = jnp.where(keep, total[part, :], 0.0).astype(BF)
    arrived(weight_expand, sems.at[1])
    grad_norm = nt(grad_wide[...], flat(weight_expand[...]))
    back, gain = norm_back(after_cross[...], gains[2:3, :], grad_norm)
    grad_cross[...] = kept[...].astype(F32) + back
    gain_part[...] = gain
    arrived(expand_grad, sems.at[2])


def writer_back_kernel(held, me, grad_cross, mixed, *rest):
    k = len(held.arrays)
    refs, outs = rest[:k], rest[k:]
    grad_mixed, grads, (weight, grad_scratch, sems) = outs[0], outs[1:-3], outs[-3:]
    load("writer", held, refs, weight, me, sems.at[0])
    branch = grad_cross[...].astype(BF)
    put_rows(grad_scratch, tn(mixed[...], branch).astype(BF), slice(None))
    store("writer", grad_scratch, grads, 0, me, sems.at[1])
    arrived(weight, sems.at[0])
    grad_mixed[...] = nt(branch, flat(weight[...])).astype(BF)
    arrived(grad_scratch, sems.at[1])


def query_back_kernel(
    packed_mode,
    held_query,
    held_out,
    me,
    grad_asks,
    n2,
    gains,
    after_hbm,
    cross_hbm,
    mixed_hbm,
    *rest,
):
    k, both = len(held_query.arrays), len(held_query.arrays) + len(held_out.arrays)
    refs_query, refs_out = rest[:k], rest[k:both]
    rest = rest[both:]
    grad_self, grad_mixed, gain_part = rest[:3]
    weight_query, weight_out, query_grad, out_grad, after_self, grad_cross, mixed, sems = rest[-8:]
    grads = rest[3:-8]
    load("query", held_query, refs_query, weight_query, me, sems.at[0])
    pltpu.make_async_copy(after_hbm, after_self, sems.at[4]).start()
    pltpu.make_async_copy(cross_hbm, grad_cross, sems.at[5]).start()
    load("outward", held_out, refs_out, weight_out, me, sems.at[1])
    pltpu.make_async_copy(mixed_hbm, mixed, sems.at[6]).start()
    put_rows(query_grad, tn(n2[...], grad_asks[...]).astype(BF), slice(None))
    store("query", query_grad, grads if packed_mode else grads[:1], 0, me, sems.at[2])
    arrived(weight_query, sems.at[0])
    arrived(after_self, sems.at[4])
    back, gain = norm_back(
        after_self[...], gains[1:2, :], nt(grad_asks[...], flat(weight_query[...]))
    )
    arrived(grad_cross, sems.at[5])
    total = grad_cross[...] + back
    grad_self[...] = total
    gain_part[...] = gain
    branch = total.astype(BF)
    arrived(weight_out, sems.at[1])
    grad_mixed[...] = nt(branch, flat(weight_out[...])).astype(BF)
    arrived(mixed, sems.at[6])
    put_rows(out_grad, tn(mixed[...], branch).astype(BF), slice(None))
    store("outward", out_grad, grads if packed_mode else grads[1:], 1, me, sems.at[3])
    arrived(query_grad, sems.at[2])
    arrived(out_grad, sems.at[3])


def inward_grad_kernel(me, n1, gq, gk, gv, *rest):
    grads, (scratch, sem) = rest[:-2], rest[-2:]
    size = n1.shape[1]
    turned = n1[...].T
    for block, grad in enumerate((gq, gk, gv)):
        cols = slice(block * size, (block + 1) * size)
        put_rows(scratch, nn(turned, grad[...]).astype(BF), cols)
    store("inward", scratch, grads, 0, me, sem)
    arrived(scratch, sem)


def inputs_grad_kernel(held, me, gq, gk, gv, gains, x_hbm, self_hbm, *rest):
    k = len(held.arrays)
    refs, (out, gain_part, weight, x, grad_self, sems) = rest[:k], rest[k:]
    load("inward", held, refs, weight, me, sems.at[0])
    pltpu.make_async_copy(x_hbm, x, sems.at[1]).start()
    pltpu.make_async_copy(self_hbm, grad_self, sems.at[2]).start()
    arrived(weight, sems.at[0])
    size = gq.shape[1]
    total = 0.0
    for block, grad in enumerate((gq, gk, gv)):
        cols = slice(block * size, (block + 1) * size)
        total = total + nt(grad[...], flat(weight[..., cols]))
    arrived(x, sems.at[1])
    arrived(grad_self, sems.at[2])
    back, gain = norm_back(x[...].astype(F32), gains[0:1, :], total)
    out[...] = grad_self[...] + back
    gain_part[...] = gain


def reader_grad_kernel(me, lens, encoded, gk, gv, *rest):
    grads, (scratch, total, sem) = rest[:-3], rest[-3:]
    step = pl.program_id(0)
    size = encoded.shape[1]
    valid = lens[step]
    for tiles in range(1, encoded.shape[0] // KEY_TILE + 1):

        @pl.when((valid + KEY_TILE - 1) // KEY_TILE == tiles)
        def _():
            rows = tiles * KEY_TILE
            turned = encoded[:rows].T
            for block, grad in enumerate((gk, gv)):
                cols = slice(block * size, (block + 1) * size)
                before = jnp.where(step == 0, 0.0, total[:, cols])
                total[:, cols] = before + nn(turned, grad[:rows])

    @pl.when(step == pl.num_programs(0) - 1)
    def _():
        put_rows(scratch, total[...].astype(BF), slice(None))
        store("reader", scratch, grads, 0, me, sem)
        arrived(scratch, sem)


def encoded_grad_kernel(held, me, lens, gk, gv, *rest):
    refs, (out, weight, sem) = rest[: len(held.arrays)], rest[len(held.arrays) :]
    step = pl.program_id(0)
    steps = pl.num_programs(0) // lens.shape[0]
    height, size = gk.shape
    left = lens[step // steps] - lax.rem(step, steps) * height

    @pl.when(step == 0)
    def _():
        load("reader", held, refs, weight, me, sem)
        arrived(weight, sem)

    for tiles in range(1, height // KEY_TILE + 1):
        rows = tiles * KEY_TILE
        last = tiles == height // KEY_TILE
        fits = left > rows - KEY_TILE

        @pl.when(fits if last else jnp.logical_and(fits, left <= rows))
        def _():
            out[:rows] = nt(gk[:rows], flat(weight[..., :size])) + nt(
                gv[:rows], flat(weight[..., size:])
            )
            if rows < height:
                out[rows:] = jnp.zeros((height - rows, size), F32)

    @pl.when(left <= 0)
    def _():
        out[...] = jnp.zeros_like(out)


def table_kernel(count, buckets, grad_bias, out, hot):
    pairs, length = grad_bias.shape[:2]
    group = hot.shape[0]
    lane = lax.broadcasted_iota(jnp.int32, out.shape, 1)

    def one(step, total):
        for k in range(group):
            hot[k] = jnp.where(buckets[...] == step * group + k, 1.0, 0.0)
        rows = [[] for _ in range(group)]
        for h in range(2 * pairs):
            cols = slice((h % 2) * length, (h % 2 + 1) * length)
            sums = [jnp.zeros((8, length), F32) for _ in range(group)]
            for part in chunks(length):
                value = grad_bias[h // 2, part, cols]
                for k in range(group):
                    sums[k] = sums[k] + folded(hot[k, part] * value, jnp.sum)
            for k in range(group):
                rows[k].append(jnp.sum(sums[k], axis=0, keepdims=True))
        for k in range(group):
            value = jnp.sum(jnp.concatenate(rows[k], axis=0), axis=1, keepdims=True)
            total = total + jnp.where(lane == step * group + k, value, 0.0)
        return total

    out[...] = lax.fori_loop(0, count // group, one, jnp.zeros(out.shape, F32))


def shared_places(widths, piece, width):
    starts = [0]
    for w in widths:
        starts.append(starts[-1] + w // piece)
    return starts[:-1], starts[-1], starts[-1] + 1, starts[-1] + 1 + 3 * (width // piece)


def statistics_kernel(piece, *refs):
    grads, gains, table, rows, shared = refs[:7], refs[7:10], refs[10], refs[11], refs[12]
    width = gains[0].shape[1]
    starts, totals_at, gains_at, table_at = shared_places([g.shape[1] for g in grads], piece, width)
    rows[...] = jnp.zeros_like(rows)
    shared[...] = jnp.zeros_like(shared)
    lane = lax.broadcasted_iota(jnp.int32, (1, 128), 1)
    lane_piece = lax.broadcasted_iota(jnp.int32, (1, piece), 1)
    totals = jnp.zeros((1, piece), F32)
    for j, grad in enumerate(grads):
        square = grad[...] * grad[...]
        count, wide = square.shape
        sums = jnp.sum(square, axis=1, keepdims=True)
        rows[:count, :] += jnp.where(lane == j, sums, 0.0)
        columns = jnp.sum(square, axis=0, keepdims=True)
        for p in range(wide // piece):
            at = starts[j] + p
            shared[at : at + 1, :] = columns[:, p * piece : (p + 1) * piece]
        totals = totals + jnp.where(lane_piece == j, jnp.sum(sums, axis=0, keepdims=True), 0.0)
    shared[totals_at : totals_at + 1, :] = totals
    for k in range(3):
        for p in range(width // piece):
            at = gains_at + k * (width // piece) + p
            shared[at : at + 1, :] = gains[k][:, p * piece : (p + 1) * piece]
    keep = min(piece, table.shape[1])
    shared[table_at : table_at + table.shape[0], :keep] = table[:, :keep]


def steps_kernel(wide, narrow, *refs):
    grads, rows, shared = refs[:7], refs[7], refs[8]
    outs = refs[9:]
    piece = shared.shape[1]
    starts, totals_at, _, _ = shared_places([g.shape[1] for g in grads], piece, piece)
    turned = rows[...].T
    for j, grad in enumerate(grads):
        step, row_out, col_out = outs[3 * j : 3 * j + 3]
        count, width = grad.shape
        full_rows, full_cols = count * wide, width * narrow
        row = rows[:count, j : j + 1] / full_cols + TINY
        mean = shared[totals_at : totals_at + 1, j : j + 1] / (full_rows * full_cols) + TINY
        cols = []
        for p in range(width // piece):
            at = starts[j] + p
            part = slice(p * piece, (p + 1) * piece)
            col = shared[at : at + 1, :] / full_rows + TINY
            step[:, part] = grad[:, part] * lax.rsqrt(row * col / mean)
            cols.append(col)
        row_out[...] = (turned[j : j + 1, :count] / full_cols + TINY).reshape(count)
        col = cols[0] if len(cols) == 1 else jnp.concatenate(cols, axis=1)
        col_out[...] = col.reshape(width)


def tie(value, after):
    after = tuple(after)
    return lax.optimization_barrier((value,) + after)[0] if after else value


def join(gathers, arrays=()):
    keys = [(g, key) for g in gathers for key in g.live]
    flat_values, tree = jax.tree.flatten(([g.live[key] for g, key in keys], list(arrays)))
    values, arrays = jax.tree.unflatten(tree, lax.optimization_barrier(tuple(flat_values)))
    for (g, key), value in zip(keys, values):
        g.live[key] = value
    return arrays


class Hyper:
    MASKS = {"y": 1, "c": 2, "x": 4, "xy": 5, "z1": 8, "z2": 16, "z3": 24}

    def __init__(self):
        wide = lax.axis_index("wide")
        self.z, self.x, self.c = wide // 4, (wide // 2) % 2, wide % 2
        self.y = lax.axis_index("narrow")
        self.me = jnp.stack((self.z, self.x, self.c, self.y)).astype(jnp.int32)

    def swap(self, value, bit, after=()):
        mask = self.MASKS[bit]
        return lax.ppermute(tie(value, after), BOTH, [(i, i ^ mask) for i in range(32)])


class Gather:
    def __init__(self, hyper, shards, plan, width):
        self.hyper, self.plan = hyper, plan
        self.live = {"own": jnp.stack([cut(name, shards[name], width)[p] for name, p in plan])}

    def z(self):
        own = self.live["own"]
        self.live["others"] = [self.hyper.swap(own, bit) for bit in ("z1", "z2", "z3")]

    def z1(self):
        self.live["other"] = self.hyper.swap(self.live["own"], "z1")

    def z2(self):
        h = self.hyper
        own, other = self.live.pop("own"), self.live.pop("other")
        pair = jnp.where(h.z % 2 == 0, jnp.stack((own, other)), jnp.stack((other, own)))
        self.live["own"], self.live["other"] = pair, h.swap(pair, "z2")

    def plane(self):
        h = self.hyper
        own = self.live.pop("own")
        if "others" in self.live:
            one, two, three = self.live.pop("others")
            even = h.z % 2 == 0
            own = jnp.where(even, jnp.stack((own, one)), jnp.stack((one, own)))
            other = jnp.where(even, jnp.stack((two, three)), jnp.stack((three, two)))
        else:
            other = self.live.pop("other")
        quad = jnp.where(
            h.z // 2 == 0, jnp.concatenate((own, other)), jnp.concatenate((other, own))
        )
        self.live["quads"] = [quad] + [h.swap(quad, bit) for bit in ("x", "y", "xy")]

    def core_own(self):
        self.live["first"] = self.hyper.swap(self.live["quads"][0], "c")

    def core(self):
        self.live["cores"] = [self.live.pop("first")] + [
            self.hyper.swap(quad, "c") for quad in self.live["quads"][1:]
        ]

    def held(self, name):
        arrays = [a for two in zip(self.live["quads"], self.live["cores"]) for a in two]
        return Held(arrays, self.plan.index((name, 0)))


def fold_kernel(counts, joint, names, me, *refs):
    na, nb, nj = counts
    first, second, both, outs = refs[:na], refs[na : na + nb], refs[na + nb : na + nb + nj], refs[na + nb + nj :]
    pa = first[0].shape[3]

    def add(parts, part):
        return sum([r[...].astype(F32) for r in parts] + [r[:, :, :, part].astype(F32) for r in both])

    one = add(first, slice(0, pa))
    two = add(second, slice(pa, None))
    if names:
        pieces = [one[0, 0, 0, p] for p in range(one.shape[3])]
        pieces += [two[0, 0, 0, p] for p in range(two.shape[3])]
        for out, (name, start) in zip(outs, names):
            for p in range(COUNTS[name]):
                piece = pieces[start + p]
                if name == "shrink":
                    out[p * piece.shape[0] : (p + 1) * piece.shape[0], :] = piece
                else:
                    out[:, p * piece.shape[1] : (p + 1) * piece.shape[1]] = piece
    elif joint:
        outs[0][:, :, :, :pa] = one.astype(outs[0].dtype)
        outs[0][:, :, :, pa:] = two.astype(outs[0].dtype)
    else:
        outs[0][...] = one.astype(outs[0].dtype)
        outs[1][...] = two.astype(outs[1].dtype)


class HalvedScatter:
    def __init__(self, hyper, first, second, name):
        self.hyper, self.halves, self.name = hyper, (first, second), name
        self.parts = [[], []]
        self.joint = []
        self.sizes = [half[0].shape[3] for half in (first, second)]
        self.block = first[0].shape[4:]

    def core(self, half, after=()):
        keep, send = self.halves[half]
        recv = self.hyper.swap(send, "c", after)
        self.parts[half] = [keep, recv]
        return [recv]

    def fold(self, picks, out_dims, joint, after, step):
        ins = []
        for half in range(2):
            p = self.sizes[half]
            for array, (dims, index) in zip(self.parts[half], picks[half]):
                spec = pl.BlockSpec(
                    tuple(dims) + (p,) + self.block,
                    lambda i, me, index=index: tuple(index(me)) + (0, 0, 0),
                )
                ins.append((array, spec))
        whole = sum(self.sizes)
        for array, index in zip(self.joint, picks[2]):
            spec = pl.BlockSpec(
                (1, 1, 1, whole) + self.block,
                lambda i, me, index=index: (index(me), 0, 0, 0, 0, 0),
            )
            ins.append((array, spec))
        outs = []
        rows, cols = self.block
        for dims, kind in out_dims:
            if isinstance(dims, str):
                count = COUNTS[dims]
                full = (count * rows, cols) if dims == "shrink" else (rows, count * cols)
                outs.append((shape(full, F32), pl.BlockSpec(full, lambda i, me: (0, 0))))
                continue
            p = whole if joint else self.sizes[len(outs)]
            full = tuple(dims) + (p,) + self.block
            outs.append((shape(full, kind), pl.BlockSpec(full, lambda i, me: (0,) * 6)))
        counts = (len(self.parts[0]), len(self.parts[1]), len(self.joint))
        names = out_dims if step == "last" else None
        self.sent = launch(
            functools.partial(fold_kernel, counts, joint, names),
            ins,
            outs,
            grid=(1,),
            gflop=1.0,
            name=f"{self.name}_{step}",
            after=after,
            prefetch=(self.hyper.me,),
        )
        return self.sent

    def p1(self, after=()):
        a = [((4, 2, 1), lambda me: (0, 0, 1 - me[3]))] * 2
        b = [((4, 1, 2), lambda me: (0, 1 - me[1], 0))] * 2
        sent = self.fold((a, b, ()), (((4, 2, 1), BF), ((4, 1, 2), BF)), False, after, "p1")
        recv = [self.hyper.swap(value, bit) for value, bit in zip(sent, "yx")]
        for half in range(2):
            self.parts[half].append(recv[half])
        return recv

    def p2(self, after=()):
        four = (4, 1, 1)
        a = [(four, lambda me: (0, 1 - me[1], me[3]))] * 2
        a += [(four, lambda me: (0, 1 - me[1], 0))]
        b = [(four, lambda me: (0, me[1], 1 - me[3]))] * 2
        b += [(four, lambda me: (0, 0, 1 - me[3]))]
        sent = self.fold((a, b, ()), ((four, BF), (four, BF)), False, after, "p2")
        recv = [self.hyper.swap(value, bit) for value, bit in zip(sent, "xy")]
        for half in range(2):
            self.parts[half].append(recv[half])
        return recv

    def own(self, count, place):
        dims = (count, 1, 1)
        a = [(dims, lambda me: (place(me), me[1], me[3]))] * 2
        a += [(dims, lambda me: (place(me), me[1], 0)), (dims, lambda me: (place(me), 0, 0))]
        b = [(dims, lambda me: (place(me), me[1], me[3]))] * 2
        b += [(dims, lambda me: (place(me), 0, me[3])), (dims, lambda me: (place(me), 0, 0))]
        return a, b

    def z2(self, after=()):
        a, b = self.own(2, lambda me: 1 - me[0] // 2)
        (sent,) = self.fold((a, b, ()), (((2, 1, 1), BF),), True, after, "z2")
        recv = self.hyper.swap(sent, "z2")
        self.joint.append(recv)
        return [recv]

    def z1(self, after=()):
        a, b = self.own(1, lambda me: (me[0] // 2) * 2 + 1 - lax.rem(me[0], 2))
        j = [lambda me: 1 - lax.rem(me[0], 2)]
        (sent,) = self.fold((a, b, j), (((1, 1, 1), BF),), True, after, "z1")
        recv = self.hyper.swap(sent, "z1")
        self.joint.append(recv)
        return [recv]

    def last(self, weights, after=()):
        a, b = self.own(1, lambda me: me[0])
        j = [lambda me: lax.rem(me[0], 2), lambda me: 0]
        return self.fold((a, b, j), weights, True, after, "last")


def plane_kernel(me, *refs):
    groups, outs = refs[:-4], refs[-4:]
    for k, out in enumerate(outs):
        x, y = me[1] ^ (k & 1), me[3] ^ (k >> 1)
        at = 0
        for keep, recv in zip(groups[::2], groups[1::2]):
            total = keep[:, x, y].astype(F32) + recv[:, x, y].astype(F32)
            out[:, at : at + total.shape[1]] = total.astype(out.dtype)
            at += total.shape[1]


def line_kernel(me, own, one, two, three, *outs):
    for k, out in enumerate(outs):
        z = me[0] ^ k
        total = own[z] + one[z].astype(F32) + two[z].astype(F32) + three[z].astype(F32)
        out[...] = total.astype(out.dtype)


def last_kernel(names, own, one, two, three, *outs):
    total = own[...] + one[...].astype(F32) + two[...].astype(F32) + three[...].astype(F32)
    at = 0
    for out, name in zip(outs, names):
        for p in range(COUNTS[name]):
            piece = total[at + p]
            if name == "shrink":
                out[p * piece.shape[0] : (p + 1) * piece.shape[0], :] = piece
            else:
                out[:, p * piece.shape[1] : (p + 1) * piece.shape[1]] = piece
        at += COUNTS[name]


class Scatter:
    def __init__(self, hyper, name, weights):
        self.hyper, self.name, self.weights = hyper, name, weights
        self.groups = []

    def core(self, keep, send):
        self.groups.append((keep, self.hyper.swap(send, "c")))

    def plane(self, after=()):
        count = sum(keep.shape[3] for keep, _ in self.groups)
        block = self.groups[0][0].shape[4:]
        dims = (4, count) + block
        self.own, *sent = launch(
            plane_kernel,
            [(self.hyper.me, SM)] + [(a, VM) for group in self.groups for a in group],
            [(shape(dims, F32), VM)] + [(shape(dims, BF), VM)] * 3,
            name=self.name + "_plane",
            after=after,
        )
        self.sent = sent
        self.got = [self.hyper.swap(a, bit) for a, bit in zip(sent, ("x", "y", "xy"))]

    def line(self, after=()):
        dims = self.own.shape[1:]
        self.own, *sent = launch(
            line_kernel,
            [(self.hyper.me, SM), (self.own, VM)] + [(a, VM) for a in self.got],
            [(shape(dims, F32), VM)] + [(shape(dims, BF), VM)] * 3,
            name=self.name + "_line",
            after=after,
        )
        self.sent = sent
        self.got = [self.hyper.swap(a, bit) for a, bit in zip(sent, ("z1", "z2", "z3"))]

    def last(self, after=()):
        rows, cols = self.own.shape[1:]
        outs = []
        for name in self.weights:
            count = COUNTS[name]
            full = (count * rows, cols) if name == "shrink" else (rows, count * cols)
            outs.append((shape(full, F32), VM))
        totals = launch(
            functools.partial(last_kernel, self.weights),
            [(self.own, VM)] + [(a, VM) for a in self.got],
            outs,
            name=self.name + "_last",
            after=after,
        )
        self.sent = totals
        return dict(zip(self.weights, totals))


def cut(name, shard, width):
    count = COUNTS[name]
    if name == "shrink":
        return shard.reshape(count, shard.shape[0] // count, shard.shape[1])
    rows, cols = shard.shape
    return jnp.transpose(shard.reshape(rows, count, cols // count), (1, 0, 2))


def whole_shape(name, width):
    if name == "shrink":
        return (4, 2, 2, 4, width // 16, width)
    return (4, 2, 2, width // 16, width * COUNTS[name])


def local(
    inputs,
    encoded,
    target_lengths,
    memory_lengths,
    buckets,
    cotangent,
    self_inward,
    self_outward,
    cross_query,
    cross_reader,
    cross_writer,
    expand_weight,
    shrink_weight,
    norm_gains,
    bias_table,
):
    wide_count = lax.axis_size("wide")
    narrow_count = lax.axis_size("narrow")
    fast = (wide_count, narrow_count) == (16, 2)
    seqs, length, width = inputs.shape
    memory_size = encoded.shape[1]
    rows, mem_rows = seqs * length, seqs * memory_size
    wide_hidden = expand_weight.shape[1] * narrow_count
    shards = dict(
        zip(
            NAMES,
            (
                self_inward,
                self_outward,
                cross_query,
                cross_reader,
                cross_writer,
                expand_weight,
                shrink_weight,
            ),
        )
    )
    hyper = Hyper() if fast else None
    me = hyper.me if fast else jnp.zeros((4,), jnp.int32)
    none = []

    def grad_outs(name, count):
        if fast:
            block = shape((4, 2, 2, count, width // 16, width // 2), BF)
            return [(block, HB), (block, HB)]
        return [(shape(whole_shape(name, width), BF), HB)]

    dma = pltpu.SemaphoreType.DMA
    x_rows = inputs.reshape(rows, width)
    mem_flat = encoded.reshape(mem_rows, width)
    heads = HEADS
    pairs_count = heads // 2
    turned = buckets.T
    table = jnp.pad(bias_table.T, ((0, 0), (0, 128 - bias_table.shape[0])))

    def weights(*names):
        return [entry for name in names for entry in held[name].ins()]

    held = {}
    if fast:
        ga, gb, gc, gd = [Gather(hyper, shards, plan, width) for plan in GATHERS]
        ga.z()
    else:
        for name in NAMES:
            full = lax.all_gather(shards[name], "narrow", axis=1, tiled=True)
            full = lax.all_gather(full, "wide", axis=0, tiled=True)
            full = full.reshape(whole_shape(name, width))
            held[name] = Held((full,))

    n1, kept, bias = launch(
        prepare_kernel,
        [
            (target_lengths, SM),
            (inputs, VM),
            (cotangent, VM),
            (norm_gains, VM),
            (turned, VM),
            (table, VM),
        ],
        [
            (shape((rows, width), BF), VM),
            (shape((rows, width), BF), VM),
            (shape((pairs_count, length, 2 * length), F32), VM),
        ],
        name="prepare",
    )

    if fast:
        n1, kept, bias = join((ga,), (n1, kept, bias))
        ga.plane()
        ga.core_own()
        gb.z1()
        gb.z2()
        join((ga, gb))
        ga.core()
        gb.plane()
        gc.z1()
        for name in ("inward", "outward"):
            held[name] = ga.held(name)

    (packed,) = launch(
        functools.partial(inward_kernel, held["inward"]),
        [(me, SM), (n1, VM)] + weights("inward"),
        [(shape((rows, 3 * width), BF), VM)],
        [weight_scratch("inward", width), dma],
        gflop=2.0,
        name="inward",
    )

    bias_spec = pl.BlockSpec((2, length, 2 * length), lambda p: (p, 0, 0))
    log_both = pl.BlockSpec((2, seqs, 1, 2 * length), lambda p: (p, 0, 0, 0))
    log_spec = pl.BlockSpec((2, 1, 1, 2 * length), lambda s, p: (p, s, 0, 0))
    log_shape = shape((pairs_count, seqs, 1, 2 * length), F32)
    blocks = pairs_count // 2
    self_mixed, self_log = launch(
        self_forward_kernel,
        [
            (packed, both_spec(rows)),
            (packed, both_spec(rows, blocks)),
            (packed, both_spec(rows, 2 * blocks)),
            (bias, bias_spec),
        ],
        [(shape((rows, width), BF), both_spec(rows)), (log_shape, log_both)],
        attend_scratch(4, length, length, False),
        grid=(blocks,),
        gflop=5.0,
        name="self_forward",
    )

    if fast:
        self_mixed, self_log = join((gc,), (self_mixed, self_log))
        gc.z2()

    after_self, n2 = launch(
        functools.partial(outward_kernel, held["outward"]),
        [(me, SM), (x_rows, VM), (self_mixed, VM), (norm_gains, VM)] + weights("outward"),
        [(shape((rows, width), F32), VM), (shape((rows, width), BF), VM)],
        [weight_scratch("outward", width), dma],
        gflop=2.0,
        name="outward",
    )

    if fast:
        after_self, n2 = join((gb, gc), (after_self, n2))
        gb.core_own()
        gb.core()
        gc.plane()
        gd.z1()
        for name in ("query", "writer", "reader"):
            held[name] = gb.held(name)

    tile_spec = pl.BlockSpec((KEY_TILE, width), lambda i: (i, 0))
    asks, pairs = launch(
        functools.partial(memory_kernel, held["query"], held["reader"]),
        [(me, SM), (memory_lengths, SM), (n2, VM), (mem_flat, pl.BlockSpec((2 * KEY_TILE, width), lambda i: (i, 0)))]
        + weights("query", "reader"),
        [
            (shape((rows, width), BF), pl.BlockSpec((rows, width), lambda i: (0, 0))),
            (
                shape((mem_rows, 2 * width), BF),
                pl.BlockSpec((2 * KEY_TILE, 2 * width), lambda i: (i, 0)),
            ),
        ],
        [weight_scratch("query", width), weight_scratch("reader", width), dma((2,))],
        grid=(mem_rows // (2 * KEY_TILE),),
        gflop=6.0,
        name="memory",
    )

    if fast:
        asks, pairs = join((gd,), (asks, pairs))
        gc.core_own()
        gd.z2()

    cross_mixed, cross_log = launch(
        cross_forward_kernel,
        [
            (memory_lengths, SM),
            (asks, pair_spec(length)),
            (pairs, pair_spec(memory_size)),
            (pairs, pair_spec(memory_size, blocks)),
        ],
        [(shape((rows, width), BF), pair_spec(length)), (log_shape, log_spec)],
        attend_scratch(2, memory_size, length, False),
        grid=(seqs, blocks),
        gflop=10.0,
        name="cross_forward",
    )

    if fast:
        cross_mixed, cross_log = join((gc, gd), (cross_mixed, cross_log))
        gc.core()
        held["expand"] = gc.held("expand")
        gd.plane()
        gd.core_own()

    after_cross, n3, hidden, slope, *shrink_parts = launch(
        functools.partial(widen_kernel, held["writer"], held["expand"]),
        [(me, SM), (after_self, VM), (cross_mixed, VM), (norm_gains, VM), (kept, VM)]
        + weights("writer", "expand"),
        [
            (shape((rows, width), F32), VM),
            (shape((rows, width), BF), VM),
            (shape((rows, wide_hidden), BF), VM),
            (shape((rows, wide_hidden), BF), VM),
        ]
        + grad_outs("shrink", 4),
        [
            weight_scratch("writer", width),
            weight_scratch("expand", width),
            weight_scratch("shrink", width),
            dma((3,)),
        ],
        gflop=10.0,
        name="widen",
    )

    if fast:
        after_cross, n3, hidden, slope = join((gd,), (after_cross, n3, hidden, slope))
        gd.core()
        held["shrink"] = gd.held("shrink")

    layer_out, grad_cross, gain_third, *expand_parts = launch(
        functools.partial(narrow_kernel, held["shrink"], held["expand"]),
        [
            (me, SM),
            (target_lengths, SM),
            (n3, VM),
            (kept, VM),
            (norm_gains, VM),
            (after_cross, HB),
            (hidden, HB),
            (slope, HB),
        ]
        + weights("shrink", "expand"),
        [
            (shape((seqs, length, width), BF), VM),
            (shape((rows, width), F32), VM),
            (shape((1, width), F32), VM),
        ]
        + grad_outs("expand", 4),
        [
            weight_scratch("shrink", width),
            weight_scratch("expand", width),
            weight_scratch("expand", width),
            pltpu.VMEM((rows, wide_hidden), BF),
            pltpu.VMEM((rows, width), F32),
            pltpu.VMEM((rows, wide_hidden), BF),
            pltpu.VMEM((rows, wide_hidden), BF),
            dma((6,)),
        ],
        gflop=14.0,
        name="narrow",
    )

    if fast:
        sf = HalvedScatter(hyper, shrink_parts, expand_parts, "ffn")
        sf.core(0)
        sf.core(1)

    grad_mixed, *writer_parts = launch(
        functools.partial(writer_back_kernel, held["writer"]),
        [(me, SM), (grad_cross, VM), (cross_mixed, VM)] + weights("writer"),
        [(shape((rows, width), BF), VM)] + grad_outs("writer", 1),
        [weight_scratch("writer", width), weight_scratch("writer", width), dma((2,))],
        gflop=2.0,
        name="writer_back",
    )

    if fast:
        sf.p1([grad_mixed])

    grad_asks, grad_mem_keys, grad_mem_values = launch(
        cross_backward_kernel,
        [
            (memory_lengths, SM),
            (asks, pair_spec(length)),
            (pairs, pair_spec(memory_size)),
            (pairs, pair_spec(memory_size, blocks)),
            (grad_mixed, pair_spec(length)),
            (cross_mixed, pair_spec(length)),
            (cross_log, log_spec),
        ],
        [
            (shape((rows, width), BF), pair_spec(length)),
            (shape((mem_rows, width), BF), pair_spec(memory_size)),
            (shape((mem_rows, width), BF), pair_spec(memory_size)),
        ],
        attend_scratch(2, memory_size, length, True),
        grid=(seqs, blocks),
        gflop=20.0,
        name="cross_backward",
        after=sf.sent if fast else none,
    )

    whole_spec = pl.BlockSpec((memory_size, width), lambda i: (i, 0))
    reader_parts = launch(
        reader_grad_kernel,
        [
            (me, SM),
            (memory_lengths, SM),
            (mem_flat, whole_spec),
            (grad_mem_keys, whole_spec),
            (grad_mem_values, whole_spec),
        ],
        grad_outs("reader", 2),
        [weight_scratch("reader", width), pltpu.VMEM((width, 2 * width), F32), dma],
        grid=(seqs,),
        gflop=5.0,
        name="reader_grad",
    )

    if fast:
        sf.p2([reader_parts[0]])
        sm = Scatter(hyper, "middle", ("writer", "reader", "query", "outward"))
        sm.core(*writer_parts)
        sm.core(*reader_parts)

    grad_self, grad_mixed, gain_second, *rest_parts = launch(
        functools.partial(query_back_kernel, fast, held["query"], held["outward"]),
        [
            (me, SM),
            (grad_asks, VM),
            (n2, VM),
            (norm_gains, VM),
            (after_self, HB),
            (grad_cross, HB),
            (self_mixed, HB),
        ]
        + weights("query", "outward"),
        [
            (shape((rows, width), F32), VM),
            (shape((rows, width), BF), VM),
            (shape((1, width), F32), VM),
        ]
        + (grad_outs("query", 2) if fast else grad_outs("query", 1) + grad_outs("outward", 1)),
        [
            weight_scratch("query", width),
            weight_scratch("outward", width),
            weight_scratch("query", width),
            weight_scratch("outward", width),
            pltpu.VMEM((rows, width), F32),
            pltpu.VMEM((rows, width), F32),
            pltpu.VMEM((rows, width), BF),
            dma((7,)),
        ],
        gflop=4.0,
        name="query_back",
        after=sf.sent if fast else none,
    )

    if fast:
        sm.core(*rest_parts)
        sf.z2([grad_mixed])
        sm.plane(sf.sent)

    grad_query, grad_keys, grad_values, grad_bias = launch(
        self_backward_kernel,
        [
            (packed, both_spec(rows)),
            (packed, both_spec(rows, blocks)),
            (packed, both_spec(rows, 2 * blocks)),
            (grad_mixed, both_spec(rows)),
            (self_mixed, both_spec(rows)),
            (bias, bias_spec),
            (self_log, log_both),
        ],
        [(shape((rows, width), BF), both_spec(rows))] * 3
        + [(shape((pairs_count, length, 2 * length), F32), bias_spec)],
        attend_scratch(4, length, length, True),
        grid=(blocks,),
        gflop=6.0,
        name="self_backward",
        after=sm.sent if fast else none,
    )

    inward_parts = launch(
        inward_grad_kernel,
        [(me, SM), (n1, VM), (grad_query, VM), (grad_keys, VM), (grad_values, VM)],
        grad_outs("inward", 3),
        [weight_scratch("inward", width), dma],
        gflop=2.0,
        name="inward_grad",
    )

    if fast:
        si = Scatter(hyper, "inward", ("inward",))
        si.core(*inward_parts)
        sf.z1([inward_parts[0]])

    inputs_grad, gain_first = launch(
        functools.partial(inputs_grad_kernel, held["inward"]),
        [
            (me, SM),
            (grad_query, VM),
            (grad_keys, VM),
            (grad_values, VM),
            (norm_gains, VM),
            (x_rows, HB),
            (grad_self, HB),
        ]
        + weights("inward"),
        [(shape((rows, width), F32), VM), (shape((1, width), F32), VM)],
        [
            weight_scratch("inward", width),
            pltpu.VMEM((rows, width), BF),
            pltpu.VMEM((rows, width), F32),
            dma((3,)),
        ],
        gflop=2.0,
        name="inputs_grad",
        after=sf.sent if fast else none,
    )

    if fast:
        si.plane([inputs_grad])
        sm.line(si.sent)
        sums = dict(zip(("shrink", "expand"), sf.last((("shrink", 0), ("expand", 4)), sm.sent)))

    double_spec = pl.BlockSpec((2 * KEY_TILE, width), lambda i: (i, 0))
    (encoded_grad,) = launch(
        functools.partial(encoded_grad_kernel, held["reader"]),
        [(me, SM), (memory_lengths, SM), (grad_mem_keys, double_spec), (grad_mem_values, double_spec)]
        + weights("reader"),
        [(shape((mem_rows, width), F32), double_spec)],
        [weight_scratch("reader", width), dma],
        grid=(mem_rows // (2 * KEY_TILE),),
        gflop=5.0,
        name="encoded_grad",
        after=sf.sent if fast else none,
    )

    if fast:
        si.line([encoded_grad])

    (table_part,) = launch(
        functools.partial(table_kernel, bias_table.shape[0]),
        [(turned, VM), (grad_bias, VM)],
        [(shape((heads, 128), F32), VM)],
        [pltpu.VMEM((4, length, length), F32)],
        gflop=6.0,
        name="table",
        after=si.sent if fast else none,
    )

    if fast:
        sums.update(sm.last([table_part]))
        sums.update(si.last(sm.sent))
    else:
        sums = {}
        parts = {
            "shrink": shrink_parts[0],
            "expand": expand_parts[0],
            "writer": writer_parts[0],
            "reader": reader_parts[0],
            "query": rest_parts[0],
            "outward": rest_parts[1],
            "inward": inward_parts[0],
        }
        for name in NAMES:
            full = parts[name].reshape(-1, parts[name].shape[-1]).astype(F32)
            full = lax.psum_scatter(full, "wide", scatter_dimension=0, tiled=True)
            sums[name] = lax.psum_scatter(full, "narrow", scatter_dimension=1, tiled=True)

    grads = [sums[name] for name in NAMES]
    tallest = max(g.shape[0] for g in grads)
    piece = width // narrow_count
    _, totals_at, gains_at, table_at = shared_places([g.shape[1] for g in grads], piece, width)
    row_sums, shared = launch(
        functools.partial(statistics_kernel, piece),
        [(g, VM) for g in grads]
        + [(gain_first, VM), (gain_second, VM), (gain_third, VM), (table_part, VM)],
        [(shape((tallest, 128), F32), VM), (shape((-(-(table_at + heads) // 8) * 8, piece), F32), VM)],
        name="statistics",
    )
    add_y = lax.broadcasted_iota(jnp.int32, shared.shape, 0) >= totals_at
    if fast:
        other = hyper.swap(row_sums, "y")
        shared = shared + jnp.where(add_y, hyper.swap(shared, "y"), 0.0)
        row_sums = row_sums + other
        shared = tie(shared, [other])
        for bit in ("c", "x", "z1", "z2"):
            shared = shared + hyper.swap(shared, bit)
    else:
        row_sums = lax.psum(row_sums, "narrow")
        shared = lax.psum(jnp.where(add_y, lax.psum(shared, "narrow"), shared), "wide")

    step_outs = []
    for g in grads:
        step_outs.append((shape(g.shape, F32), VM))
        step_outs.append((shape((g.shape[0],), F32), VM))
        step_outs.append((shape((g.shape[1],), F32), VM))
    made = launch(
        functools.partial(steps_kernel, wide_count, narrow_count),
        [(g, VM) for g in grads] + [(row_sums, VM), (shared, VM)],
        step_outs,
        name="steps",
    )
    results = []
    for j, grad in enumerate(grads):
        step, row_stat, col_stat = made[3 * j : 3 * j + 3]
        results.extend([grad, step, row_stat, col_stat])
    gains_grad = shared[gains_at:table_at].reshape(3, width)
    table_grad = shared[table_at : table_at + heads, : bias_table.shape[0]].T
    return (
        (
            layer_out,
            inputs_grad.reshape(inputs.shape),
            encoded_grad.reshape(encoded.shape),
        )
        + tuple(results)
        + (gains_grad, table_grad)
    )


def solution(mesh):
    tokens = P(BOTH, None, None)
    weight = P("wide", "narrow")
    per_weight = (weight, weight, P("wide"), P("narrow"))
    return jax.shard_map(
        local,
        mesh=mesh,
        in_specs=(tokens, tokens, P(BOTH), P(BOTH), P(), tokens) + (weight,) * 7 + (P(), P()),
        out_specs=(tokens, tokens, tokens) + per_weight * 7 + (P(), P()),
        check_vma=False,
    )
```
